256 devices in a mesh: pipe: 8 (over z), tensor: 2 (over x_lo), dp: 16 (over y, x_hi, core).
Axes of the slice: x: 4 (x_hi: 2, x_lo: 2; x = x_hi * 2 + x_lo), y: 4, z: 8, core: 2. Of those that a mesh axis runs over, the one named last changes fastest.
Arguments:
- section_proj: bfloat16 [8, 4608, 2048], P('pipe', 'dp', 'tensor'), may hold values from -0.125 to 0.125
- attn_values: bfloat16 [8, 4, 512, 2048], P('pipe', None, 'dp', 'tensor'), may hold values from -6 to 6
- post_gain: float32 [8, 4608], P('pipe'), may hold values from 0.5 to 1.5
- section_input: bfloat16 [4, 512, 4608], P(None, 'dp'), may hold values from -6 to 6
- final_gain: float32 [4608], replicated, may hold values from 0.5 to 1.5
- embed_block: bfloat16 [2048, 4608], P('tensor'), may hold values from -0.26367188 to 0.26367188
- token_ids: int32 [4, 512], P(None, 'dp'), may hold values from 0 to 4095
- target_ids: int32 [4, 512], P(None, 'dp'), may hold values from 0 to 4095
- block_offset: int32 [1], replicated, may hold values from 0 to 2048
- rest_lse: float32 [4, 512], P(None, 'dp'), may hold values from 7 to 13
Outputs:
- proj_grad: float32 [8, 4608, 2048], P('pipe', 'dp', 'tensor')
- tied_grad: float32 [2048, 4608], P(('tensor', 'dp'), 'pipe')
The draws below stay inside these ranges and needn't reach their ends.
Inputs may be any that keep to these rules, and one draw needn't show every extreme that they name: `token_ids`: token ids lie in [0, 4096); about half fall inside the block.
All inputs are finite; a program needn't handle non-finite values.
Results may differ from the reference program's by a relative error of at most 0.028.
Values may be sent and summed in bfloat16 or wider, within the bound.
A program may use at most 128 MiB of HBM per device.

```python
import math
import jax
import jax.numpy as jnp
from jax import lax

D = 4608
HV = 2048
VROWS = 1024
MICRO = 4
TOK_DEV = 32
TOKENS = 512
SECTIONS = 8
VBLOCK = 2048
N_PIPE = 8
N_TENSOR = 2
N_DP = 16


def place_ends(array, rng, low, high):
    place = [jax.random.randint(jax.random.fold_in(rng, axis), (), 0, length) for axis, length in enumerate(array.shape)]
    widest = array.shape.index(max(array.shape))
    neighbour = place[:widest] + [(place[widest] + 1) % array.shape[widest]] + place[widest + 1:]
    return array.at[tuple(place)].set(low).at[tuple(neighbour)].set(high)


def steps_of(rng, shape, shards, low, top_value):
    loudness, own = 1.0, jax.random.fold_in(rng, 6)
    for dim, parts in shards:
        heights = jnp.exp(jax.random.uniform(jax.random.fold_in(own, dim), (parts,), jnp.float32, low / len(shards), top_value / len(shards)))
        loudness = loudness * jnp.repeat(heights, shape[dim] // parts).reshape([-1 if axis == dim else 1 for axis in range(len(shape))])
    return loudness


def centred(key, shape, deviation, limit, cuts=(), kind=jnp.bfloat16):
    drawn = deviation * jax.random.normal(key, shape, jnp.float32)
    if cuts:
        drawn = drawn * steps_of(key, shape, cuts, -0.22, 0.18)
    return jnp.clip(drawn, -limit, limit).astype(kind)


def setup_inputs(seed: int = 0) -> dict:
    key_of = jax.random.split(jax.random.key(seed), 11)
    section_proj = centred(key_of[0], (SECTIONS, D, HV), HV ** -0.5, 0.125, ((0, 8), (1, 16), (2, 2)))
    attn_values = centred(key_of[1], (SECTIONS, MICRO, TOKENS, HV), 1.0, 6.0, ((0, 8), (2, 16), (3, 2)))
    post_gain = jnp.clip(1.0 + 0.1 * jax.random.normal(key_of[2], (SECTIONS, D), jnp.float32), 0.5, 1.5)
    section_input = centred(key_of[3], (MICRO, TOKENS, D), 1.0, 6.0, ((1, 16),))
    final_gain = jnp.clip(1.0 + 0.1 * jax.random.normal(key_of[4], (D,), jnp.float32), 0.5, 1.5)
    embed_block = centred(key_of[5], (VBLOCK, D), (3.0 / D ** 0.5), 0.26367188, ((0, 2),))
    token_ids = place_ends(jax.random.randint(key_of[6], (MICRO, TOKENS), 0, 2 * VBLOCK), jax.random.fold_in(key_of[6], 1), 0, (2 * VBLOCK) - 1).astype(jnp.int32)
    target_ids = place_ends(jax.random.randint(key_of[7], (MICRO, TOKENS), 0, 2 * VBLOCK), jax.random.fold_in(key_of[7], 1), 0, (2 * VBLOCK) - 1).astype(jnp.int32)
    block_offset = jax.random.randint(key_of[8], (1,), 0, VBLOCK + 1).astype(jnp.int32)
    rest_lse = jnp.clip(7.0 + 6.0 * jax.random.uniform(key_of[9], (MICRO, TOKENS), jnp.float32) ** steps_of(key_of[9], (MICRO, TOKENS), ((1, 16),), -0.2, 0.2), 7.0, 13.0)
    return {"section_proj": section_proj, "attn_values": attn_values, "post_gain": post_gain, "section_input": section_input, "final_gain": final_gain, "embed_block": embed_block, "token_ids": token_ids, "target_ids": target_ids, "block_offset": block_offset, "rest_lse": rest_lse}


EPS = 1e-06
CAP = 30.0

def to_half(value):
    return lax.optimization_barrier(value.astype(jnp.bfloat16)).astype(jnp.float32)

def project(values, weight):
    width = HV // N_TENSOR
    total = jnp.zeros((values.shape[0], D), jnp.float32)
    for group in range(N_TENSOR):
        part = jnp.dot(values[:, group * width:(group + 1) * width], weight[:, group * width:(group + 1) * width].T, preferred_element_type=jnp.float32)
        total = total + to_half(part)
    return total

def normalize(value):
    scale = lax.rsqrt(lax.optimization_barrier(jnp.mean(value * value, axis=-1, keepdims=True)) + EPS)
    return (scale, value * scale)

def norm_back(scale, normed, grad):
    return scale * (grad - normed * lax.optimization_barrier(jnp.mean(grad * normed, axis=-1, keepdims=True)))

def per_replica(left, right, factor):
    left_split = left.reshape(MICRO, N_DP, TOK_DEV, left.shape[-1])
    right_split = right.reshape(MICRO, N_DP, TOK_DEV, right.shape[-1])

    def step(carry, index):
        lhs = lax.dynamic_index_in_dim(left_split, index, 1, False).astype(jnp.float32)
        rhs = lax.dynamic_index_in_dim(right_split, index, 1, False).astype(jnp.float32)
        part = factor * jnp.einsum('mtp,mtq->pq', lhs, rhs)
        return (carry + to_half(part), None)
    start = jnp.zeros((left.shape[-1], right.shape[-1]), jnp.float32)
    total, _ = lax.scan(step, start, jnp.arange(N_DP, dtype=jnp.int32))
    return total

def reference(section_proj, attn_values, post_gain, section_input, final_gain, embed_block, token_ids, target_ids, block_offset, rest_lse):
    count = MICRO * TOKENS
    last = N_PIPE - 1
    scales = []
    normeds = []
    for section in range(N_PIPE):
        output = project(attn_values[section].reshape(count, HV), section_proj[section])
        scale, normed = normalize(output)
        scales.append(scale)
        normeds.append(normed)
    resid = section_input.reshape(count, D).astype(jnp.float32) + normeds[last] * post_gain[last]
    y_scale, y_normed = normalize(resid)
    head_in = (y_normed * final_gain).astype(jnp.bfloat16)
    raw = jnp.dot(head_in, embed_block.T, preferred_element_type=jnp.float32)
    capped = jnp.tanh(raw / CAP)
    logits = CAP * capped
    total = lax.optimization_barrier(jnp.sum(jnp.exp(logits), axis=1))
    lse = jnp.logaddexp(rest_lse.reshape(count), jnp.log(total))
    column = jnp.arange(VBLOCK, dtype=jnp.int32)
    hit = (target_ids.reshape(count, 1) - block_offset[0] == column[None, :]).astype(jnp.float32)
    delta = ((jnp.exp(logits - lse[:, None]) - hit) * (1.0 - capped * capped)).astype(jnp.bfloat16)
    back = jnp.zeros((count, D), jnp.float32)
    for group in range(N_TENSOR):
        part = jnp.dot(delta[:, group * VROWS:(group + 1) * VROWS], embed_block[group * VROWS:(group + 1) * VROWS], preferred_element_type=jnp.float32)
        back = back + to_half(part)
    top_grad = norm_back(y_scale, y_normed, back * final_gain).astype(jnp.bfloat16)
    grads = []
    for section in range(N_PIPE):
        out_grad = norm_back(scales[section], normeds[section], top_grad.astype(jnp.float32) * post_gain[section]).astype(jnp.bfloat16)
        grads.append(per_replica(out_grad.reshape(MICRO, TOKENS, D), attn_values[section], 1.0))
    proj_grad = jnp.stack(grads)
    used = (token_ids.reshape(count, 1) - block_offset[0] == column[None, :]).astype(jnp.bfloat16)
    head_part = per_replica(delta.reshape(MICRO, TOKENS, VBLOCK), head_in.reshape(MICRO, TOKENS, D), 1.0)
    embed_part = per_replica(used.reshape(MICRO, TOKENS, VBLOCK), top_grad.reshape(MICRO, TOKENS, D), math.sqrt(D))
    return (proj_grad, head_part + embed_part)
```

```python
import functools
import math

import jax
import jax.numpy as jnp
from jax import lax
from jax.experimental import pallas as pl
from jax.experimental.pallas import tpu as pltpu
from jax.sharding import PartitionSpec as P

EPS = 1e-06
CAP = 30.0
MESH = pl.DeviceIdType.MESH
ANY = pl.BlockSpec(memory_space=pl.ANY)
VMEM = pl.BlockSpec(memory_space=pltpu.VMEM)
CONTRACT_LAST = (((1,), (1,)), ((), ()))
CONTRACT_FIRST = (((0,), (0,)), ((), ()))
W_CHUNK = 32
BACK_CHUNKS = 4


def position():
    return lax.axis_index("pipe"), lax.axis_index("tensor"), lax.axis_index("dp")


def remote(src, dst, send_sem, recv_sem, device):
    return pltpu.make_async_remote_copy(
        src_ref=src,
        dst_ref=dst,
        send_sem=send_sem,
        recv_sem=recv_sem,
        device_id=device,
        device_id_type=MESH,
    )


def signal(sem, device):
    pl.semaphore_signal(sem, inc=1, device_id=device, device_id_type=MESH)


def greet_pipe(barrier, n_pipe):
    p, t, j = position()

    @pl.loop(1, n_pipe)
    def _(k):
        signal(barrier, (lax.rem(p + k, n_pipe), t, j))


def greet_dp(barrier, n_dp):
    p, t, j = position()

    @pl.loop(1, n_dp)
    def _(k):
        signal(barrier, (p, t, lax.rem(j + k, n_dp)))


def gather_kernel(
    n_pipe, n_dp,
    w_ref, a_ref, gain_ref,
    w7_ref, a7_ref, g7_ref, all_ref,
    local_sem, w_recv, w_up, w_down, s_recv, s_send, g_recv, g_send,
    a_recv, a_send, v_recv, v_send, v_fwd,
):
    p, t, j = position()
    last = n_pipe - 1
    up_hops = n_pipe // 2
    down_hops = last - up_hops
    core = lax.rem(j, 2)
    sibling = j + 1 - 2 * core
    n_chips = n_dp // 2
    chip = j // 2
    chunks = w_ref.shape[0] // W_CHUNK
    is_last = p == last

    barrier = pltpu.get_barrier_semaphore()
    greet_pipe(barrier, n_pipe)
    greet_dp(barrier, n_dp)
    pl.semaphore_wait(barrier, n_pipe - 1 + n_dp - 1)

    def rows(ref, c):
        return ref.at[pl.ds(pl.multiple_of(c * W_CHUNK, W_CHUNK), W_CHUNK)]

    def slice_copy(q):
        return remote(a_ref.at[q], a7_ref.at[j], s_send.at[q], s_recv, (q, t, j))

    def gain_copy(q):
        return remote(gain_ref, g7_ref, g_send.at[q], g_recv, (q, t, j))

    def weight_copy(source, c, sems, q):
        return remote(rows(source, c), rows(w7_ref, c), sems.at[c], w_recv.at[c], (q, t, j))

    up = lax.rem(p + 1, n_pipe)
    down = lax.rem(p + last, n_pipe)

    @pl.when(is_last)
    def _():
        pltpu.make_async_copy(a_ref.at[last], a7_ref.at[j], local_sem.at[0]).start()

        @pl.loop(0, last)
        def _(q):
            slice_copy(q).start()

        @pl.loop(0, chunks)
        def _(c):
            weight_copy(w_ref, c, w_up, up).start()
            if down_hops:
                weight_copy(w_ref, c, w_down, down).start()

        @pl.loop(0, last)
        def _(q):
            gain_copy(q).start()

        pltpu.make_async_copy(w_ref, w7_ref, local_sem.at[1]).start()
        pltpu.make_async_copy(gain_ref, g7_ref, local_sem.at[2]).start()

    own_values = pltpu.make_async_copy(a_ref, all_ref.at[:, j], local_sem.at[3])
    own_values.start()

    def values_copy(k):
        other = lax.rem(chip + k, n_chips) * 2 + core
        return remote(a_ref, all_ref.at[:, j], v_send.at[k], v_recv.at[j], (p, t, other))

    def forward_copy(k):
        owner = lax.rem(chip + n_chips - k, n_chips) * 2 + core
        return remote(
            all_ref.at[:, owner], all_ref.at[:, owner], v_fwd.at[k], v_recv.at[owner], (p, t, sibling)
        )

    def arrived_values(owner):
        return remote(a_ref, all_ref.at[:, owner], v_send.at[0], v_recv.at[owner], (p, t, sibling))

    own_pair = remote(a_ref, all_ref.at[:, j], v_send.at[0], v_recv.at[j], (p, t, sibling))

    @pl.when(is_last)
    def _():
        pltpu.make_async_copy(a_ref.at[last], a7_ref.at[j], local_sem.at[0]).wait()

    @pl.when(jnp.logical_not(is_last))
    def _():
        slice_copy(p).wait_recv()

    def token_copy(k):
        return remote(
            a7_ref.at[j], a7_ref.at[j], a_send.at[k], a_recv.at[j], (p, t, lax.rem(j + k, n_dp))
        )

    def arrived_tokens(owner):
        return remote(a7_ref.at[j], a7_ref.at[owner], a_send.at[0], a_recv.at[owner], (p, t, sibling))

    @pl.loop(1, n_dp)
    def _(k):
        token_copy(k).start()

    own_pair.start()

    @pl.loop(1, n_chips)
    def _(k):
        values_copy(k).start()

    @pl.when(p < last)
    def _():
        @pl.loop(0, chunks)
        def _(c):
            weight_copy(w_ref, c, w_up, up).wait_recv()

            @pl.when(p < up_hops - 1)
            def _():
                weight_copy(w7_ref, c, w_up, up).start()

            @pl.when(p > up_hops)
            def _():
                weight_copy(w7_ref, c, w_down, down).start()

    @pl.loop(1, n_chips)
    def _(k):
        arrived_values(lax.rem(chip + n_chips - k, n_chips) * 2 + core).wait_recv()
        forward_copy(k).start()

    @pl.loop(1, n_dp)
    def _(k):
        arrived_tokens(lax.rem(j + k, n_dp)).wait_recv()

    arrived_values(sibling).wait_recv()

    @pl.loop(1, n_chips)
    def _(k):
        arrived_values(lax.rem(chip + n_chips - k, n_chips) * 2 + 1 - core).wait_recv()

    @pl.loop(1, n_dp)
    def _(k):
        token_copy(k).wait_send()

    own_pair.wait_send()
    own_values.wait()

    @pl.loop(1, n_chips)
    def _(k):
        values_copy(k).wait_send()
        forward_copy(k).wait_send()

    @pl.when(is_last)
    def _():
        @pl.loop(0, last)
        def _(q):
            slice_copy(q).wait_send()
            gain_copy(q).wait_send()

        @pl.loop(0, chunks)
        def _(c):
            weight_copy(w_ref, c, w_up, up).wait_send()
            if down_hops:
                weight_copy(w_ref, c, w_down, down).wait_send()

        pltpu.make_async_copy(w_ref, w7_ref, local_sem.at[1]).wait()
        pltpu.make_async_copy(gain_ref, g7_ref, local_sem.at[2]).wait()

    @pl.when(jnp.logical_not(is_last))
    def _():
        gain_copy(p).wait_recv()

        @pl.when(p < up_hops - 1)
        def _():
            @pl.loop(0, chunks)
            def _(c):
                weight_copy(w7_ref, c, w_up, up).wait_send()

        @pl.when(p > up_hops)
        def _():
            @pl.loop(0, chunks)
            def _(c):
                weight_copy(w7_ref, c, w_down, down).wait_send()


def gather(weight, values, gain, n_pipe, n_dp):
    dma = pltpu.SemaphoreType.DMA
    chunks = weight.shape[0] // W_CHUNK
    tokens, width = values.shape[1:]
    kind = jnp.bfloat16
    return pl.pallas_call(
        functools.partial(gather_kernel, n_pipe, n_dp),
        out_shape=(
            jax.ShapeDtypeStruct(weight.shape, kind),
            jax.ShapeDtypeStruct((n_dp, tokens, width), kind),
            jax.ShapeDtypeStruct(gain.shape, jnp.float32),
            jax.ShapeDtypeStruct((n_pipe, n_dp, tokens, width), kind),
        ),
        in_specs=[ANY] * 3,
        out_specs=(ANY,) * 4,
        scratch_shapes=[
            dma((4,)),
            dma((chunks,)), dma((chunks,)), dma((chunks,)),
            dma, dma((n_pipe,)), dma, dma((n_pipe,)),
            dma((n_dp,)), dma((n_dp,)),
            dma((n_dp,)), dma((n_dp // 2,)), dma((n_dp // 2,)),
        ],
        compiler_params=pltpu.CompilerParams(collective_id=0, has_side_effects=True),
        name="gather_sections",
    )(weight, values, gain)


def normalize(value):
    scale = lax.rsqrt(jnp.mean(value * value, axis=-1, keepdims=True) + EPS)
    return scale, value * scale


def flatten(blocks):
    return jnp.concatenate(blocks, axis=1)


def head_kernel(
    n_pipe, n_dp,
    part_ref, embed_ref, input_ref, g7_ref, gain_ref, target_ref, rest_ref,
    tg_ref, delta_ref, hz_ref, tz_ref,
    embed, parts, sum_out, sum_in, back_out, back_in, block,
    embed_sem, p_recv, p_send, sum_sem, back_recv, back_send,
    d_recv, d_send, h_recv, h_send, z_recv, z_send,
    t_recv, t_send, r_recv, r_up, r_down, local_sem,
):
    p, t, j = position()
    last = n_pipe - 1
    up_hops = n_pipe // 2
    down_hops = last - up_hops
    other = 1 - t
    per_pipe = hz_ref.shape[1]
    tokens = part_ref.shape[1]
    width = part_ref.shape[2]
    vrows, model = embed_ref.shape

    load = pltpu.make_async_copy(embed_ref, embed, embed_sem)
    load.start()
    barrier = pltpu.get_barrier_semaphore()
    greet_dp(barrier, n_dp)

    @pl.loop(0, n_dp)
    def _(k):
        signal(barrier, (p, other, k))

    greet_pipe(barrier, n_pipe)
    pl.semaphore_wait(barrier, 2 * n_dp - 1 + n_pipe - 1)

    def same_copy(k):
        q = lax.rem(j + k, n_dp)
        return remote(part_ref.at[q], parts.at[t, j], p_send.at[0, k], p_recv.at[t, j], (p, t, q))

    def cross_copy(k):
        q = lax.rem(j + k, n_dp)
        return remote(part_ref.at[q], parts.at[t, j], p_send.at[1, k], p_recv.at[t, j], (p, other, q))

    own_part = pltpu.make_async_copy(part_ref.at[j], parts.at[t, j], local_sem.at[0])
    own_part.start()

    @pl.loop(0, n_dp)
    def _(k):
        cross_copy(k).start()

    @pl.loop(1, n_dp)
    def _(k):
        same_copy(k).start()

    def arrived(group, q):
        return remote(part_ref.at[q], parts.at[group, q], p_send.at[0, 0], p_recv.at[group, q], (p, other, j))

    own_part.wait()

    @pl.loop(0, n_dp)
    def _(k):
        arrived(other, k).wait_recv()

    @pl.loop(1, n_dp)
    def _(k):
        arrived(t, lax.rem(j + k, n_dp)).wait_recv()

    output = flatten(
        [parts[0, q].astype(jnp.float32) + parts[1, q].astype(jnp.float32) for q in range(n_dp)]
    )
    _, normed = normalize(output)
    mine = pl.ds(pl.multiple_of(p * tokens, tokens), tokens)
    resid = input_ref[mine, :].astype(jnp.float32) + normed * g7_ref[...]
    y_scale, y_normed = normalize(resid)
    head_in = (y_normed * gain_ref[...]).astype(jnp.bfloat16)

    for b in range(n_dp):
        block[0, b] = head_in[:, b * width:(b + 1) * width]

    def line_copy(slot, out_ref, send, recv, k):
        q = lax.rem(p + k, n_pipe)
        return remote(
            block.at[slot, pl.ds(q * per_pipe, per_pipe)], out_ref.at[p], send.at[k], recv.at[p], (q, t, j)
        )

    def line_arrived(slot, out_ref, send, recv, q):
        return remote(
            block.at[slot, pl.ds(0, per_pipe)], out_ref.at[q], send.at[0], recv.at[q], (q, t, j)
        )

    own_head = pltpu.make_async_copy(
        block.at[0, pl.ds(p * per_pipe, per_pipe)], hz_ref.at[p], local_sem.at[1]
    )
    own_head.start()

    @pl.loop(1, n_pipe)
    def _(k):
        line_copy(0, hz_ref, h_send, h_recv, k).start()

    load.wait()
    raw = lax.dot_general(head_in, embed[...], CONTRACT_LAST, preferred_element_type=jnp.float32)
    capped = jnp.tanh(raw / CAP)
    logits = CAP * capped
    own_sum = jnp.sum(jnp.exp(logits), axis=1, keepdims=True)
    sum_out[...] = jnp.broadcast_to(own_sum, sum_out.shape)
    pair = (p, other, j)
    sums = remote(sum_out, sum_in, sum_sem.at[0], sum_sem.at[1], pair)
    sums.start()
    column = lax.broadcasted_iota(jnp.int32, (tokens, vrows), 1)
    hit = (target_ref[mine, :] - t * vrows == column).astype(jnp.float32)
    slope = 1.0 - capped * capped
    sums.wait_recv()
    log_total = jnp.log(own_sum + sum_in[:, 0:1])
    rest = rest_ref[mine, :]
    high = jnp.maximum(rest, log_total)
    lse = high + jnp.log(1.0 + jnp.exp(-jnp.abs(rest - log_total)))
    delta = ((jnp.exp(logits - lse) - hit) * slope).astype(jnp.bfloat16)

    sum_out_delta = back_out.at[BACK_CHUNKS, :, pl.ds(0, vrows)]
    sum_out_delta[...] = delta
    own_delta = pltpu.make_async_copy(sum_out_delta, delta_ref.at[p], local_sem.at[2])
    own_delta.start()

    def delta_copy(k):
        q = lax.rem(p + k, n_pipe)
        return remote(sum_out_delta, delta_ref.at[p], d_send.at[k], d_recv.at[p], (q, t, j))

    def delta_arrived(q):
        return remote(sum_out_delta, delta_ref.at[q], d_send.at[0], d_recv.at[q], (q, t, j))

    @pl.loop(1, n_pipe)
    def _(k):
        delta_copy(k).start()

    step = model // BACK_CHUNKS
    copies = []
    for c in range(BACK_CHUNKS):
        piece = jnp.dot(delta, embed[:, c * step:(c + 1) * step], preferred_element_type=jnp.float32)
        back_out[c, :, 0:step] = piece.astype(jnp.bfloat16)
        copy = remote(
            back_out.at[c, :, pl.ds(0, step)], back_in.at[c], back_send.at[c], back_recv.at[c], pair
        )
        copy.start()
        copies.append(copy)
    grads = []
    for c in range(BACK_CHUNKS):
        copies[c].wait_recv()
        grads.append(back_out[c, :, 0:step].astype(jnp.float32) + back_in[c].astype(jnp.float32))
    grad = flatten(grads) * gain_ref[...]
    top = y_scale * (grad - y_normed * jnp.mean(grad * y_normed, axis=-1, keepdims=True))
    top = top.astype(jnp.bfloat16)
    for b in range(n_dp):
        block[1, b] = top[:, b * width:(b + 1) * width]

    def column_copy(k):
        q = lax.rem(j + k, n_dp)
        return remote(block.at[1, q], tg_ref.at[p, j], t_send.at[k], t_recv.at[j], (p, t, q))

    def column_arrived(q):
        return remote(block.at[1, q], tg_ref.at[p, q], t_send.at[0], t_recv.at[q], pair)

    own_column = pltpu.make_async_copy(block.at[1, j], tg_ref.at[p, j], local_sem.at[3])
    own_column.start()

    @pl.loop(1, n_dp)
    def _(k):
        column_copy(k).start()

    own_top = pltpu.make_async_copy(
        block.at[1, pl.ds(p * per_pipe, per_pipe)], tz_ref.at[p], local_sem.at[4]
    )
    own_top.start()

    @pl.loop(1, n_pipe)
    def _(k):
        line_copy(1, tz_ref, z_send, z_recv, k).start()

    own_column.wait()

    @pl.loop(1, n_dp)
    def _(k):
        column_arrived(lax.rem(j + k, n_dp)).wait_recv()

    up = (lax.rem(p + 1, n_pipe), t, j)
    down = (lax.rem(p + last, n_pipe), t, j)

    def ring_copy(plane, send, device):
        return remote(tg_ref.at[plane], tg_ref.at[plane], send.at[plane], r_recv.at[plane], device)

    def above(s):
        return lax.rem(p + s, n_pipe)

    def below(s):
        return lax.rem(p + n_pipe - s, n_pipe)

    for s in range(up_hops + 1):
        if s > 0:
            ring_copy(below(s), r_up, up).wait_recv()
        if s < up_hops:
            ring_copy(below(s), r_up, up).start()
        if 0 < s <= down_hops:
            ring_copy(above(s), r_down, down).wait_recv()
        if s < down_hops:
            ring_copy(above(s), r_down, down).start()

    own_head.wait()
    own_delta.wait()
    own_top.wait()

    @pl.loop(1, n_pipe)
    def _(k):
        q = lax.rem(p + k, n_pipe)
        line_arrived(0, hz_ref, h_send, h_recv, q).wait_recv()
        line_arrived(1, tz_ref, z_send, z_recv, q).wait_recv()
        delta_arrived(q).wait_recv()
        line_copy(0, hz_ref, h_send, h_recv, k).wait_send()
        line_copy(1, tz_ref, z_send, z_recv, k).wait_send()
        delta_copy(k).wait_send()

    @pl.loop(0, n_dp)
    def _(k):
        cross_copy(k).wait_send()

    @pl.loop(1, n_dp)
    def _(k):
        same_copy(k).wait_send()
        column_copy(k).wait_send()

    sums.wait_send()
    for copy in copies:
        copy.wait_send()
    for s in range(up_hops):
        ring_copy(below(s), r_up, up).wait_send()
    for s in range(down_hops):
        ring_copy(above(s), r_down, down).wait_send()


def head(part, embed, section_input, g7, final_gain, target, rest, n_pipe, n_dp):
    dma = pltpu.SemaphoreType.DMA
    _, tokens, width = part.shape
    vrows, model = embed.shape
    per_pipe = n_dp // n_pipe
    step = model // BACK_CHUNKS
    kind = jnp.bfloat16
    return pl.pallas_call(
        functools.partial(head_kernel, n_pipe, n_dp),
        out_shape=(
            jax.ShapeDtypeStruct((n_pipe, n_dp, tokens, width), kind),
            jax.ShapeDtypeStruct((n_pipe, tokens, vrows), kind),
            jax.ShapeDtypeStruct((n_pipe, per_pipe, tokens, width), kind),
            jax.ShapeDtypeStruct((n_pipe, per_pipe, tokens, width), kind),
        ),
        in_specs=[VMEM, ANY, VMEM, VMEM, VMEM, VMEM, VMEM],
        out_specs=(ANY,) * 4,
        scratch_shapes=[
            pltpu.VMEM((vrows, model), kind),
            pltpu.VMEM((2, n_dp, tokens, width), kind),
            pltpu.VMEM((tokens, 128), jnp.float32),
            pltpu.VMEM((tokens, 128), jnp.float32),
            pltpu.VMEM((BACK_CHUNKS + 1, tokens, max(step, vrows)), kind),
            pltpu.VMEM((BACK_CHUNKS, tokens, step), kind),
            pltpu.VMEM((2, n_dp, tokens, width), kind),
            dma, dma((2, n_dp)), dma((2, n_dp)), dma((2,)), dma((BACK_CHUNKS,)), dma((BACK_CHUNKS,)),
            dma((n_pipe,)), dma((n_pipe,)), dma((n_pipe,)), dma((n_pipe,)), dma((n_pipe,)), dma((n_pipe,)),
            dma((n_dp,)), dma((n_dp,)), dma((n_pipe,)), dma((n_pipe,)), dma((n_pipe,)), dma((5,)),
        ],
        compiler_params=pltpu.CompilerParams(
            collective_id=1, has_side_effects=True, vmem_limit_bytes=40 * 1024 * 1024
        ),
        cost_estimate=pl.CostEstimate(flops=40_000_000_000, bytes_accessed=100_000_000, transcendentals=0),
        name="head_block",
    )(part, embed, section_input, g7, final_gain, target, rest)


def exchange_kernel(
    n_dp, term_ref, stat_ref, terms_ref, stats_ref, t_recv, t_send, s_recv, s_send, local_sem
):
    p, t, j = position()
    barrier = pltpu.get_barrier_semaphore()
    greet_dp(barrier, n_dp)
    pl.semaphore_wait(barrier, n_dp - 1)

    def stat_copy(k):
        return remote(stat_ref, stats_ref.at[j], s_send.at[k], s_recv.at[j], (p, t, lax.rem(j + k, n_dp)))

    def term_copy(k):
        q = lax.rem(j + k, n_dp)
        return remote(term_ref.at[:, q], terms_ref.at[j], t_send.at[k], t_recv.at[j], (p, t, q))

    def stat_arrived(q):
        return remote(stat_ref, stats_ref.at[q], s_send.at[0], s_recv.at[q], (p, t, q))

    def term_arrived(q):
        return remote(term_ref.at[:, q], terms_ref.at[q], t_send.at[0], t_recv.at[q], (p, t, q))

    @pl.loop(1, n_dp)
    def _(k):
        stat_copy(k).start()

    @pl.loop(1, n_dp)
    def _(k):
        term_copy(k).start()

    own_stat = pltpu.make_async_copy(stat_ref, stats_ref.at[j], local_sem.at[0])
    own_term = pltpu.make_async_copy(term_ref.at[:, j], terms_ref.at[j], local_sem.at[1])
    own_stat.start()
    own_term.start()
    own_stat.wait()
    own_term.wait()

    @pl.loop(1, n_dp)
    def _(k):
        q = lax.rem(j + k, n_dp)
        stat_arrived(q).wait_recv()
        term_arrived(q).wait_recv()
        stat_copy(k).wait_send()
        term_copy(k).wait_send()


def exchange(term, stat, n_dp):
    dma = pltpu.SemaphoreType.DMA
    groups, _, rows, width = term.shape
    return pl.pallas_call(
        functools.partial(exchange_kernel, n_dp),
        out_shape=(
            jax.ShapeDtypeStruct((n_dp, groups, rows, width), term.dtype),
            jax.ShapeDtypeStruct((n_dp,) + stat.shape, stat.dtype),
        ),
        in_specs=[ANY] * 2,
        out_specs=(ANY,) * 2,
        scratch_shapes=[dma((n_dp,)), dma((n_dp,)), dma((n_dp,)), dma((n_dp,)), dma((2,))],
        compiler_params=pltpu.CompilerParams(collective_id=2, has_side_effects=True),
        name="exchange_terms",
    )(term, stat)


def per_device(
    section_proj,
    attn_values,
    post_gain,
    section_input,
    final_gain,
    embed_block,
    token_ids,
    target_ids,
    block_offset,
    rest_lse,
):
    n_pipe, n_dp = lax.axis_size("pipe"), lax.axis_size("dp")
    weight = section_proj[0]
    width, depth = weight.shape
    model = section_input.shape[2]
    vrows = embed_block.shape[0]
    count = section_input.shape[0] * section_input.shape[1]
    tokens = count // n_pipe
    values = attn_values.reshape(n_pipe, tokens, depth)
    every = n_pipe * n_dp * tokens

    w7, a7, g7, gathered = gather(weight, values, post_gain, n_pipe, n_dp)
    part = lax.dot_general(
        a7.reshape(n_dp * tokens, depth), w7, CONTRACT_LAST, preferred_element_type=jnp.float32
    ).astype(jnp.bfloat16)
    gathered = gathered.reshape(every, depth)
    own_part = lax.dot_general(
        gathered, weight, CONTRACT_LAST, preferred_element_type=jnp.float32
    ).astype(jnp.bfloat16)
    part, own_part = lax.optimization_barrier((part, own_part))
    pair_part = lax.ppermute(own_part, "tensor", [(0, 1), (1, 0)])
    top, delta, head_cols, top_cols = head(
        part.reshape(n_dp, tokens, width),
        embed_block,
        section_input.reshape(count, model),
        g7,
        final_gain.reshape(1, model),
        target_ids.reshape(count, 1) - block_offset[0],
        rest_lse.reshape(count, 1),
        n_pipe,
        n_dp,
    )

    first_row = block_offset[0] + lax.axis_index("tensor") * vrows
    column = lax.broadcasted_iota(jnp.int32, (count, vrows), 1)
    used = (token_ids.reshape(count, 1) - first_row == column).astype(jnp.bfloat16)
    delta = delta.reshape(count, vrows)
    terms = []
    for b in range(n_dp // n_pipe):
        head_term = lax.dot_general(
            delta, head_cols[:, b].reshape(count, width), CONTRACT_FIRST, preferred_element_type=jnp.float32
        )
        embed_term = math.sqrt(model) * lax.dot_general(
            used, top_cols[:, b].reshape(count, width), CONTRACT_FIRST, preferred_element_type=jnp.float32
        )
        terms.append((head_term + embed_term).astype(jnp.bfloat16).reshape(n_dp, vrows // n_dp, width))
    term = jnp.stack(terms)

    output = own_part.astype(jnp.float32) + pair_part.astype(jnp.float32)
    own = lax.axis_index("dp") * width
    gain = lax.dynamic_slice(post_gain, (0, own), (1, width))
    grad = top.reshape(every, width).astype(jnp.float32) * gain
    stat = jnp.stack([jnp.sum(output * output, axis=1), jnp.sum(output * grad, axis=1)])
    terms, stats = exchange(term, stat.reshape(2 * every // 128, 128), n_dp)
    tied = jnp.sum(terms.astype(jnp.float32), axis=0)
    tied = jnp.concatenate([tied[b] for b in range(n_dp // n_pipe)], axis=1)
    square, cross = jnp.sum(stats, axis=0).reshape(2, every)
    scale = lax.rsqrt(square / model + EPS)
    out_grad = scale[:, None] * (grad - output * (scale * scale * cross / model)[:, None])
    own_grad = lax.dot_general(
        out_grad.astype(jnp.bfloat16), gathered, CONTRACT_FIRST, preferred_element_type=jnp.float32
    )
    return (own_grad[None], tied)


def solution(mesh):
    in_specs = (
        P("pipe", "dp", "tensor"),
        P("pipe", None, "dp", "tensor"),
        P("pipe", None),
        P(None, "dp", None),
        P(),
        P("tensor", None),
        P(None, "dp"),
        P(None, "dp"),
        P(),
        P(None, "dp"),
    )
    out_specs = (P("pipe", "dp", "tensor"), P(("tensor", "dp"), "pipe"))
    return jax.shard_map(
        per_device, mesh=mesh, in_specs=in_specs, out_specs=out_specs, check_vma=False
    )
```

```python
import functools
import math

import jax
import jax.numpy as jnp
from jax import lax
from jax.experimental import pallas as pl
from jax.experimental.pallas import tpu as pltpu
from jax.sharding import PartitionSpec as P

EPS = 1e-06
CAP = 30.0
MESH = pl.DeviceIdType.MESH
ANY = pl.BlockSpec(memory_space=pl.ANY)
VMEM = pl.BlockSpec(memory_space=pltpu.VMEM)
CONTRACT_LAST = (((1,), (1,)), ((), ()))
W_CHUNK = 32
BACK_CHUNKS = 4
RING_CHUNKS = 3


def position():
    return lax.axis_index("pipe"), lax.axis_index("tensor"), lax.axis_index("dp")


def remote(src, dst, send_sem, recv_sem, device):
    return pltpu.make_async_remote_copy(
        src_ref=src,
        dst_ref=dst,
        send_sem=send_sem,
        recv_sem=recv_sem,
        device_id=device,
        device_id_type=MESH,
    )


def signal(sem, device):
    pl.semaphore_signal(sem, inc=1, device_id=device, device_id_type=MESH)


def greet_pipe(barrier, n_pipe):
    p, t, j = position()

    @pl.loop(1, n_pipe)
    def _(k):
        signal(barrier, (lax.rem(p + k, n_pipe), t, j))


def greet_dp(barrier, n_dp):
    p, t, j = position()

    @pl.loop(1, n_dp)
    def _(k):
        signal(barrier, (p, t, lax.rem(j + k, n_dp)))


def normalize(value):
    scale = lax.rsqrt(jnp.mean(value * value, axis=-1, keepdims=True) + EPS)
    return scale, value * scale


def flatten(blocks):
    return jnp.concatenate(blocks, axis=1)


def section_kernel(
    n_pipe, n_dp,
    w_ref, a_ref, gain_ref, embed_ref, input_ref, fgain_ref, target_ref, rest_ref, ids_ref, column_ref,
    proj_ref, tied_ref,
    embed, w, w7, a7, g7, every, rows_in, part, parts, sum_out, sum_in, delta_out, delta_all,
    back_out, back_in, block, hz, tz, col, tg, ps, ps_in, term, terms, stat, stats, coef,
    l_sem, w_recv, w_up, w_down, s_recv, s_send, g_recv, g_send, a_recv, a_send, v_recv, v_send, v_fwd,
    p_recv, p_send, sum_sem, back_recv, back_send, d_recv, d_send, h_recv, h_send, z_recv, z_send,
    c_recv, c_send, r_recv, r_up, r_down, o_recv, o_send, t_recv, t_send, st_recv, st_send,
):
    p, t, j = position()
    last = n_pipe - 1
    up_hops = n_pipe // 2
    down_hops = last - up_hops
    other = 1 - t
    core = lax.rem(j, 2)
    sibling = j + 1 - 2 * core
    n_chips = n_dp // 2
    chip = j // 2
    chunks = w_ref.shape[0] // W_CHUNK
    is_last = p == last
    up = (lax.rem(p + 1, n_pipe), t, j)
    down = (lax.rem(p + last, n_pipe), t, j)
    pair = (p, other, j)
    tokens, width = part.shape[1:]
    vrows, model = embed.shape
    per_pipe = n_dp // n_pipe
    plane = n_dp * tokens
    depth = w.shape[1]
    mine = pl.ds(pl.multiple_of(p * tokens, tokens), tokens)

    def dp_at(k):
        return lax.rem(j + k, n_dp)

    def pipe_at(k):
        return lax.rem(p + k, n_pipe)

    load_embed = pltpu.make_async_copy(embed_ref, embed, l_sem.at[0])
    load_weight = pltpu.make_async_copy(w_ref, w, l_sem.at[1])
    load_rows = pltpu.make_async_copy(input_ref.at[mine], rows_in, l_sem.at[2])
    load_values = pltpu.make_async_copy(a_ref, every.at[:, j], l_sem.at[3])
    load_weight.start()
    load_rows.start()

    barrier = pltpu.get_barrier_semaphore()
    greet_pipe(barrier, n_pipe)
    greet_dp(barrier, n_dp)

    @pl.loop(0, n_dp)
    def _(k):
        signal(barrier, (p, other, k))

    pl.semaphore_wait(barrier, 2 * n_dp - 1 + n_pipe - 1)

    def piece(ref, c):
        return ref.at[pl.ds(pl.multiple_of(c * W_CHUNK, W_CHUNK), W_CHUNK)]

    def slice_copy(q):
        return remote(a_ref.at[q], a7.at[j], s_send.at[q], s_recv, (q, t, j))

    def gain_copy(q):
        return remote(gain_ref, g7, g_send.at[q], g_recv, (q, t, j))

    def weight_copy(source, c, sems, device):
        return remote(piece(source, c), piece(w7, c), sems.at[c], w_recv.at[c], device)

    own_slice = pltpu.make_async_copy(a_ref.at[last], a7.at[j], l_sem.at[4])
    own_weight = pltpu.make_async_copy(w_ref, w7, l_sem.at[5])
    own_gain = pltpu.make_async_copy(gain_ref, g7, l_sem.at[6])

    @pl.when(is_last)
    def _():
        own_slice.start()

        @pl.loop(0, last)
        def _(q):
            slice_copy(q).start()

        @pl.loop(0, chunks)
        def _(c):
            weight_copy(w_ref, c, w_up, up).start()
            if down_hops:
                weight_copy(w_ref, c, w_down, down).start()

        @pl.loop(0, last)
        def _(q):
            gain_copy(q).start()

        own_weight.start()
        own_gain.start()

    load_values.start()
    load_embed.start()

    def values_copy(k):
        q = lax.rem(chip + k, n_chips) * 2 + core
        return remote(a_ref, every.at[:, j], v_send.at[k], v_recv.at[j], (p, t, q))

    def behind(k):
        return lax.rem(chip + n_chips - k, n_chips) * 2

    def forward_copy(k):
        owner = behind(k) + core
        return remote(
            every.at[:, owner], every.at[:, owner], v_fwd.at[k], v_recv.at[owner], (p, t, sibling)
        )

    def values_arrived(owner):
        return remote(a_ref, every.at[:, owner], v_send.at[0], v_recv.at[owner], (p, t, sibling))

    own_values = remote(a_ref, every.at[:, j], v_send.at[0], v_recv.at[j], (p, t, sibling))

    @pl.when(is_last)
    def _():
        own_slice.wait()

    @pl.when(jnp.logical_not(is_last))
    def _():
        slice_copy(p).wait_recv()

    def token_copy(k):
        return remote(a7.at[j], a7.at[j], a_send.at[k], a_recv.at[j], (p, t, dp_at(k)))

    def tokens_arrived(q):
        return remote(a7.at[j], a7.at[q], a_send.at[0], a_recv.at[q], (p, t, sibling))

    @pl.loop(1, n_dp)
    def _(k):
        token_copy(k).start()

    own_values.start()

    @pl.loop(1, n_chips)
    def _(k):
        values_copy(k).start()

    @pl.when(is_last)
    def _():
        own_weight.wait()
        own_gain.wait()

    @pl.when(jnp.logical_not(is_last))
    def _():
        @pl.loop(0, chunks)
        def _(c):
            weight_copy(w_ref, c, w_up, up).wait_recv()

            @pl.when(p < up_hops - 1)
            def _():
                weight_copy(w7, c, w_up, up).start()

            @pl.when(p > up_hops)
            def _():
                weight_copy(w7, c, w_down, down).start()

        gain_copy(p).wait_recv()

    @pl.loop(1, n_dp)
    def _(k):
        tokens_arrived(dp_at(k)).wait_recv()

    part[...] = (
        lax.dot_general(
            a7[...].reshape(plane, depth), w7[...], CONTRACT_LAST, preferred_element_type=jnp.float32
        )
        .astype(jnp.bfloat16)
        .reshape(n_dp, tokens, width)
    )

    def same_copy(k):
        q = dp_at(k)
        return remote(part.at[q], parts.at[t, j], p_send.at[0, k], p_recv.at[t, j], (p, t, q))

    def cross_copy(k):
        q = dp_at(k)
        return remote(part.at[q], parts.at[t, j], p_send.at[1, k], p_recv.at[t, j], (p, other, q))

    def part_arrived(group, q):
        return remote(part.at[q], parts.at[group, q], p_send.at[0, 0], p_recv.at[group, q], pair)

    @pl.loop(0, n_dp)
    def _(k):
        cross_copy(k).start()

    @pl.loop(1, n_dp)
    def _(k):
        same_copy(k).start()

    parts[t, j] = part[j]

    @pl.loop(1, n_chips)
    def _(k):
        values_arrived(behind(k) + core).wait_recv()
        forward_copy(k).start()

    load_rows.wait()
    load_embed.wait()

    @pl.loop(0, n_dp)
    def _(k):
        part_arrived(other, k).wait_recv()

    @pl.loop(1, n_dp)
    def _(k):
        part_arrived(t, dp_at(k)).wait_recv()

    output = flatten(
        [parts[0, q].astype(jnp.float32) + parts[1, q].astype(jnp.float32) for q in range(n_dp)]
    )
    _, normed = normalize(output)
    resid = rows_in[...].astype(jnp.float32) + normed * g7[...]
    y_scale, y_normed = normalize(resid)
    head_in = (y_normed * fgain_ref[...]).astype(jnp.bfloat16)
    for b in range(n_dp):
        block[0, b] = head_in[:, b * width:(b + 1) * width]

    def line_copy(slot, dst, send, recv, k):
        q = pipe_at(k)
        return remote(
            block.at[slot, pl.ds(q * per_pipe, per_pipe)], dst.at[p], send.at[k], recv.at[p], (q, t, j)
        )

    def line_arrived(slot, dst, send, recv, q):
        return remote(block.at[slot, pl.ds(0, per_pipe)], dst.at[q], send.at[0], recv.at[q], (q, t, j))

    @pl.loop(1, n_pipe)
    def _(k):
        line_copy(0, hz, h_send, h_recv, k).start()

    for b in range(per_pipe):
        hz[p, b] = block[0, p * per_pipe + b]

    raw = lax.dot_general(head_in, embed[...], CONTRACT_LAST, preferred_element_type=jnp.float32)
    capped = jnp.tanh(raw / CAP)
    logits = CAP * capped
    own_sum = jnp.sum(jnp.exp(logits), axis=1, keepdims=True)
    sum_out[...] = jnp.broadcast_to(own_sum, sum_out.shape)
    sums = remote(sum_out, sum_in, sum_sem.at[0], sum_sem.at[1], pair)
    sums.start()
    lane = lax.broadcasted_iota(jnp.int32, (tokens, vrows), 1)
    hit = (target_ref[mine, :] - t * vrows == lane).astype(jnp.float32)
    slope = 1.0 - capped * capped
    sums.wait_recv()
    log_total = jnp.log(own_sum + sum_in[:, 0:1])
    rest = rest_ref[mine, :]
    lse = jnp.maximum(rest, log_total) + jnp.log(1.0 + jnp.exp(-jnp.abs(rest - log_total)))
    delta = ((jnp.exp(logits - lse) - hit) * slope).astype(jnp.bfloat16)
    delta_out[...] = delta
    delta_all[p] = delta

    step = model // BACK_CHUNKS
    copies = []
    for c in range(BACK_CHUNKS):
        grad = jnp.dot(delta, embed[:, c * step:(c + 1) * step], preferred_element_type=jnp.float32)
        back_out[c] = grad.astype(jnp.bfloat16)
        copy = remote(back_out.at[c], back_in.at[c], back_send.at[c], back_recv.at[c], pair)
        copy.start()
        copies.append(copy)

    def delta_copy(k):
        return remote(delta_out, delta_all.at[p], d_send.at[k], d_recv.at[p], (pipe_at(k), t, j))

    def delta_arrived(q):
        return remote(delta_out, delta_all.at[q], d_send.at[0], d_recv.at[q], (q, t, j))

    @pl.loop(1, n_pipe)
    def _(k):
        delta_copy(k).start()

    load_weight.wait()
    load_values.wait()
    values_arrived(sibling).wait_recv()

    @pl.loop(1, n_chips)
    def _(k):
        values_arrived(behind(k) + 1 - core).wait_recv()

    def output_copy(q):
        return remote(ps.at[q], ps_in.at[q], o_send.at[q], o_recv.at[q], pair)

    @pl.loop(0, n_pipe)
    def _(q):
        ps[q] = lax.dot_general(
            w[...], every[q].reshape(plane, depth), CONTRACT_LAST, preferred_element_type=jnp.float32
        ).astype(jnp.bfloat16)
        output_copy(q).start()

    grads = []
    for c in range(BACK_CHUNKS):
        copies[c].wait_recv()
        grads.append(back_out[c].astype(jnp.float32) + back_in[c].astype(jnp.float32))
    grad = flatten(grads) * fgain_ref[...]
    top = y_scale * (grad - y_normed * jnp.mean(grad * y_normed, axis=-1, keepdims=True))
    top = top.astype(jnp.bfloat16)
    for b in range(n_dp):
        block[1, b] = top[:, b * width:(b + 1) * width]

    def column_copy(k):
        q = dp_at(k)
        return remote(block.at[1, q], col.at[j], c_send.at[k], c_recv.at[j], (p, t, q))

    def column_arrived(q):
        return remote(block.at[1, q], col.at[q], c_send.at[0], c_recv.at[q], pair)

    @pl.loop(1, n_dp)
    def _(k):
        column_copy(k).start()

    @pl.loop(1, n_pipe)
    def _(k):
        line_copy(1, tz, z_send, z_recv, k).start()

    col[j] = block[1, j]
    for b in range(per_pipe):
        tz[p, b] = block[1, p * per_pipe + b]

    @pl.loop(1, n_dp)
    def _(k):
        column_arrived(dp_at(k)).wait_recv()

    tg[p] = col[...].reshape(plane, width).T

    ring_rows = width // RING_CHUNKS

    def ring_copy(source, c, send, device):
        ref = tg.at[source, pl.ds(c * ring_rows, ring_rows)]
        return remote(ref, ref, send.at[source, c], r_recv.at[source, c], device)

    def above(s):
        return lax.rem(p + s, n_pipe)

    def below(s):
        return lax.rem(p + n_pipe - s, n_pipe)

    for c in range(RING_CHUNKS):
        ring_copy(p, c, r_up, up).start()
        if down_hops:
            ring_copy(p, c, r_down, down).start()

    @pl.loop(1, n_pipe)
    def _(k):
        q = pipe_at(k)
        line_arrived(0, hz, h_send, h_recv, q).wait_recv()
        line_arrived(1, tz, z_send, z_recv, q).wait_recv()
        delta_arrived(q).wait_recv()

    count = n_pipe * tokens
    head_cols = flatten([hz[:, b].reshape(count, width) for b in range(per_pipe)])
    top_cols = flatten([tz[:, b].reshape(count, width) for b in range(per_pipe)])
    delta_rows = delta_all[...].reshape(count, vrows).T
    row = lax.broadcasted_iota(jnp.int32, (vrows, count), 0)
    used = (ids_ref[...] == row).astype(jnp.bfloat16)
    term[...] = (
        (
            jnp.dot(delta_rows, head_cols, preferred_element_type=jnp.float32)
            + math.sqrt(model) * jnp.dot(used, top_cols, preferred_element_type=jnp.float32)
        )
        .astype(jnp.bfloat16)
        .reshape(term.shape)
    )

    def term_copy(k):
        q = dp_at(k)
        return remote(term.at[q], terms.at[j], t_send.at[k], t_recv.at[j], (p, t, q))

    def term_arrived(q):
        return remote(term.at[q], terms.at[q], t_send.at[0], t_recv.at[q], pair)

    @pl.loop(1, n_dp)
    def _(k):
        term_copy(k).start()

    terms[j] = term[j]

    for s in range(1, up_hops + 1):
        for c in range(RING_CHUNKS):
            ring_copy(below(s), c, r_up, up).wait_recv()
            if s < up_hops:
                ring_copy(below(s), c, r_up, up).start()
            if s <= down_hops:
                ring_copy(above(s), c, r_down, down).wait_recv()
                if s < down_hops:
                    ring_copy(above(s), c, r_down, down).start()

    @pl.loop(0, n_pipe)
    def _(q):
        output_copy(q).wait_recv()
        out = ps[q].astype(jnp.float32) + ps_in[q].astype(jnp.float32)
        grad = tg[q].astype(jnp.float32) * column_ref[...]
        stat[pl.ds(q, 1), :] = jnp.sum(out * out, axis=0, keepdims=True)
        stat[pl.ds(n_pipe + q, 1), :] = jnp.sum(out * grad, axis=0, keepdims=True)

    def stat_copy(k):
        return remote(stat, stats.at[j], st_send.at[k], st_recv.at[j], (p, t, dp_at(k)))

    def stat_arrived(q):
        return remote(stat, stats.at[q], st_send.at[0], st_recv.at[q], pair)

    @pl.loop(1, n_dp)
    def _(k):
        stat_copy(k).start()

    stats[j] = stat[...]

    @pl.loop(1, n_dp)
    def _(k):
        term_arrived(dp_at(k)).wait_recv()

    total = terms[0].astype(jnp.float32)
    for q in range(1, n_dp):
        total = total + terms[q].astype(jnp.float32)
    tied_ref[...] = total

    @pl.loop(1, n_dp)
    def _(k):
        stat_arrived(dp_at(k)).wait_recv()

    both = jnp.sum(stats[...], axis=0)
    scale = lax.rsqrt(both[:n_pipe] / model + EPS)
    coef[0:n_pipe] = scale
    coef[n_pipe:2 * n_pipe] = scale * scale * both[n_pipe:] / model
    proj_ref[...] = jnp.zeros_like(proj_ref)

    @pl.loop(0, n_pipe)
    def _(q):
        out = ps[q].astype(jnp.float32) + ps_in[q].astype(jnp.float32)
        grad = tg[q].astype(jnp.float32) * column_ref[...]
        out_grad = coef[pl.ds(q, 1), :] * (grad - out * coef[pl.ds(n_pipe + q, 1), :])
        proj_ref[...] += jnp.dot(
            out_grad.astype(jnp.bfloat16),
            every[q].reshape(plane, depth),
            preferred_element_type=jnp.float32,
        )

    @pl.when(is_last)
    def _():
        @pl.loop(0, last)
        def _(q):
            slice_copy(q).wait_send()
            gain_copy(q).wait_send()

        @pl.loop(0, chunks)
        def _(c):
            weight_copy(w_ref, c, w_up, up).wait_send()
            if down_hops:
                weight_copy(w_ref, c, w_down, down).wait_send()

    @pl.when(jnp.logical_not(is_last))
    def _():
        @pl.when(p < up_hops - 1)
        def _():
            @pl.loop(0, chunks)
            def _(c):
                weight_copy(w7, c, w_up, up).wait_send()

        @pl.when(p > up_hops)
        def _():
            @pl.loop(0, chunks)
            def _(c):
                weight_copy(w7, c, w_down, down).wait_send()

    own_values.wait_send()
    cross_copy(0).wait_send()
    sums.wait_send()

    @pl.loop(1, n_chips)
    def _(k):
        values_copy(k).wait_send()
        forward_copy(k).wait_send()

    @pl.loop(1, n_dp)
    def _(k):
        token_copy(k).wait_send()
        cross_copy(k).wait_send()
        same_copy(k).wait_send()
        column_copy(k).wait_send()
        term_copy(k).wait_send()
        stat_copy(k).wait_send()

    @pl.loop(1, n_pipe)
    def _(k):
        line_copy(0, hz, h_send, h_recv, k).wait_send()
        line_copy(1, tz, z_send, z_recv, k).wait_send()
        delta_copy(k).wait_send()

    @pl.loop(0, n_pipe)
    def _(q):
        output_copy(q).wait_send()

    for copy in copies:
        copy.wait_send()
    for c in range(RING_CHUNKS):
        for s in range(up_hops):
            ring_copy(below(s), c, r_up, up).wait_send()
        for s in range(down_hops):
            ring_copy(above(s), c, r_down, down).wait_send()


def sections(weight, values, gain, embed, section_input, final_gain, target, rest, ids, column, n_pipe, n_dp):
    dma = pltpu.SemaphoreType.DMA
    vmem = pltpu.VMEM
    half, full = jnp.bfloat16, jnp.float32
    width, depth = weight.shape
    tokens = values.shape[1]
    vrows, model = embed.shape
    per_pipe = n_dp // n_pipe
    step = model // BACK_CHUNKS
    plane = n_dp * tokens
    rows = vrows // n_dp
    cols = per_pipe * width
    chunks = width // W_CHUNK
    return pl.pallas_call(
        functools.partial(section_kernel, n_pipe, n_dp),
        out_shape=(
            jax.ShapeDtypeStruct((width, depth), full),
            jax.ShapeDtypeStruct((rows, cols), full),
        ),
        in_specs=[ANY] * 5 + [VMEM] * 5,
        out_specs=(VMEM, VMEM),
        scratch_shapes=[
            vmem((vrows, model), half),
            vmem((width, depth), half),
            vmem((width, depth), half),
            vmem((n_dp, tokens, depth), half),
            vmem((1, model), full),
            vmem((n_pipe, n_dp, tokens, depth), half),
            vmem((tokens, model), half),
            vmem((n_dp, tokens, width), half),
            vmem((2, n_dp, tokens, width), half),
            vmem((tokens, 128), full),
            vmem((tokens, 128), full),
            vmem((tokens, vrows), half),
            vmem((n_pipe, tokens, vrows), half),
            vmem((BACK_CHUNKS, tokens, step), half),
            vmem((BACK_CHUNKS, tokens, step), half),
            vmem((2, n_dp, tokens, width), half),
            vmem((n_pipe, per_pipe, tokens, width), half),
            vmem((n_pipe, per_pipe, tokens, width), half),
            vmem((n_dp, tokens, width), half),
            vmem((n_pipe, width, plane), half),
            vmem((n_pipe, width, plane), half),
            vmem((n_pipe, width, plane), half),
            vmem((n_dp, rows, cols), half),
            vmem((n_dp, rows, cols), half),
            vmem((2 * n_pipe, plane), full),
            vmem((n_dp, 2 * n_pipe, plane), full),
            vmem((2 * n_pipe, plane), full),
            dma((7,)), dma((chunks,)), dma((chunks,)), dma((chunks,)),
            dma, dma((n_pipe,)), dma, dma((n_pipe,)),
            dma((n_dp,)), dma((n_dp,)), dma((n_dp,)), dma((n_dp // 2,)), dma((n_dp // 2,)),
            dma((2, n_dp)), dma((2, n_dp)), dma((2,)), dma((BACK_CHUNKS,)), dma((BACK_CHUNKS,)),
            dma((n_pipe,)), dma((n_pipe,)), dma((n_pipe,)), dma((n_pipe,)), dma((n_pipe,)), dma((n_pipe,)),
            dma((n_dp,)), dma((n_dp,)),
            dma((n_pipe, RING_CHUNKS)), dma((n_pipe, RING_CHUNKS)), dma((n_pipe, RING_CHUNKS)),
            dma((n_pipe,)), dma((n_pipe,)), dma((n_dp,)), dma((n_dp,)), dma((n_dp,)), dma((n_dp,)),
        ],
        compiler_params=pltpu.CompilerParams(
            collective_id=0, has_side_effects=True, vmem_limit_bytes=56 * 1024 * 1024
        ),
        name="sections",
    )(weight, values, gain, embed, section_input, final_gain, target, rest, ids, column)


def per_device(
    section_proj,
    attn_values,
    post_gain,
    section_input,
    final_gain,
    embed_block,
    token_ids,
    target_ids,
    block_offset,
    rest_lse,
):
    n_pipe, n_dp = lax.axis_size("pipe"), lax.axis_size("dp")
    weight = section_proj[0]
    width, depth = weight.shape
    model = section_input.shape[2]
    vrows = embed_block.shape[0]
    count = section_input.shape[0] * section_input.shape[1]
    first_row = block_offset[0] + lax.axis_index("tensor") * vrows
    column = lax.dynamic_slice(post_gain, (0, lax.axis_index("dp") * width), (1, width))
    own_grad, tied = sections(
        weight,
        attn_values.reshape(n_pipe, count // n_pipe, depth),
        post_gain,
        embed_block,
        section_input.reshape(count, model),
        final_gain.reshape(1, model),
        target_ids.reshape(count, 1) - block_offset[0],
        rest_lse.reshape(count, 1),
        token_ids.reshape(1, count) - first_row,
        column.reshape(width, 1),
        n_pipe,
        n_dp,
    )
    return (own_grad[None], tied)


def solution(mesh):
    in_specs = (
        P("pipe", "dp", "tensor"),
        P("pipe", None, "dp", "tensor"),
        P("pipe", None),
        P(None, "dp", None),
        P(),
        P("tensor", None),
        P(None, "dp"),
        P(None, "dp"),
        P(),
        P(None, "dp"),
    )
    out_specs = (P("pipe", "dp", "tensor"), P(("tensor", "dp"), "pipe"))
    return jax.shard_map(
        per_device, mesh=mesh, in_specs=in_specs, out_specs=out_specs, check_vma=False
    )
```

```python
import functools
import math

import jax
import jax.numpy as jnp
from jax import lax
from jax.experimental import pallas as pl
from jax.experimental.pallas import tpu as pltpu
from jax.sharding import PartitionSpec as P

EPS = 1e-06
CAP = 30.0
MESH = pl.DeviceIdType.MESH
ANY = pl.BlockSpec(memory_space=pl.ANY)
VMEM = pl.BlockSpec(memory_space=pltpu.VMEM)
SMEM = pl.BlockSpec(memory_space=pltpu.SMEM)
CONTRACT_LAST = (((1,), (1,)), ((), ()))
W_CHUNK = 32
BACK_CHUNKS = 4
RING_CHUNKS = 3


def position():
    return lax.axis_index("pipe"), lax.axis_index("tensor"), lax.axis_index("dp")


def remote(src, dst, send_sem, recv_sem, device):
    return pltpu.make_async_remote_copy(
        src_ref=src,
        dst_ref=dst,
        send_sem=send_sem,
        recv_sem=recv_sem,
        device_id=device,
        device_id_type=MESH,
    )


def signal(sem, device):
    pl.semaphore_signal(sem, inc=1, device_id=device, device_id_type=MESH)


def greet_pipe(barrier, n_pipe):
    p, t, j = position()

    @pl.loop(1, n_pipe)
    def _(k):
        signal(barrier, (lax.rem(p + k, n_pipe), t, j))


def greet_dp(barrier, n_dp):
    p, t, j = position()

    @pl.loop(1, n_dp)
    def _(k):
        signal(barrier, (p, t, lax.rem(j + k, n_dp)))


def normalize(value):
    scale = lax.rsqrt(jnp.mean(value * value, axis=-1, keepdims=True) + EPS)
    return scale, value * scale


def own_tokens(ref, first, tokens):
    micro, per = ref.shape
    lane = lax.broadcasted_iota(jnp.int32, (tokens, per), 1)
    token = lax.broadcasted_iota(jnp.int32, (tokens, per), 0) + first
    found = jnp.zeros((tokens, per), jnp.float32)
    for m in range(micro):
        row = jnp.broadcast_to(ref[m:m + 1, :].astype(jnp.float32), (tokens, per))
        found = found + jnp.where(lane + m * per == token, row, 0.0)
    return jnp.sum(found, axis=1, keepdims=True)


def flatten(blocks):
    return jnp.concatenate(blocks, axis=1)


def section_kernel(
    n_pipe, n_dp,
    w_ref, a_ref, gain_ref, embed_ref, input_ref, fgain_ref, target_ref, rest_ref, ids_ref, offset_ref,
    proj_ref, tied_ref,
    embed, w, w7, a7, g7, every, rows_in, part, parts, sum_out, sum_in, delta_out, delta_all,
    back_out, back_in, block, hz, tz, col, tg, ps, ps_in, term, terms, stat, stats, coef, gains, column,
    l_sem, w_recv, w_up, w_down, s_recv, s_send, g_recv, g_send, a_recv, a_send, v_recv, v_send, v_fwd,
    p_recv, p_send, sum_sem, back_recv, back_send, d_recv, d_send, h_recv, h_send, z_recv, z_send,
    c_recv, c_send, r_recv, r_up, r_down, o_recv, o_send, t_recv, t_send, st_recv, st_send,
):
    p, t, j = position()
    last = n_pipe - 1
    up_hops = n_pipe // 2
    down_hops = last - up_hops
    other = 1 - t
    core = lax.rem(j, 2)
    sibling = j + 1 - 2 * core
    n_chips = n_dp // 2
    chip = j // 2
    chunks = w_ref.shape[0] // W_CHUNK
    is_last = p == last
    up = (lax.rem(p + 1, n_pipe), t, j)
    down = (lax.rem(p + last, n_pipe), t, j)
    pair = (p, other, j)
    tokens, width = part.shape[1:]
    vrows, model = embed.shape
    per_pipe = n_dp // n_pipe
    plane = n_dp * tokens
    depth = w.shape[1]
    mine = pl.ds(pl.multiple_of(p * tokens, tokens), tokens)

    def dp_at(k):
        return lax.rem(j + k, n_dp)

    def pipe_at(k):
        return lax.rem(p + k, n_pipe)

    load_embed = pltpu.make_async_copy(embed_ref, embed, l_sem.at[0])
    load_weight = pltpu.make_async_copy(w_ref, w, l_sem.at[1])
    load_rows = pltpu.make_async_copy(input_ref.at[mine], rows_in, l_sem.at[2])
    load_values = pltpu.make_async_copy(a_ref, every.at[:, j], l_sem.at[3])
    load_gains = pltpu.make_async_copy(gain_ref, gains, l_sem.at[7])
    load_weight.start()
    load_rows.start()
    load_gains.start()

    barrier = pltpu.get_barrier_semaphore()
    greet_pipe(barrier, n_pipe)
    greet_dp(barrier, n_dp)

    @pl.loop(0, n_dp)
    def _(k):
        signal(barrier, (p, other, k))

    pl.semaphore_wait(barrier, 2 * n_dp - 1 + n_pipe - 1)

    def piece(ref, c):
        return ref.at[pl.ds(pl.multiple_of(c * W_CHUNK, W_CHUNK), W_CHUNK)]

    def slice_copy(q):
        return remote(a_ref.at[q], a7.at[j], s_send.at[q], s_recv, (q, t, j))

    def gain_copy(q):
        return remote(gain_ref, g7, g_send.at[q], g_recv, (q, t, j))

    def weight_copy(source, c, sems, device):
        return remote(piece(source, c), piece(w7, c), sems.at[c], w_recv.at[c], device)

    def values_copy(k):
        q = lax.rem(chip + k, n_chips) * 2 + core
        return remote(a_ref, every.at[:, j], v_send.at[k], v_recv.at[j], (p, t, q))

    def behind(k):
        return lax.rem(chip + n_chips - k, n_chips) * 2

    def forward_copy(k):
        owner = behind(k) + core
        return remote(
            every.at[:, owner], every.at[:, owner], v_fwd.at[k], v_recv.at[owner], (p, t, sibling)
        )

    def values_arrived(owner):
        return remote(a_ref, every.at[:, owner], v_send.at[0], v_recv.at[owner], (p, t, sibling))

    def sibling_copy():
        return remote(a_ref, every.at[:, j], v_send.at[0], v_recv.at[j], (p, t, sibling))

    own_slice = pltpu.make_async_copy(a_ref.at[last], a7.at[j], l_sem.at[4])
    own_weight = pltpu.make_async_copy(w_ref, w7, l_sem.at[5])
    own_gain = pltpu.make_async_copy(gain_ref, g7, l_sem.at[6])

    @pl.when(is_last)
    def _():
        own_slice.start()

        @pl.loop(0, last)
        def _(q):
            slice_copy(q).start()

        @pl.loop(0, chunks)
        def _(c):
            weight_copy(w_ref, c, w_up, up).start()
            if down_hops:
                weight_copy(w_ref, c, w_down, down).start()

        @pl.loop(0, last)
        def _(q):
            gain_copy(q).start()

        own_weight.start()
        own_gain.start()

    @pl.loop(1, n_chips)
    def _(k):
        values_copy(k).start()

    sibling_copy().start()
    load_values.start()
    load_embed.start()

    load_gains.wait()
    wide = pl.cdiv(width, 128) * 128
    turned = pltpu.roll(
        jnp.broadcast_to(gains[...], (8, model)), lax.rem(model - width * j, model), 1
    )
    column[...] = turned[:, :wide].T[:width, 0:1]

    @pl.when(is_last)
    def _():
        own_slice.wait()

    @pl.when(jnp.logical_not(is_last))
    def _():
        slice_copy(p).wait_recv()

    def token_copy(k):
        return remote(a7.at[j], a7.at[j], a_send.at[k], a_recv.at[j], (p, t, dp_at(k)))

    def tokens_arrived(q):
        return remote(a7.at[j], a7.at[q], a_send.at[0], a_recv.at[q], (p, t, sibling))

    @pl.loop(1, n_dp)
    def _(k):
        token_copy(k).start()

    @pl.when(is_last)
    def _():
        own_weight.wait()
        own_gain.wait()

    @pl.when(jnp.logical_not(is_last))
    def _():
        @pl.loop(0, chunks)
        def _(c):
            weight_copy(w_ref, c, w_up, up).wait_recv()

            @pl.when(p < up_hops - 1)
            def _():
                weight_copy(w7, c, w_up, up).start()

            @pl.when(p > up_hops)
            def _():
                weight_copy(w7, c, w_down, down).start()

        gain_copy(p).wait_recv()

    @pl.loop(1, n_dp)
    def _(k):
        tokens_arrived(dp_at(k)).wait_recv()

    part[...] = (
        lax.dot_general(
            a7[...].reshape(plane, depth), w7[...], CONTRACT_LAST, preferred_element_type=jnp.float32
        )
        .astype(jnp.bfloat16)
        .reshape(n_dp, tokens, width)
    )

    def same_copy(k):
        q = dp_at(k)
        return remote(part.at[q], parts.at[t, j], p_send.at[0, k], p_recv.at[t, j], (p, t, q))

    def cross_copy(k):
        q = dp_at(k)
        return remote(part.at[q], parts.at[t, j], p_send.at[1, k], p_recv.at[t, j], (p, other, q))

    def part_arrived(group, q):
        return remote(part.at[q], parts.at[group, q], p_send.at[0, 0], p_recv.at[group, q], pair)

    @pl.loop(0, n_dp)
    def _(k):
        cross_copy(k).start()

    @pl.loop(1, n_dp)
    def _(k):
        same_copy(k).start()

    parts[t, j] = part[j]

    @pl.loop(1, n_chips)
    def _(k):
        values_arrived(behind(k) + core).wait_recv()
        forward_copy(k).start()

    load_weight.wait()
    load_values.wait()
    values_arrived(sibling).wait_recv()

    @pl.loop(1, n_chips)
    def _(k):
        values_arrived(behind(k) + 1 - core).wait_recv()

    def output_copy(q):
        return remote(ps.at[q], ps_in.at[q], o_send.at[q], o_recv.at[q], pair)

    @pl.loop(0, n_pipe)
    def _(q):
        ps[q] = lax.dot_general(
            w[...], every[q].reshape(plane, depth), CONTRACT_LAST, preferred_element_type=jnp.float32
        ).astype(jnp.bfloat16)
        output_copy(q).start()

    load_rows.wait()
    load_embed.wait()

    @pl.loop(0, n_dp)
    def _(k):
        part_arrived(other, k).wait_recv()

    @pl.loop(1, n_dp)
    def _(k):
        part_arrived(t, dp_at(k)).wait_recv()

    output = flatten(
        [parts[0, q].astype(jnp.float32) + parts[1, q].astype(jnp.float32) for q in range(n_dp)]
    )
    _, normed = normalize(output)
    final_gain = fgain_ref[...].reshape(1, model)
    resid = rows_in[...].astype(jnp.float32) + normed * g7[...]
    y_scale, y_normed = normalize(resid)
    head_in = (y_normed * final_gain).astype(jnp.bfloat16)
    for b in range(n_dp):
        block[0, b] = head_in[:, b * width:(b + 1) * width]

    def line_copy(slot, dst, send, recv, k):
        q = pipe_at(k)
        return remote(
            block.at[slot, pl.ds(q * per_pipe, per_pipe)], dst.at[p], send.at[k], recv.at[p], (q, t, j)
        )

    def line_arrived(slot, dst, send, recv, q):
        return remote(block.at[slot, pl.ds(0, per_pipe)], dst.at[q], send.at[0], recv.at[q], (q, t, j))

    @pl.loop(1, n_pipe)
    def _(k):
        line_copy(0, hz, h_send, h_recv, k).start()

    for b in range(per_pipe):
        hz[p, b] = block[0, p * per_pipe + b]

    raw = lax.dot_general(head_in, embed[...], CONTRACT_LAST, preferred_element_type=jnp.float32)
    capped = jnp.tanh(raw / CAP)
    logits = CAP * capped
    own_sum = jnp.sum(jnp.exp(logits), axis=1, keepdims=True)
    sum_out[...] = jnp.broadcast_to(own_sum, sum_out.shape)

    def sum_copy():
        return remote(sum_out, sum_in, sum_sem.at[0], sum_sem.at[1], pair)

    sum_copy().start()
    lane = lax.broadcasted_iota(jnp.int32, (tokens, vrows), 1)
    first_row = offset_ref[0] + t * vrows
    target = own_tokens(target_ref, p * tokens, tokens)
    hit = (target == (first_row + lane).astype(jnp.float32)).astype(jnp.float32)
    slope = 1.0 - capped * capped
    sum_copy().wait_recv()
    log_total = jnp.log(own_sum + sum_in[:, 0:1])
    rest = own_tokens(rest_ref, p * tokens, tokens)
    lse = jnp.maximum(rest, log_total) + jnp.log(1.0 + jnp.exp(-jnp.abs(rest - log_total)))
    delta = ((jnp.exp(logits - lse) - hit) * slope).astype(jnp.bfloat16)
    delta_out[...] = delta
    delta_all[p] = delta

    step = model // BACK_CHUNKS

    def back_copy(c):
        return remote(back_out.at[c], back_in.at[c], back_send.at[c], back_recv.at[c], pair)

    for c in range(BACK_CHUNKS):
        grad = jnp.dot(delta, embed[:, c * step:(c + 1) * step], preferred_element_type=jnp.float32)
        back_out[c] = grad.astype(jnp.bfloat16)
        back_copy(c).start()

    def delta_copy(k):
        return remote(delta_out, delta_all.at[p], d_send.at[k], d_recv.at[p], (pipe_at(k), t, j))

    def delta_arrived(q):
        return remote(delta_out, delta_all.at[q], d_send.at[0], d_recv.at[q], (q, t, j))

    @pl.loop(1, n_pipe)
    def _(k):
        delta_copy(k).start()

    grads = []
    for c in range(BACK_CHUNKS):
        back_copy(c).wait_recv()
        grads.append(back_out[c].astype(jnp.float32) + back_in[c].astype(jnp.float32))
    grad = flatten(grads) * final_gain
    top = y_scale * (grad - y_normed * jnp.mean(grad * y_normed, axis=-1, keepdims=True))
    top = top.astype(jnp.bfloat16)
    for b in range(n_dp):
        block[1, b] = top[:, b * width:(b + 1) * width]

    def column_copy(k):
        q = dp_at(k)
        return remote(block.at[1, q], col.at[j], c_send.at[k], c_recv.at[j], (p, t, q))

    def column_arrived(q):
        return remote(block.at[1, q], col.at[q], c_send.at[0], c_recv.at[q], pair)

    @pl.loop(1, n_dp)
    def _(k):
        column_copy(k).start()

    @pl.loop(1, n_pipe)
    def _(k):
        line_copy(1, tz, z_send, z_recv, k).start()

    col[j] = block[1, j]
    for b in range(per_pipe):
        tz[p, b] = block[1, p * per_pipe + b]

    @pl.loop(1, n_dp)
    def _(k):
        column_arrived(dp_at(k)).wait_recv()

    tg[p] = col[...].reshape(plane, width).T

    ring_rows = width // RING_CHUNKS

    def ring_copy(source, c, send, device):
        ref = tg.at[source, pl.ds(c * ring_rows, ring_rows)]
        return remote(ref, ref, send.at[source, c], r_recv.at[source, c], device)

    def above(s):
        return lax.rem(p + s, n_pipe)

    def below(s):
        return lax.rem(p + n_pipe - s, n_pipe)

    for c in range(RING_CHUNKS):
        ring_copy(p, c, r_up, up).start()
        if down_hops:
            ring_copy(p, c, r_down, down).start()

    @pl.loop(1, n_pipe)
    def _(k):
        q = pipe_at(k)
        line_arrived(0, hz, h_send, h_recv, q).wait_recv()
        line_arrived(1, tz, z_send, z_recv, q).wait_recv()
        delta_arrived(q).wait_recv()

    count = n_pipe * tokens
    head_cols = flatten([hz[:, b].reshape(count, width) for b in range(per_pipe)])
    top_cols = flatten([tz[:, b].reshape(count, width) for b in range(per_pipe)])
    delta_rows = delta_all[...].reshape(count, vrows).T
    row = lax.broadcasted_iota(jnp.int32, (vrows, count), 0)
    ids = flatten([ids_ref[m:m + 1, :] for m in range(ids_ref.shape[0])])
    used = (ids == first_row + row).astype(jnp.bfloat16)
    term[...] = (
        (
            jnp.dot(delta_rows, head_cols, preferred_element_type=jnp.float32)
            + math.sqrt(model) * jnp.dot(used, top_cols, preferred_element_type=jnp.float32)
        )
        .astype(jnp.bfloat16)
        .reshape(term.shape)
    )

    def term_copy(k):
        q = dp_at(k)
        return remote(term.at[q], terms.at[j], t_send.at[k], t_recv.at[j], (p, t, q))

    def term_arrived(q):
        return remote(term.at[q], terms.at[q], t_send.at[0], t_recv.at[q], pair)

    @pl.loop(1, n_dp)
    def _(k):
        term_copy(k).start()

    terms[j] = term[j]

    for s in range(1, up_hops + 1):
        for c in range(RING_CHUNKS):
            ring_copy(below(s), c, r_up, up).wait_recv()
            if s < up_hops:
                ring_copy(below(s), c, r_up, up).start()
            if s <= down_hops:
                ring_copy(above(s), c, r_down, down).wait_recv()
                if s < down_hops:
                    ring_copy(above(s), c, r_down, down).start()

    @pl.loop(0, n_pipe)
    def _(q):
        output_copy(q).wait_recv()
        out = ps[q].astype(jnp.float32) + ps_in[q].astype(jnp.float32)
        grad = tg[q].astype(jnp.float32) * column[...]
        stat[pl.ds(q, 1), :] = jnp.sum(out * out, axis=0, keepdims=True)
        stat[pl.ds(n_pipe + q, 1), :] = jnp.sum(out * grad, axis=0, keepdims=True)

    def stat_copy(k):
        return remote(stat, stats.at[j], st_send.at[k], st_recv.at[j], (p, t, dp_at(k)))

    def stat_arrived(q):
        return remote(stat, stats.at[q], st_send.at[0], st_recv.at[q], pair)

    @pl.loop(1, n_dp)
    def _(k):
        stat_copy(k).start()

    stats[j] = stat[...]

    @pl.loop(1, n_dp)
    def _(k):
        term_arrived(dp_at(k)).wait_recv()

    total = terms[0].astype(jnp.float32)
    for q in range(1, n_dp):
        total = total + terms[q].astype(jnp.float32)
    tied_ref[...] = total

    @pl.loop(1, n_dp)
    def _(k):
        stat_arrived(dp_at(k)).wait_recv()

    both = jnp.sum(stats[...], axis=0)
    scale = lax.rsqrt(both[:n_pipe] / model + EPS)
    coef[0:n_pipe] = scale
    coef[n_pipe:2 * n_pipe] = scale * scale * both[n_pipe:] / model
    proj_ref[...] = jnp.zeros_like(proj_ref)

    @pl.loop(0, n_pipe)
    def _(q):
        out = ps[q].astype(jnp.float32) + ps_in[q].astype(jnp.float32)
        grad = tg[q].astype(jnp.float32) * column[...]
        out_grad = coef[pl.ds(q, 1), :] * (grad - out * coef[pl.ds(n_pipe + q, 1), :])
        proj_ref[...] += jnp.dot(
            out_grad.astype(jnp.bfloat16),
            every[q].reshape(plane, depth),
            preferred_element_type=jnp.float32,
        )

    @pl.when(is_last)
    def _():
        @pl.loop(0, last)
        def _(q):
            slice_copy(q).wait_send()
            gain_copy(q).wait_send()

        @pl.loop(0, chunks)
        def _(c):
            weight_copy(w_ref, c, w_up, up).wait_send()
            if down_hops:
                weight_copy(w_ref, c, w_down, down).wait_send()

    @pl.when(jnp.logical_not(is_last))
    def _():
        @pl.when(p < up_hops - 1)
        def _():
            @pl.loop(0, chunks)
            def _(c):
                weight_copy(w7, c, w_up, up).wait_send()

        @pl.when(p > up_hops)
        def _():
            @pl.loop(0, chunks)
            def _(c):
                weight_copy(w7, c, w_down, down).wait_send()

    sibling_copy().wait_send()
    cross_copy(0).wait_send()
    sum_copy().wait_send()

    @pl.loop(1, n_chips)
    def _(k):
        values_copy(k).wait_send()
        forward_copy(k).wait_send()

    @pl.loop(1, n_dp)
    def _(k):
        token_copy(k).wait_send()
        cross_copy(k).wait_send()
        same_copy(k).wait_send()
        column_copy(k).wait_send()
        term_copy(k).wait_send()
        stat_copy(k).wait_send()

    @pl.loop(1, n_pipe)
    def _(k):
        line_copy(0, hz, h_send, h_recv, k).wait_send()
        line_copy(1, tz, z_send, z_recv, k).wait_send()
        delta_copy(k).wait_send()

    @pl.loop(0, n_pipe)
    def _(q):
        output_copy(q).wait_send()

    for c in range(BACK_CHUNKS):
        back_copy(c).wait_send()
    for c in range(RING_CHUNKS):
        for s in range(up_hops):
            ring_copy(below(s), c, r_up, up).wait_send()
        for s in range(down_hops):
            ring_copy(above(s), c, r_down, down).wait_send()


def sections(weight, values, gain, embed, section_input, final_gain, target, rest, ids, offset, n_pipe, n_dp):
    dma = pltpu.SemaphoreType.DMA
    vmem = pltpu.VMEM
    half, full = jnp.bfloat16, jnp.float32
    width, depth = weight.shape
    tokens = values.shape[1]
    vrows, model = embed.shape
    per_pipe = n_dp // n_pipe
    step = model // BACK_CHUNKS
    plane = n_dp * tokens
    rows = vrows // n_dp
    cols = per_pipe * width
    chunks = width // W_CHUNK
    return pl.pallas_call(
        functools.partial(section_kernel, n_pipe, n_dp),
        out_shape=(
            jax.ShapeDtypeStruct((width, depth), full),
            jax.ShapeDtypeStruct((rows, cols), full),
        ),
        in_specs=[ANY] * 5 + [VMEM] * 4 + [SMEM],
        out_specs=(VMEM, VMEM),
        scratch_shapes=[
            vmem((vrows, model), half),
            vmem((width, depth), half),
            vmem((width, depth), half),
            vmem((n_dp, tokens, depth), half),
            vmem((1, model), full),
            vmem((n_pipe, n_dp, tokens, depth), half),
            vmem((tokens, model), half),
            vmem((n_dp, tokens, width), half),
            vmem((2, n_dp, tokens, width), half),
            vmem((tokens, 128), full),
            vmem((tokens, 128), full),
            vmem((tokens, vrows), half),
            vmem((n_pipe, tokens, vrows), half),
            vmem((BACK_CHUNKS, tokens, step), half),
            vmem((BACK_CHUNKS, tokens, step), half),
            vmem((2, n_dp, tokens, width), half),
            vmem((n_pipe, per_pipe, tokens, width), half),
            vmem((n_pipe, per_pipe, tokens, width), half),
            vmem((n_dp, tokens, width), half),
            vmem((n_pipe, width, plane), half),
            vmem((n_pipe, width, plane), half),
            vmem((n_pipe, width, plane), half),
            vmem((n_dp, rows, cols), half),
            vmem((n_dp, rows, cols), half),
            vmem((2 * n_pipe, plane), full),
            vmem((n_dp, 2 * n_pipe, plane), full),
            vmem((2 * n_pipe, plane), full),
            vmem((1, model), full),
            vmem((width, 1), full),
            dma((8,)), dma((chunks,)), dma((chunks,)), dma((chunks,)),
            dma, dma((n_pipe,)), dma, dma((n_pipe,)),
            dma((n_dp,)), dma((n_dp,)), dma((n_dp,)), dma((n_dp // 2,)), dma((n_dp // 2,)),
            dma((2, n_dp)), dma((2, n_dp)), dma((2,)), dma((BACK_CHUNKS,)), dma((BACK_CHUNKS,)),
            dma((n_pipe,)), dma((n_pipe,)), dma((n_pipe,)), dma((n_pipe,)), dma((n_pipe,)), dma((n_pipe,)),
            dma((n_dp,)), dma((n_dp,)),
            dma((n_pipe, RING_CHUNKS)), dma((n_pipe, RING_CHUNKS)), dma((n_pipe, RING_CHUNKS)),
            dma((n_pipe,)), dma((n_pipe,)), dma((n_dp,)), dma((n_dp,)), dma((n_dp,)), dma((n_dp,)),
        ],
        compiler_params=pltpu.CompilerParams(
            collective_id=0, has_side_effects=True, vmem_limit_bytes=56 * 1024 * 1024
        ),
        name="sections",
    )(weight, values, gain, embed, section_input, final_gain, target, rest, ids, offset)


def per_device(
    section_proj,
    attn_values,
    post_gain,
    section_input,
    final_gain,
    embed_block,
    token_ids,
    target_ids,
    block_offset,
    rest_lse,
):
    n_pipe, n_dp = lax.axis_size("pipe"), lax.axis_size("dp")
    weight = section_proj[0]
    count = section_input.shape[0] * section_input.shape[1]
    own_grad, tied = sections(
        weight,
        attn_values.reshape(n_pipe, count // n_pipe, weight.shape[1]),
        post_gain,
        embed_block,
        section_input.reshape(count, section_input.shape[2]),
        final_gain,
        target_ids,
        rest_lse,
        token_ids,
        block_offset,
        n_pipe,
        n_dp,
    )
    return (own_grad[None], tied)


def solution(mesh):
    in_specs = (
        P("pipe", "dp", "tensor"),
        P("pipe", None, "dp", "tensor"),
        P("pipe", None),
        P(None, "dp", None),
        P(),
        P("tensor", None),
        P(None, "dp"),
        P(None, "dp"),
        P(),
        P(None, "dp"),
    )
    out_specs = (P("pipe", "dp", "tensor"), P(("tensor", "dp"), "pipe"))
    return jax.shard_map(
        per_device, mesh=mesh, in_specs=in_specs, out_specs=out_specs, check_vma=False
    )
```

```python
import functools
import math

import jax
import jax.numpy as jnp
from jax import lax
from jax.experimental import pallas as pl
from jax.experimental.pallas import tpu as pltpu
from jax.sharding import PartitionSpec as P

EPS = 1e-06
CAP = 30.0
MESH = pl.DeviceIdType.MESH
ANY = pl.BlockSpec(memory_space=pl.ANY)
VMEM = pl.BlockSpec(memory_space=pltpu.VMEM)
SMEM = pl.BlockSpec(memory_space=pltpu.SMEM)
CONTRACT_LAST = (((1,), (1,)), ((), ()))
W_CHUNK = 32
BACK_CHUNKS = 4
RING_CHUNKS = 3


def position():
    return lax.axis_index("pipe"), lax.axis_index("tensor"), lax.axis_index("dp")


def remote(src, dst, send_sem, recv_sem, device):
    return pltpu.make_async_remote_copy(
        src_ref=src,
        dst_ref=dst,
        send_sem=send_sem,
        recv_sem=recv_sem,
        device_id=device,
        device_id_type=MESH,
    )


def signal(sem, device):
    pl.semaphore_signal(sem, inc=1, device_id=device, device_id_type=MESH)


def greet_pipe(barrier, n_pipe):
    p, t, j = position()

    @pl.loop(1, n_pipe)
    def _(k):
        signal(barrier, (lax.rem(p + k, n_pipe), t, j))


def greet_dp(barrier, n_dp):
    p, t, j = position()

    @pl.loop(1, n_dp)
    def _(k):
        signal(barrier, (p, t, lax.rem(j + k, n_dp)))


def normalize(value):
    scale = lax.rsqrt(jnp.mean(value * value, axis=-1, keepdims=True) + EPS)
    return scale, value * scale


def own_tokens(ref, first, tokens):
    micro, per = ref.shape
    lane = lax.broadcasted_iota(jnp.int32, (tokens, per), 1)
    token = lax.broadcasted_iota(jnp.int32, (tokens, per), 0) + first
    found = jnp.zeros((tokens, per), jnp.float32)
    for m in range(micro):
        row = jnp.broadcast_to(ref[m:m + 1, :].astype(jnp.float32), (tokens, per))
        found = found + jnp.where(lane + m * per == token, row, 0.0)
    return jnp.sum(found, axis=1, keepdims=True)


def flatten(blocks):
    return jnp.concatenate(blocks, axis=1)


def section_kernel(
    n_pipe, n_dp,
    w_ref, a_ref, gain_ref, embed_ref, input_ref, fgain_ref, target_ref, rest_ref, ids_ref, offset_ref,
    proj_ref, tied_ref,
    embed, w, w7, a7, g7, every, rows_in, part, parts, sum_out, sum_in, delta_out, delta_all,
    back_out, back_in, block, hz, tz, col, tg, ps, ps_in, term, terms, stat, stats, coef, gains, column,
    l_sem, w_recv, w_up, w_down, s_recv, s_send, g_recv, g_send, a_recv, a_send, a_fwd, v_recv, v_send, v_relay, v_fwd,
    p_recv, p_send, sum_sem, back_recv, back_send, d_recv, d_send, h_recv, h_send, z_recv, z_send,
    c_recv, c_send, r_recv, r_up, r_down, o_recv, o_send, t_recv, t_send, st_recv, st_send,
):
    p, t, j = position()
    last = n_pipe - 1
    up_hops = n_pipe // 2
    down_hops = last - up_hops
    other = 1 - t
    core = lax.rem(j, 2)
    sibling = j + 1 - 2 * core
    n_chips = n_dp // 2
    n_rows = n_chips // 2
    chip = j // 2
    side = lax.rem(chip, 2)
    line = chip // 2
    across = 2 * (chip + 1 - 2 * side) + core
    chunks = w_ref.shape[0] // W_CHUNK
    is_last = p == last
    up = (lax.rem(p + 1, n_pipe), t, j)
    down = (lax.rem(p + last, n_pipe), t, j)
    pair = (p, other, j)
    tokens, width = part.shape[1:]
    vrows, model = embed.shape
    per_pipe = n_dp // n_pipe
    plane = n_dp * tokens
    depth = w.shape[1]
    mine = pl.ds(pl.multiple_of(p * tokens, tokens), tokens)

    def dp_at(k):
        return lax.rem(j + k, n_dp)

    def pipe_at(k):
        return lax.rem(p + k, n_pipe)

    load_embed = pltpu.make_async_copy(embed_ref, embed, l_sem.at[0])
    load_weight = pltpu.make_async_copy(w_ref, w, l_sem.at[1])
    load_rows = pltpu.make_async_copy(input_ref.at[mine], rows_in, l_sem.at[2])
    load_values = pltpu.make_async_copy(a_ref, every.at[:, j], l_sem.at[3])
    load_gains = pltpu.make_async_copy(gain_ref, gains, l_sem.at[7])
    load_weight.start()
    load_rows.start()
    load_gains.start()

    barrier = pltpu.get_barrier_semaphore()
    greet_pipe(barrier, n_pipe)
    greet_dp(barrier, n_dp)

    @pl.loop(0, n_dp)
    def _(k):
        signal(barrier, (p, other, k))

    pl.semaphore_wait(barrier, 2 * n_dp - 1 + n_pipe - 1)

    def piece(ref, c):
        return ref.at[pl.ds(pl.multiple_of(c * W_CHUNK, W_CHUNK), W_CHUNK)]

    def slice_copy(q):
        return remote(a_ref.at[q], a7.at[j], s_send.at[q], s_recv, (q, t, j))

    def gain_copy(q):
        return remote(gain_ref, g7, g_send.at[q], g_recv, (q, t, j))

    def weight_copy(source, c, sems, device):
        return remote(piece(source, c), piece(w7, c), sems.at[c], w_recv.at[c], device)

    def along(k):
        return (lax.rem(line + k, n_rows) * 2 + side) * 2 + core

    def source_of(k, far):
        place = lax.rem(line + n_rows - k, n_rows) * 2
        return (place + (1 - side if far else side)) * 2 + core

    def values_copy(q, sem):
        return remote(a_ref, every.at[:, j], v_send.at[sem], v_recv.at[j], (p, t, q))

    def pass_copy(owner, q, sem):
        return remote(every.at[:, owner], every.at[:, owner], sem, v_recv.at[owner], (p, t, q))

    def relay_copy(k):
        return pass_copy(across, along(k), v_relay.at[k])

    def forward_copy(k, far):
        return pass_copy(source_of(k, far), sibling, v_fwd.at[k + (n_rows if far else 0)])

    def values_arrived(owner):
        return remote(a_ref, every.at[:, owner], v_send.at[0], v_recv.at[owner], (p, t, sibling))

    own_slice = pltpu.make_async_copy(a_ref.at[last], a7.at[j], l_sem.at[4])
    own_weight = pltpu.make_async_copy(w_ref, w7, l_sem.at[5])
    own_gain = pltpu.make_async_copy(gain_ref, g7, l_sem.at[6])

    @pl.when(is_last)
    def _():
        own_slice.start()

        @pl.loop(0, last)
        def _(q):
            slice_copy(q).start()

        @pl.loop(0, chunks)
        def _(c):
            weight_copy(w_ref, c, w_up, up).start()
            if down_hops:
                weight_copy(w_ref, c, w_down, down).start()

        @pl.loop(0, last)
        def _(q):
            gain_copy(q).start()

        own_weight.start()
        own_gain.start()

    values_copy(across, 1).start()

    @pl.loop(1, n_rows)
    def _(k):
        values_copy(along(k), k + 1).start()

    values_copy(sibling, 0).start()
    load_values.start()
    load_embed.start()

    load_gains.wait()
    wide = pl.cdiv(width, 128) * 128
    turned = pltpu.roll(
        jnp.broadcast_to(gains[...], (8, model)), lax.rem(model - width * j, model), 1
    )
    column[...] = turned[:, :wide].T[:width, 0:1]

    @pl.when(is_last)
    def _():
        own_slice.wait()

    @pl.when(jnp.logical_not(is_last))
    def _():
        slice_copy(p).wait_recv()

    def token_copy(k):
        q = lax.rem(chip + k, n_chips) * 2 + core
        return remote(a7.at[j], a7.at[j], a_send.at[k], a_recv.at[j], (p, t, q))

    def tokens_arrived(q):
        return remote(a7.at[j], a7.at[q], a_send.at[0], a_recv.at[q], (p, t, sibling))

    def tokens_forward(k):
        owner = lax.rem(chip + n_chips - k, n_chips) * 2 + core
        return remote(a7.at[owner], a7.at[owner], a_fwd.at[k], a_recv.at[owner], (p, t, sibling))

    @pl.loop(1, n_chips)
    def _(k):
        token_copy(k).start()

    tokens_forward(0).start()

    def relay():
        values_arrived(across).wait_recv()

        @pl.loop(1, n_rows)
        def _(k):
            relay_copy(k).start()

        forward_copy(0, True).start()

        @pl.loop(1, n_chips)
        def _(k):
            tokens_arrived(lax.rem(chip + n_chips - k, n_chips) * 2 + core).wait_recv()
            tokens_forward(k).start()

    next_to_last = jnp.logical_or(p == 0, p == last - 1)
    relay_at = jnp.where(next_to_last, min(4, chunks - 1), 0)

    @pl.when(is_last)
    def _():
        relay()
        own_weight.wait()
        own_gain.wait()

    @pl.when(jnp.logical_not(is_last))
    def _():
        @pl.loop(0, chunks)
        def _(c):
            weight_copy(w_ref, c, w_up, up).wait_recv()

            @pl.when(p < up_hops - 1)
            def _():
                weight_copy(w7, c, w_up, up).start()

            @pl.when(p > up_hops)
            def _():
                weight_copy(w7, c, w_down, down).start()

            @pl.when(c == relay_at)
            def _():
                relay()

        gain_copy(p).wait_recv()

    @pl.loop(0, n_chips)
    def _(k):
        tokens_arrived(2 * k + 1 - core).wait_recv()

    part[...] = (
        lax.dot_general(
            a7[...].reshape(plane, depth), w7[...], CONTRACT_LAST, preferred_element_type=jnp.float32
        )
        .astype(jnp.bfloat16)
        .reshape(n_dp, tokens, width)
    )

    def same_copy(k):
        q = dp_at(k)
        return remote(part.at[q], parts.at[t, j], p_send.at[0, k], p_recv.at[t, j], (p, t, q))

    def cross_copy(k):
        q = dp_at(k)
        return remote(part.at[q], parts.at[t, j], p_send.at[1, k], p_recv.at[t, j], (p, other, q))

    def part_arrived(group, q):
        return remote(part.at[q], parts.at[group, q], p_send.at[0, 0], p_recv.at[group, q], pair)

    @pl.loop(0, n_dp)
    def _(k):
        cross_copy(k).start()

    @pl.loop(1, n_dp)
    def _(k):
        same_copy(k).start()

    parts[t, j] = part[j]

    @pl.loop(1, n_rows)
    def _(k):
        for far in (False, True):
            values_arrived(source_of(k, far)).wait_recv()
            forward_copy(k, far).start()

    load_weight.wait()
    load_values.wait()

    @pl.loop(0, n_chips)
    def _(k):
        values_arrived(2 * k + 1 - core).wait_recv()

    def output_copy(q):
        return remote(ps.at[q], ps_in.at[q], o_send.at[q], o_recv.at[q], pair)

    @pl.loop(0, n_pipe)
    def _(q):
        ps[q] = lax.dot_general(
            w[...], every[q].reshape(plane, depth), CONTRACT_LAST, preferred_element_type=jnp.float32
        ).astype(jnp.bfloat16)
        output_copy(q).start()

    load_rows.wait()
    load_embed.wait()

    @pl.loop(0, n_dp)
    def _(k):
        part_arrived(other, k).wait_recv()

    @pl.loop(1, n_dp)
    def _(k):
        part_arrived(t, dp_at(k)).wait_recv()

    output = flatten(
        [parts[0, q].astype(jnp.float32) + parts[1, q].astype(jnp.float32) for q in range(n_dp)]
    )
    _, normed = normalize(output)
    final_gain = fgain_ref[...].reshape(1, model)
    resid = rows_in[...].astype(jnp.float32) + normed * g7[...]
    y_scale, y_normed = normalize(resid)
    head_in = (y_normed * final_gain).astype(jnp.bfloat16)
    for b in range(n_dp):
        block[0, b] = head_in[:, b * width:(b + 1) * width]

    def line_copy(slot, dst, send, recv, k):
        q = pipe_at(k)
        return remote(
            block.at[slot, pl.ds(q * per_pipe, per_pipe)], dst.at[p], send.at[k], recv.at[p], (q, t, j)
        )

    def line_arrived(slot, dst, send, recv, q):
        return remote(block.at[slot, pl.ds(0, per_pipe)], dst.at[q], send.at[0], recv.at[q], (q, t, j))

    @pl.loop(1, n_pipe)
    def _(k):
        line_copy(0, hz, h_send, h_recv, k).start()

    for b in range(per_pipe):
        hz[p, b] = block[0, p * per_pipe + b]

    raw = lax.dot_general(head_in, embed[...], CONTRACT_LAST, preferred_element_type=jnp.float32)
    capped = jnp.tanh(raw / CAP)
    logits = CAP * capped
    own_sum = jnp.sum(jnp.exp(logits), axis=1, keepdims=True)
    sum_out[...] = jnp.broadcast_to(own_sum, sum_out.shape)

    def sum_copy():
        return remote(sum_out, sum_in, sum_sem.at[0], sum_sem.at[1], pair)

    sum_copy().start()
    lane = lax.broadcasted_iota(jnp.int32, (tokens, vrows), 1)
    first_row = offset_ref[0] + t * vrows
    target = own_tokens(target_ref, p * tokens, tokens)
    hit = (target == (first_row + lane).astype(jnp.float32)).astype(jnp.float32)
    slope = 1.0 - capped * capped
    sum_copy().wait_recv()
    log_total = jnp.log(own_sum + sum_in[:, 0:1])
    rest = own_tokens(rest_ref, p * tokens, tokens)
    lse = jnp.maximum(rest, log_total) + jnp.log(1.0 + jnp.exp(-jnp.abs(rest - log_total)))
    delta = ((jnp.exp(logits - lse) - hit) * slope).astype(jnp.bfloat16)
    delta_out[...] = delta
    delta_all[p] = delta

    step = model // BACK_CHUNKS

    def back_copy(c):
        return remote(back_out.at[c], back_in.at[c], back_send.at[c], back_recv.at[c], pair)

    for c in range(BACK_CHUNKS):
        grad = jnp.dot(delta, embed[:, c * step:(c + 1) * step], preferred_element_type=jnp.float32)
        back_out[c] = grad.astype(jnp.bfloat16)
        back_copy(c).start()

    def delta_copy(k):
        return remote(delta_out, delta_all.at[p], d_send.at[k], d_recv.at[p], (pipe_at(k), t, j))

    def delta_arrived(q):
        return remote(delta_out, delta_all.at[q], d_send.at[0], d_recv.at[q], (q, t, j))

    @pl.loop(1, n_pipe)
    def _(k):
        delta_copy(k).start()

    grads = []
    for c in range(BACK_CHUNKS):
        back_copy(c).wait_recv()
        grads.append(back_out[c].astype(jnp.float32) + back_in[c].astype(jnp.float32))
    grad = flatten(grads) * final_gain
    top = y_scale * (grad - y_normed * jnp.mean(grad * y_normed, axis=-1, keepdims=True))
    top = top.astype(jnp.bfloat16)
    for b in range(n_dp):
        block[1, b] = top[:, b * width:(b + 1) * width]

    def column_copy(k):
        q = dp_at(k)
        return remote(block.at[1, q], col.at[j], c_send.at[k], c_recv.at[j], (p, t, q))

    def column_arrived(q):
        return remote(block.at[1, q], col.at[q], c_send.at[0], c_recv.at[q], pair)

    @pl.loop(1, n_dp)
    def _(k):
        column_copy(k).start()

    @pl.loop(1, n_pipe)
    def _(k):
        line_copy(1, tz, z_send, z_recv, k).start()

    col[j] = block[1, j]
    for b in range(per_pipe):
        tz[p, b] = block[1, p * per_pipe + b]

    @pl.loop(1, n_dp)
    def _(k):
        column_arrived(dp_at(k)).wait_recv()

    tg[p] = col[...].reshape(plane, width).T

    ring_rows = width // RING_CHUNKS

    def ring_copy(source, c, send, device):
        ref = tg.at[source, pl.ds(c * ring_rows, ring_rows)]
        return remote(ref, ref, send.at[source, c], r_recv.at[source, c], device)

    def above(s):
        return lax.rem(p + s, n_pipe)

    def below(s):
        return lax.rem(p + n_pipe - s, n_pipe)

    for c in range(RING_CHUNKS):
        ring_copy(p, c, r_up, up).start()
        if down_hops:
            ring_copy(p, c, r_down, down).start()

    @pl.loop(1, n_pipe)
    def _(k):
        q = pipe_at(k)
        line_arrived(0, hz, h_send, h_recv, q).wait_recv()
        line_arrived(1, tz, z_send, z_recv, q).wait_recv()
        delta_arrived(q).wait_recv()

    count = n_pipe * tokens
    head_cols = flatten([hz[:, b].reshape(count, width) for b in range(per_pipe)])
    top_cols = flatten([tz[:, b].reshape(count, width) for b in range(per_pipe)])
    delta_rows = delta_all[...].reshape(count, vrows).T
    row = lax.broadcasted_iota(jnp.int32, (vrows, count), 0)
    ids = flatten([ids_ref[m:m + 1, :] for m in range(ids_ref.shape[0])])
    used = (ids == first_row + row).astype(jnp.bfloat16)
    term[...] = (
        (
            jnp.dot(delta_rows, head_cols, preferred_element_type=jnp.float32)
            + math.sqrt(model) * jnp.dot(used, top_cols, preferred_element_type=jnp.float32)
        )
        .astype(jnp.bfloat16)
        .reshape(term.shape)
    )

    def term_copy(k):
        q = dp_at(k)
        return remote(term.at[q], terms.at[j], t_send.at[k], t_recv.at[j], (p, t, q))

    def term_arrived(q):
        return remote(term.at[q], terms.at[q], t_send.at[0], t_recv.at[q], pair)

    @pl.loop(1, n_dp)
    def _(k):
        term_copy(k).start()

    terms[j] = term[j]

    for s in range(1, up_hops + 1):
        for c in range(RING_CHUNKS):
            ring_copy(below(s), c, r_up, up).wait_recv()
            if s < up_hops:
                ring_copy(below(s), c, r_up, up).start()
            if s <= down_hops:
                ring_copy(above(s), c, r_down, down).wait_recv()
                if s < down_hops:
                    ring_copy(above(s), c, r_down, down).start()

    @pl.loop(0, n_pipe)
    def _(q):
        output_copy(q).wait_recv()
        out = ps[q].astype(jnp.float32) + ps_in[q].astype(jnp.float32)
        grad = tg[q].astype(jnp.float32) * column[...]
        stat[pl.ds(q, 1), :] = jnp.sum(out * out, axis=0, keepdims=True)
        stat[pl.ds(n_pipe + q, 1), :] = jnp.sum(out * grad, axis=0, keepdims=True)

    def stat_copy(k):
        return remote(stat, stats.at[j], st_send.at[k], st_recv.at[j], (p, t, dp_at(k)))

    def stat_arrived(q):
        return remote(stat, stats.at[q], st_send.at[0], st_recv.at[q], pair)

    @pl.loop(1, n_dp)
    def _(k):
        stat_copy(k).start()

    stats[j] = stat[...]

    @pl.loop(1, n_dp)
    def _(k):
        term_arrived(dp_at(k)).wait_recv()

    total = terms[0].astype(jnp.float32)
    for q in range(1, n_dp):
        total = total + terms[q].astype(jnp.float32)
    tied_ref[...] = total

    @pl.loop(1, n_dp)
    def _(k):
        stat_arrived(dp_at(k)).wait_recv()

    both = jnp.sum(stats[...], axis=0)
    scale = lax.rsqrt(both[:n_pipe] / model + EPS)
    coef[0:n_pipe] = scale
    coef[n_pipe:2 * n_pipe] = scale * scale * both[n_pipe:] / model
    proj_ref[...] = jnp.zeros_like(proj_ref)

    @pl.loop(0, n_pipe)
    def _(q):
        out = ps[q].astype(jnp.float32) + ps_in[q].astype(jnp.float32)
        grad = tg[q].astype(jnp.float32) * column[...]
        out_grad = coef[pl.ds(q, 1), :] * (grad - out * coef[pl.ds(n_pipe + q, 1), :])
        proj_ref[...] += jnp.dot(
            out_grad.astype(jnp.bfloat16),
            every[q].reshape(plane, depth),
            preferred_element_type=jnp.float32,
        )

    @pl.when(is_last)
    def _():
        @pl.loop(0, last)
        def _(q):
            slice_copy(q).wait_send()
            gain_copy(q).wait_send()

        @pl.loop(0, chunks)
        def _(c):
            weight_copy(w_ref, c, w_up, up).wait_send()
            if down_hops:
                weight_copy(w_ref, c, w_down, down).wait_send()

    @pl.when(jnp.logical_not(is_last))
    def _():
        @pl.when(p < up_hops - 1)
        def _():
            @pl.loop(0, chunks)
            def _(c):
                weight_copy(w7, c, w_up, up).wait_send()

        @pl.when(p > up_hops)
        def _():
            @pl.loop(0, chunks)
            def _(c):
                weight_copy(w7, c, w_down, down).wait_send()

    values_copy(sibling, 0).wait_send()
    values_copy(across, 1).wait_send()
    forward_copy(0, True).wait_send()
    tokens_forward(0).wait_send()
    cross_copy(0).wait_send()
    sum_copy().wait_send()

    @pl.loop(1, n_rows)
    def _(k):
        values_copy(along(k), k + 1).wait_send()
        relay_copy(k).wait_send()
        forward_copy(k, False).wait_send()
        forward_copy(k, True).wait_send()

    @pl.loop(1, n_chips)
    def _(k):
        token_copy(k).wait_send()
        tokens_forward(k).wait_send()

    @pl.loop(1, n_dp)
    def _(k):
        cross_copy(k).wait_send()
        same_copy(k).wait_send()
        column_copy(k).wait_send()
        term_copy(k).wait_send()
        stat_copy(k).wait_send()

    @pl.loop(1, n_pipe)
    def _(k):
        line_copy(0, hz, h_send, h_recv, k).wait_send()
        line_copy(1, tz, z_send, z_recv, k).wait_send()
        delta_copy(k).wait_send()

    @pl.loop(0, n_pipe)
    def _(q):
        output_copy(q).wait_send()

    for c in range(BACK_CHUNKS):
        back_copy(c).wait_send()
    for c in range(RING_CHUNKS):
        for s in range(up_hops):
            ring_copy(below(s), c, r_up, up).wait_send()
        for s in range(down_hops):
            ring_copy(above(s), c, r_down, down).wait_send()


def sections(weight, values, gain, embed, section_input, final_gain, target, rest, ids, offset, n_pipe, n_dp):
    dma = pltpu.SemaphoreType.DMA
    vmem = pltpu.VMEM
    half, full = jnp.bfloat16, jnp.float32
    width, depth = weight.shape
    tokens = values.shape[1]
    vrows, model = embed.shape
    per_pipe = n_dp // n_pipe
    step = model // BACK_CHUNKS
    plane = n_dp * tokens
    rows = vrows // n_dp
    cols = per_pipe * width
    chunks = width // W_CHUNK
    return pl.pallas_call(
        functools.partial(section_kernel, n_pipe, n_dp),
        out_shape=(
            jax.ShapeDtypeStruct((width, depth), full),
            jax.ShapeDtypeStruct((rows, cols), full),
        ),
        in_specs=[ANY] * 5 + [VMEM] * 4 + [SMEM],
        out_specs=(VMEM, VMEM),
        scratch_shapes=[
            vmem((vrows, model), half),
            vmem((width, depth), half),
            vmem((width, depth), half),
            vmem((n_dp, tokens, depth), half),
            vmem((1, model), full),
            vmem((n_pipe, n_dp, tokens, depth), half),
            vmem((tokens, model), half),
            vmem((n_dp, tokens, width), half),
            vmem((2, n_dp, tokens, width), half),
            vmem((tokens, 128), full),
            vmem((tokens, 128), full),
            vmem((tokens, vrows), half),
            vmem((n_pipe, tokens, vrows), half),
            vmem((BACK_CHUNKS, tokens, step), half),
            vmem((BACK_CHUNKS, tokens, step), half),
            vmem((2, n_dp, tokens, width), half),
            vmem((n_pipe, per_pipe, tokens, width), half),
            vmem((n_pipe, per_pipe, tokens, width), half),
            vmem((n_dp, tokens, width), half),
            vmem((n_pipe, width, plane), half),
            vmem((n_pipe, width, plane), half),
            vmem((n_pipe, width, plane), half),
            vmem((n_dp, rows, cols), half),
            vmem((n_dp, rows, cols), half),
            vmem((2 * n_pipe, plane), full),
            vmem((n_dp, 2 * n_pipe, plane), full),
            vmem((2 * n_pipe, plane), full),
            vmem((1, model), full),
            vmem((width, 1), full),
            dma((8,)), dma((chunks,)), dma((chunks,)), dma((chunks,)),
            dma, dma((n_pipe,)), dma, dma((n_pipe,)),
            dma((n_dp,)), dma((n_dp // 2,)), dma((n_dp // 2,)),
            dma((n_dp,)), dma((n_dp // 4 + 1,)), dma((n_dp // 4,)), dma((n_dp // 2,)),
            dma((2, n_dp)), dma((2, n_dp)), dma((2,)), dma((BACK_CHUNKS,)), dma((BACK_CHUNKS,)),
            dma((n_pipe,)), dma((n_pipe,)), dma((n_pipe,)), dma((n_pipe,)), dma((n_pipe,)), dma((n_pipe,)),
            dma((n_dp,)), dma((n_dp,)),
            dma((n_pipe, RING_CHUNKS)), dma((n_pipe, RING_CHUNKS)), dma((n_pipe, RING_CHUNKS)),
            dma((n_pipe,)), dma((n_pipe,)), dma((n_dp,)), dma((n_dp,)), dma((n_dp,)), dma((n_dp,)),
        ],
        compiler_params=pltpu.CompilerParams(
            collective_id=0, has_side_effects=True, vmem_limit_bytes=56 * 1024 * 1024
        ),
        name="sections",
    )(weight, values, gain, embed, section_input, final_gain, target, rest, ids, offset)


def per_device(
    section_proj,
    attn_values,
    post_gain,
    section_input,
    final_gain,
    embed_block,
    token_ids,
    target_ids,
    block_offset,
    rest_lse,
):
    n_pipe, n_dp = lax.axis_size("pipe"), lax.axis_size("dp")
    weight = section_proj[0]
    count = section_input.shape[0] * section_input.shape[1]
    own_grad, tied = sections(
        weight,
        attn_values.reshape(n_pipe, count // n_pipe, weight.shape[1]),
        post_gain,
        embed_block,
        section_input.reshape(count, section_input.shape[2]),
        final_gain,
        target_ids,
        rest_lse,
        token_ids,
        block_offset,
        n_pipe,
        n_dp,
    )
    return (own_grad[None], tied)


def solution(mesh):
    in_specs = (
        P("pipe", "dp", "tensor"),
        P("pipe", None, "dp", "tensor"),
        P("pipe", None),
        P(None, "dp", None),
        P(),
        P("tensor", None),
        P(None, "dp"),
        P(None, "dp"),
        P(),
        P(None, "dp"),
    )
    out_specs = (P("pipe", "dp", "tensor"), P(("tensor", "dp"), "pipe"))
    return jax.shard_map(
        per_device, mesh=mesh, in_specs=in_specs, out_specs=out_specs, check_vma=False
    )
```

```python
import functools
import math

import jax
import jax.numpy as jnp
from jax import lax
from jax.experimental import pallas as pl
from jax.experimental.pallas import tpu as pltpu
from jax.sharding import PartitionSpec as P

EPS = 1e-06
CAP = 30.0
MESH = pl.DeviceIdType.MESH
ANY = pl.BlockSpec(memory_space=pl.ANY)
VMEM = pl.BlockSpec(memory_space=pltpu.VMEM)
SMEM = pl.BlockSpec(memory_space=pltpu.SMEM)
CONTRACT_LAST = (((1,), (1,)), ((), ()))
W_CHUNK = 32
BACK_CHUNKS = 4
RING_CHUNKS = 3


def position():
    return lax.axis_index("pipe"), lax.axis_index("tensor"), lax.axis_index("dp")


def remote(src, dst, send_sem, recv_sem, device):
    return pltpu.make_async_remote_copy(
        src_ref=src,
        dst_ref=dst,
        send_sem=send_sem,
        recv_sem=recv_sem,
        device_id=device,
        device_id_type=MESH,
    )


def signal(sem, device):
    pl.semaphore_signal(sem, inc=1, device_id=device, device_id_type=MESH)


def greet_pipe(barrier, n_pipe):
    p, t, j = position()

    @pl.loop(1, n_pipe)
    def _(k):
        signal(barrier, (lax.rem(p + k, n_pipe), t, j))


def greet_dp(barrier, n_dp):
    p, t, j = position()

    @pl.loop(1, n_dp)
    def _(k):
        signal(barrier, (p, t, lax.rem(j + k, n_dp)))


def normalize(value):
    scale = lax.rsqrt(jnp.mean(value * value, axis=-1, keepdims=True) + EPS)
    return scale, value * scale


def own_tokens(ref, first, tokens):
    micro, per = ref.shape
    lane = lax.broadcasted_iota(jnp.int32, (tokens, per), 1)
    token = lax.broadcasted_iota(jnp.int32, (tokens, per), 0) + first
    found = jnp.zeros((tokens, per), jnp.float32)
    for m in range(micro):
        row = jnp.broadcast_to(ref[m:m + 1, :].astype(jnp.float32), (tokens, per))
        found = found + jnp.where(lane + m * per == token, row, 0.0)
    return jnp.sum(found, axis=1, keepdims=True)


def flatten(blocks):
    return jnp.concatenate(blocks, axis=1)


def section_kernel(
    n_pipe, n_dp,
    w_ref, a_ref, gain_ref, embed_ref, input_ref, fgain_ref, target_ref, rest_ref, ids_ref, offset_ref,
    proj_ref, tied_ref,
    embed, w, w7, a7, g7, every, rows_in, part, parts, sum_out, sum_in, delta_out, delta_all,
    back_out, back_in, block, hz, tz, col, tg, ps, ps_in, term, core_in, half, line_in, side_out, side_in, stat, stats, coef, gains, column,
    l_sem, w_recv, w_up, w_down, s_recv, s_send, g_recv, g_send, a_recv, a_send, a_fwd, v_recv, v_send, v_relay, v_fwd,
    p_recv, p_send, sum_sem, back_recv, back_send, d_recv, d_send, h_recv, h_send, z_recv, z_send,
    c_recv, c_send, r_recv, r_up, r_down, o_recv, o_send, t_recv, t_send, y_recv, y_send, x_sem, st_recv, st_send,
):
    p, t, j = position()
    last = n_pipe - 1
    up_hops = n_pipe // 2
    down_hops = last - up_hops
    other = 1 - t
    core = lax.rem(j, 2)
    sibling = j + 1 - 2 * core
    n_chips = n_dp // 2
    n_rows = n_chips // 2
    chip = j // 2
    side = lax.rem(chip, 2)
    line = chip // 2
    across = 2 * (chip + 1 - 2 * side) + core
    chunks = w_ref.shape[0] // W_CHUNK
    is_last = p == last
    up = (lax.rem(p + 1, n_pipe), t, j)
    down = (lax.rem(p + last, n_pipe), t, j)
    pair = (p, other, j)
    tokens, width = part.shape[1:]
    vrows, model = embed.shape
    per_pipe = n_dp // n_pipe
    plane = n_dp * tokens
    depth = w.shape[1]
    mine = pl.ds(pl.multiple_of(p * tokens, tokens), tokens)

    def dp_at(k):
        return lax.rem(j + k, n_dp)

    def pipe_at(k):
        return lax.rem(p + k, n_pipe)

    load_embed = pltpu.make_async_copy(embed_ref, embed, l_sem.at[0])
    load_weight = pltpu.make_async_copy(w_ref, w, l_sem.at[1])
    load_rows = pltpu.make_async_copy(input_ref.at[mine], rows_in, l_sem.at[2])
    load_values = pltpu.make_async_copy(a_ref, every.at[:, j], l_sem.at[3])
    load_gains = pltpu.make_async_copy(gain_ref, gains, l_sem.at[7])
    load_weight.start()
    load_rows.start()
    load_gains.start()

    barrier = pltpu.get_barrier_semaphore()
    greet_pipe(barrier, n_pipe)
    greet_dp(barrier, n_dp)

    @pl.loop(0, n_dp)
    def _(k):
        signal(barrier, (p, other, k))

    pl.semaphore_wait(barrier, 2 * n_dp - 1 + n_pipe - 1)

    def piece(ref, c):
        return ref.at[pl.ds(pl.multiple_of(c * W_CHUNK, W_CHUNK), W_CHUNK)]

    def slice_copy(q):
        return remote(a_ref.at[q], a7.at[j], s_send.at[q], s_recv, (q, t, j))

    def gain_copy(q):
        return remote(gain_ref, g7, g_send.at[q], g_recv, (q, t, j))

    def weight_copy(source, c, sems, device):
        return remote(piece(source, c), piece(w7, c), sems.at[c], w_recv.at[c], device)

    def along(k):
        return (lax.rem(line + k, n_rows) * 2 + side) * 2 + core

    def source_of(k, far):
        place = lax.rem(line + n_rows - k, n_rows) * 2
        return (place + (1 - side if far else side)) * 2 + core

    def values_copy(q, sem):
        return remote(a_ref, every.at[:, j], v_send.at[sem], v_recv.at[j], (p, t, q))

    def pass_copy(owner, q, sem):
        return remote(every.at[:, owner], every.at[:, owner], sem, v_recv.at[owner], (p, t, q))

    def relay_copy(k):
        return pass_copy(across, along(k), v_relay.at[k])

    def forward_copy(k, far):
        return pass_copy(source_of(k, far), sibling, v_fwd.at[k + (n_rows if far else 0)])

    def values_arrived(owner):
        return remote(a_ref, every.at[:, owner], v_send.at[0], v_recv.at[owner], (p, t, sibling))

    own_slice = pltpu.make_async_copy(a_ref.at[last], a7.at[j], l_sem.at[4])
    own_weight = pltpu.make_async_copy(w_ref, w7, l_sem.at[5])
    own_gain = pltpu.make_async_copy(gain_ref, g7, l_sem.at[6])

    @pl.when(is_last)
    def _():
        own_slice.start()

        @pl.loop(0, last)
        def _(q):
            slice_copy(q).start()

        @pl.loop(0, chunks)
        def _(c):
            weight_copy(w_ref, c, w_up, up).start()
            if down_hops:
                weight_copy(w_ref, c, w_down, down).start()

        @pl.loop(0, last)
        def _(q):
            gain_copy(q).start()

        own_weight.start()
        own_gain.start()

    values_copy(across, 1).start()

    @pl.loop(1, n_rows)
    def _(k):
        values_copy(along(k), k + 1).start()

    values_copy(sibling, 0).start()
    load_values.start()
    load_embed.start()

    load_gains.wait()
    wide = pl.cdiv(width, 128) * 128
    turned = pltpu.roll(
        jnp.broadcast_to(gains[...], (8, model)), lax.rem(model - width * j, model), 1
    )
    column[...] = turned[:, :wide].T[:width, 0:1]

    @pl.when(is_last)
    def _():
        own_slice.wait()

    @pl.when(jnp.logical_not(is_last))
    def _():
        slice_copy(p).wait_recv()

    def token_copy(k):
        q = lax.rem(chip + k, n_chips) * 2 + core
        return remote(a7.at[j], a7.at[j], a_send.at[k], a_recv.at[j], (p, t, q))

    def tokens_arrived(q):
        return remote(a7.at[j], a7.at[q], a_send.at[0], a_recv.at[q], (p, t, sibling))

    def tokens_forward(k):
        owner = lax.rem(chip + n_chips - k, n_chips) * 2 + core
        return remote(a7.at[owner], a7.at[owner], a_fwd.at[k], a_recv.at[owner], (p, t, sibling))

    @pl.loop(1, n_chips)
    def _(k):
        token_copy(k).start()

    tokens_forward(0).start()

    def relay():
        values_arrived(across).wait_recv()

        @pl.loop(1, n_rows)
        def _(k):
            relay_copy(k).start()

        forward_copy(0, True).start()

        @pl.loop(1, n_chips)
        def _(k):
            tokens_arrived(lax.rem(chip + n_chips - k, n_chips) * 2 + core).wait_recv()
            tokens_forward(k).start()

    next_to_last = jnp.logical_or(p == 0, p == last - 1)
    relay_at = jnp.where(next_to_last, min(4, chunks - 1), 0)

    @pl.when(is_last)
    def _():
        relay()
        own_weight.wait()
        own_gain.wait()

    @pl.when(jnp.logical_not(is_last))
    def _():
        @pl.loop(0, chunks)
        def _(c):
            weight_copy(w_ref, c, w_up, up).wait_recv()

            @pl.when(p < up_hops - 1)
            def _():
                weight_copy(w7, c, w_up, up).start()

            @pl.when(p > up_hops)
            def _():
                weight_copy(w7, c, w_down, down).start()

            @pl.when(c == relay_at)
            def _():
                relay()

        gain_copy(p).wait_recv()

    @pl.loop(0, n_chips)
    def _(k):
        tokens_arrived(2 * k + 1 - core).wait_recv()

    part[...] = (
        lax.dot_general(
            a7[...].reshape(plane, depth), w7[...], CONTRACT_LAST, preferred_element_type=jnp.float32
        )
        .astype(jnp.bfloat16)
        .reshape(n_dp, tokens, width)
    )

    def same_copy(k):
        q = dp_at(k)
        return remote(part.at[q], parts.at[t, j], p_send.at[0, k], p_recv.at[t, j], (p, t, q))

    def cross_copy(k):
        q = dp_at(k)
        return remote(part.at[q], parts.at[t, j], p_send.at[1, k], p_recv.at[t, j], (p, other, q))

    def part_arrived(group, q):
        return remote(part.at[q], parts.at[group, q], p_send.at[0, 0], p_recv.at[group, q], pair)

    @pl.loop(0, n_dp)
    def _(k):
        cross_copy(k).start()

    @pl.loop(1, n_dp)
    def _(k):
        same_copy(k).start()

    parts[t, j] = part[j]

    @pl.loop(1, n_rows)
    def _(k):
        for far in (False, True):
            values_arrived(source_of(k, far)).wait_recv()
            forward_copy(k, far).start()

    load_weight.wait()
    load_values.wait()

    @pl.loop(0, n_chips)
    def _(k):
        values_arrived(2 * k + 1 - core).wait_recv()

    def output_copy(q):
        return remote(ps.at[q], ps_in.at[q], o_send.at[q], o_recv.at[q], pair)

    @pl.loop(0, n_pipe)
    def _(q):
        ps[q] = lax.dot_general(
            w[...], every[q].reshape(plane, depth), CONTRACT_LAST, preferred_element_type=jnp.float32
        ).astype(jnp.bfloat16)

    def send_outputs(first, stop):
        @pl.loop(first, stop)
        def _(q):
            output_copy(q).start()

    send_outputs(0, n_pipe // 4)

    load_rows.wait()
    load_embed.wait()

    @pl.loop(0, n_dp)
    def _(k):
        part_arrived(other, k).wait_recv()

    @pl.loop(1, n_dp)
    def _(k):
        part_arrived(t, dp_at(k)).wait_recv()

    send_outputs(n_pipe // 4, n_pipe // 2)
    output = flatten(
        [parts[0, q].astype(jnp.float32) + parts[1, q].astype(jnp.float32) for q in range(n_dp)]
    )
    _, normed = normalize(output)
    final_gain = fgain_ref[...].reshape(1, model)
    resid = rows_in[...].astype(jnp.float32) + normed * g7[...]
    y_scale, y_normed = normalize(resid)
    head_in = (y_normed * final_gain).astype(jnp.bfloat16)
    for b in range(n_dp):
        block[0, b] = head_in[:, b * width:(b + 1) * width]

    def line_copy(slot, dst, send, recv, k):
        q = pipe_at(k)
        return remote(
            block.at[slot, pl.ds(q * per_pipe, per_pipe)], dst.at[p], send.at[k], recv.at[p], (q, t, j)
        )

    def line_arrived(slot, dst, send, recv, q):
        return remote(block.at[slot, pl.ds(0, per_pipe)], dst.at[q], send.at[0], recv.at[q], (q, t, j))

    @pl.loop(1, n_pipe)
    def _(k):
        line_copy(0, hz, h_send, h_recv, k).start()

    for b in range(per_pipe):
        hz[p, b] = block[0, p * per_pipe + b]

    raw = lax.dot_general(head_in, embed[...], CONTRACT_LAST, preferred_element_type=jnp.float32)
    capped = jnp.tanh(raw / CAP)
    logits = CAP * capped
    own_sum = jnp.sum(jnp.exp(logits), axis=1, keepdims=True)
    sum_out[...] = jnp.broadcast_to(own_sum, sum_out.shape)

    def sum_copy():
        return remote(sum_out, sum_in, sum_sem.at[0], sum_sem.at[1], pair)

    sum_copy().start()
    lane = lax.broadcasted_iota(jnp.int32, (tokens, vrows), 1)
    first_row = offset_ref[0] + t * vrows
    target = own_tokens(target_ref, p * tokens, tokens)
    hit = (target == (first_row + lane).astype(jnp.float32)).astype(jnp.float32)
    slope = 1.0 - capped * capped
    sum_copy().wait_recv()
    log_total = jnp.log(own_sum + sum_in[:, 0:1])
    rest = own_tokens(rest_ref, p * tokens, tokens)
    lse = jnp.maximum(rest, log_total) + jnp.log(1.0 + jnp.exp(-jnp.abs(rest - log_total)))
    delta = ((jnp.exp(logits - lse) - hit) * slope).astype(jnp.bfloat16)
    delta_out[...] = delta
    delta_all[p] = delta

    step = model // BACK_CHUNKS

    def back_copy(c):
        return remote(back_out.at[c], back_in.at[c], back_send.at[c], back_recv.at[c], pair)

    for c in range(BACK_CHUNKS):
        grad = jnp.dot(delta, embed[:, c * step:(c + 1) * step], preferred_element_type=jnp.float32)
        back_out[c] = grad.astype(jnp.bfloat16)
        back_copy(c).start()

    def delta_copy(k):
        return remote(delta_out, delta_all.at[p], d_send.at[k], d_recv.at[p], (pipe_at(k), t, j))

    def delta_arrived(q):
        return remote(delta_out, delta_all.at[q], d_send.at[0], d_recv.at[q], (q, t, j))

    @pl.loop(1, n_pipe)
    def _(k):
        delta_copy(k).start()

    grads = []
    for c in range(BACK_CHUNKS):
        back_copy(c).wait_recv()
        grads.append(back_out[c].astype(jnp.float32) + back_in[c].astype(jnp.float32))
    grad = flatten(grads) * final_gain
    top = y_scale * (grad - y_normed * jnp.mean(grad * y_normed, axis=-1, keepdims=True))
    top = top.astype(jnp.bfloat16)
    for b in range(n_dp):
        block[1, b] = top[:, b * width:(b + 1) * width]

    def column_copy(k):
        q = dp_at(k)
        return remote(block.at[1, q], col.at[j], c_send.at[k], c_recv.at[j], (p, t, q))

    def column_arrived(q):
        return remote(block.at[1, q], col.at[q], c_send.at[0], c_recv.at[q], pair)

    @pl.loop(1, n_dp)
    def _(k):
        column_copy(k).start()

    @pl.loop(1, n_pipe)
    def _(k):
        line_copy(1, tz, z_send, z_recv, k).start()

    col[j] = block[1, j]
    for b in range(per_pipe):
        tz[p, b] = block[1, p * per_pipe + b]

    @pl.loop(1, n_dp)
    def _(k):
        column_arrived(dp_at(k)).wait_recv()

    tg[p] = col[...].reshape(plane, width).T

    ring_rows = width // RING_CHUNKS

    def ring_copy(source, c, send, device):
        ref = tg.at[source, pl.ds(c * ring_rows, ring_rows)]
        return remote(ref, ref, send.at[source, c], r_recv.at[source, c], device)

    def above(s):
        return lax.rem(p + s, n_pipe)

    def below(s):
        return lax.rem(p + n_pipe - s, n_pipe)

    for c in range(RING_CHUNKS):
        ring_copy(p, c, r_up, up).start()
        if down_hops:
            ring_copy(p, c, r_down, down).start()
    send_outputs(n_pipe // 2, n_pipe)

    @pl.loop(1, n_pipe)
    def _(k):
        q = pipe_at(k)
        line_arrived(0, hz, h_send, h_recv, q).wait_recv()
        line_arrived(1, tz, z_send, z_recv, q).wait_recv()
        delta_arrived(q).wait_recv()

    count = n_pipe * tokens
    head_cols = flatten([hz[:, b].reshape(count, width) for b in range(per_pipe)])
    top_cols = flatten([tz[:, b].reshape(count, width) for b in range(per_pipe)])
    delta_rows = delta_all[...].reshape(count, vrows).T
    row = lax.broadcasted_iota(jnp.int32, (vrows, count), 0)
    ids = flatten([ids_ref[m:m + 1, :] for m in range(ids_ref.shape[0])])
    used = (ids == first_row + row).astype(jnp.bfloat16)
    term[...] = (
        (
            jnp.dot(delta_rows, head_cols, preferred_element_type=jnp.float32)
            + math.sqrt(model) * jnp.dot(used, top_cols, preferred_element_type=jnp.float32)
        )
        .astype(jnp.bfloat16)
        .reshape(term.shape)
    )

    def core_copy(k):
        return remote(term.at[2 * k + 1 - core], core_in.at[k], t_send.at[k], t_recv.at[k], (p, t, sibling))

    def line_term(k):
        q = lax.rem(line + k, n_rows)
        return remote(
            half.at[pl.ds(2 * q, 2)], line_in.at[line], y_send.at[k], y_recv.at[line], (p, t, along(k))
        )

    def line_term_arrived(q):
        return remote(half.at[pl.ds(0, 2)], line_in.at[q], y_send.at[0], y_recv.at[q], (p, t, sibling))

    def side_copy():
        return remote(side_out, side_in, x_sem.at[0], x_sem.at[1], (p, t, across))

    def sum_cores():
        @pl.loop(0, n_chips)
        def _(k):
            core_copy(k).wait_recv()
            both = term[2 * k + core].astype(jnp.float32) + core_in[k].astype(jnp.float32)
            half[k] = both.astype(jnp.bfloat16)

        @pl.loop(1, n_rows)
        def _(k):
            line_term(k).start()

    def sum_line():
        near = half[2 * line + side].astype(jnp.float32)
        far = half[2 * line + 1 - side].astype(jnp.float32)
        for k in range(1, n_rows):
            q = lax.rem(line + n_rows - k, n_rows)
            line_term_arrived(q).wait_recv()
            near = near + line_in[q, side].astype(jnp.float32)
            far = far + line_in[q, 1 - side].astype(jnp.float32)
        tied_ref[...] = near
        side_out[...] = far.astype(jnp.bfloat16)
        side_copy().start()

    @pl.loop(0, n_chips)
    def _(k):
        core_copy(k).start()

    for s in range(1, up_hops + 1):
        for c in range(RING_CHUNKS):
            ring_copy(below(s), c, r_up, up).wait_recv()
            if s < up_hops:
                ring_copy(below(s), c, r_up, up).start()
            if s <= down_hops:
                ring_copy(above(s), c, r_down, down).wait_recv()
                if s < down_hops:
                    ring_copy(above(s), c, r_down, down).start()
        if s == 1:
            sum_cores()
        if s == up_hops - 1:
            sum_line()
    if up_hops == 1:
        sum_line()

    @pl.loop(0, n_pipe)
    def _(q):
        output_copy(q).wait_recv()
        out = ps[q].astype(jnp.float32) + ps_in[q].astype(jnp.float32)
        grad = tg[q].astype(jnp.float32) * column[...]
        stat[pl.ds(q, 1), :] = jnp.sum(out * out, axis=0, keepdims=True)
        stat[pl.ds(n_pipe + q, 1), :] = jnp.sum(out * grad, axis=0, keepdims=True)

    def stat_copy(k):
        return remote(stat, stats.at[j], st_send.at[k], st_recv.at[j], (p, t, dp_at(k)))

    def stat_arrived(q):
        return remote(stat, stats.at[q], st_send.at[0], st_recv.at[q], pair)

    @pl.loop(1, n_dp)
    def _(k):
        stat_copy(k).start()

    stats[j] = stat[...]

    side_copy().wait_recv()
    tied_ref[...] += side_in[...].astype(jnp.float32)

    @pl.loop(1, n_dp)
    def _(k):
        stat_arrived(dp_at(k)).wait_recv()

    both = jnp.sum(stats[...], axis=0)
    scale = lax.rsqrt(both[:n_pipe] / model + EPS)
    coef[0:n_pipe] = scale
    coef[n_pipe:2 * n_pipe] = scale * scale * both[n_pipe:] / model
    proj_ref[...] = jnp.zeros_like(proj_ref)

    @pl.loop(0, n_pipe)
    def _(q):
        out = ps[q].astype(jnp.float32) + ps_in[q].astype(jnp.float32)
        grad = tg[q].astype(jnp.float32) * column[...]
        out_grad = coef[pl.ds(q, 1), :] * (grad - out * coef[pl.ds(n_pipe + q, 1), :])
        proj_ref[...] += jnp.dot(
            out_grad.astype(jnp.bfloat16),
            every[q].reshape(plane, depth),
            preferred_element_type=jnp.float32,
        )

    @pl.when(is_last)
    def _():
        @pl.loop(0, last)
        def _(q):
            slice_copy(q).wait_send()
            gain_copy(q).wait_send()

        @pl.loop(0, chunks)
        def _(c):
            weight_copy(w_ref, c, w_up, up).wait_send()
            if down_hops:
                weight_copy(w_ref, c, w_down, down).wait_send()

    @pl.when(jnp.logical_not(is_last))
    def _():
        @pl.when(p < up_hops - 1)
        def _():
            @pl.loop(0, chunks)
            def _(c):
                weight_copy(w7, c, w_up, up).wait_send()

        @pl.when(p > up_hops)
        def _():
            @pl.loop(0, chunks)
            def _(c):
                weight_copy(w7, c, w_down, down).wait_send()

    values_copy(sibling, 0).wait_send()
    values_copy(across, 1).wait_send()
    forward_copy(0, True).wait_send()
    tokens_forward(0).wait_send()
    cross_copy(0).wait_send()
    sum_copy().wait_send()

    @pl.loop(1, n_rows)
    def _(k):
        values_copy(along(k), k + 1).wait_send()
        relay_copy(k).wait_send()
        forward_copy(k, False).wait_send()
        forward_copy(k, True).wait_send()

    @pl.loop(1, n_chips)
    def _(k):
        token_copy(k).wait_send()
        tokens_forward(k).wait_send()

    @pl.loop(1, n_dp)
    def _(k):
        cross_copy(k).wait_send()
        same_copy(k).wait_send()
        column_copy(k).wait_send()
        stat_copy(k).wait_send()

    @pl.loop(1, n_pipe)
    def _(k):
        line_copy(0, hz, h_send, h_recv, k).wait_send()
        line_copy(1, tz, z_send, z_recv, k).wait_send()
        delta_copy(k).wait_send()

    @pl.loop(0, n_pipe)
    def _(q):
        output_copy(q).wait_send()

    @pl.loop(0, n_chips)
    def _(k):
        core_copy(k).wait_send()

    @pl.loop(1, n_rows)
    def _(k):
        line_term(k).wait_send()

    side_copy().wait_send()
    for c in range(BACK_CHUNKS):
        back_copy(c).wait_send()
    for c in range(RING_CHUNKS):
        for s in range(up_hops):
            ring_copy(below(s), c, r_up, up).wait_send()
        for s in range(down_hops):
            ring_copy(above(s), c, r_down, down).wait_send()


def sections(weight, values, gain, embed, section_input, final_gain, target, rest, ids, offset, n_pipe, n_dp):
    dma = pltpu.SemaphoreType.DMA
    vmem = pltpu.VMEM
    half, full = jnp.bfloat16, jnp.float32
    width, depth = weight.shape
    tokens = values.shape[1]
    vrows, model = embed.shape
    per_pipe = n_dp // n_pipe
    step = model // BACK_CHUNKS
    plane = n_dp * tokens
    rows = vrows // n_dp
    cols = per_pipe * width
    chunks = width // W_CHUNK
    return pl.pallas_call(
        functools.partial(section_kernel, n_pipe, n_dp),
        out_shape=(
            jax.ShapeDtypeStruct((width, depth), full),
            jax.ShapeDtypeStruct((rows, cols), full),
        ),
        in_specs=[ANY] * 5 + [VMEM] * 4 + [SMEM],
        out_specs=(VMEM, VMEM),
        scratch_shapes=[
            vmem((vrows, model), half),
            vmem((width, depth), half),
            vmem((width, depth), half),
            vmem((n_dp, tokens, depth), half),
            vmem((1, model), full),
            vmem((n_pipe, n_dp, tokens, depth), half),
            vmem((tokens, model), half),
            vmem((n_dp, tokens, width), half),
            vmem((2, n_dp, tokens, width), half),
            vmem((tokens, 128), full),
            vmem((tokens, 128), full),
            vmem((tokens, vrows), half),
            vmem((n_pipe, tokens, vrows), half),
            vmem((BACK_CHUNKS, tokens, step), half),
            vmem((BACK_CHUNKS, tokens, step), half),
            vmem((2, n_dp, tokens, width), half),
            vmem((n_pipe, per_pipe, tokens, width), half),
            vmem((n_pipe, per_pipe, tokens, width), half),
            vmem((n_dp, tokens, width), half),
            vmem((n_pipe, width, plane), half),
            vmem((n_pipe, width, plane), half),
            vmem((n_pipe, width, plane), half),
            vmem((n_dp, rows, cols), half),
            vmem((n_dp // 2, rows, cols), half),
            vmem((n_dp // 2, rows, cols), half),
            vmem((n_dp // 4, 2, rows, cols), half),
            vmem((rows, cols), half),
            vmem((rows, cols), half),
            vmem((2 * n_pipe, plane), full),
            vmem((n_dp, 2 * n_pipe, plane), full),
            vmem((2 * n_pipe, plane), full),
            vmem((1, model), full),
            vmem((width, 1), full),
            dma((8,)), dma((chunks,)), dma((chunks,)), dma((chunks,)),
            dma, dma((n_pipe,)), dma, dma((n_pipe,)),
            dma((n_dp,)), dma((n_dp // 2,)), dma((n_dp // 2,)),
            dma((n_dp,)), dma((n_dp // 4 + 1,)), dma((n_dp // 4,)), dma((n_dp // 2,)),
            dma((2, n_dp)), dma((2, n_dp)), dma((2,)), dma((BACK_CHUNKS,)), dma((BACK_CHUNKS,)),
            dma((n_pipe,)), dma((n_pipe,)), dma((n_pipe,)), dma((n_pipe,)), dma((n_pipe,)), dma((n_pipe,)),
            dma((n_dp,)), dma((n_dp,)),
            dma((n_pipe, RING_CHUNKS)), dma((n_pipe, RING_CHUNKS)), dma((n_pipe, RING_CHUNKS)),
            dma((n_pipe,)), dma((n_pipe,)), dma((n_dp // 2,)), dma((n_dp // 2,)),
            dma((n_dp // 4,)), dma((n_dp // 4,)), dma((2,)), dma((n_dp,)), dma((n_dp,)),
        ],
        compiler_params=pltpu.CompilerParams(
            collective_id=0, has_side_effects=True, vmem_limit_bytes=56 * 1024 * 1024
        ),
        name="sections",
    )(weight, values, gain, embed, section_input, final_gain, target, rest, ids, offset)


def per_device(
    section_proj,
    attn_values,
    post_gain,
    section_input,
    final_gain,
    embed_block,
    token_ids,
    target_ids,
    block_offset,
    rest_lse,
):
    n_pipe, n_dp = lax.axis_size("pipe"), lax.axis_size("dp")
    weight = section_proj[0]
    count = section_input.shape[0] * section_input.shape[1]
    own_grad, tied = sections(
        weight,
        attn_values.reshape(n_pipe, count // n_pipe, weight.shape[1]),
        post_gain,
        embed_block,
        section_input.reshape(count, section_input.shape[2]),
        final_gain,
        target_ids,
        rest_lse,
        token_ids,
        block_offset,
        n_pipe,
        n_dp,
    )
    return (own_grad[None], tied)


def solution(mesh):
    in_specs = (
        P("pipe", "dp", "tensor"),
        P("pipe", None, "dp", "tensor"),
        P("pipe", None),
        P(None, "dp", None),
        P(),
        P("tensor", None),
        P(None, "dp"),
        P(None, "dp"),
        P(),
        P(None, "dp"),
    )
    out_specs = (P("pipe", "dp", "tensor"), P(("tensor", "dp"), "pipe"))
    return jax.shard_map(
        per_device, mesh=mesh, in_specs=in_specs, out_specs=out_specs, check_vma=False
    )
```

```python
import functools
import math

import jax
import jax.numpy as jnp
from jax import lax
from jax.experimental import pallas as pl
from jax.experimental.pallas import tpu as pltpu
from jax.sharding import PartitionSpec as P

EPS = 1e-06
CAP = 30.0
MESH = pl.DeviceIdType.MESH
ANY = pl.BlockSpec(memory_space=pl.ANY)
VMEM = pl.BlockSpec(memory_space=pltpu.VMEM)
SMEM = pl.BlockSpec(memory_space=pltpu.SMEM)
CONTRACT_LAST = (((1,), (1,)), ((), ()))
W_CHUNK = 32
BACK_CHUNKS = 4
RING_CHUNKS = 3


def position():
    return lax.axis_index("pipe"), lax.axis_index("tensor"), lax.axis_index("dp")


def remote(src, dst, send_sem, recv_sem, device):
    return pltpu.make_async_remote_copy(
        src_ref=src,
        dst_ref=dst,
        send_sem=send_sem,
        recv_sem=recv_sem,
        device_id=device,
        device_id_type=MESH,
    )


def signal(sem, device):
    pl.semaphore_signal(sem, inc=1, device_id=device, device_id_type=MESH)


def greet_pipe(barrier, n_pipe):
    p, t, j = position()

    @pl.loop(1, n_pipe)
    def _(k):
        signal(barrier, (lax.rem(p + k, n_pipe), t, j))


def greet_dp(barrier, n_dp):
    p, t, j = position()

    @pl.loop(1, n_dp)
    def _(k):
        signal(barrier, (p, t, lax.rem(j + k, n_dp)))


def normalize(value):
    scale = lax.rsqrt(jnp.mean(value * value, axis=-1, keepdims=True) + EPS)
    return scale, value * scale


def own_tokens(ref, first, tokens):
    micro, per = ref.shape
    lane = lax.broadcasted_iota(jnp.int32, (tokens, per), 1)
    token = lax.broadcasted_iota(jnp.int32, (tokens, per), 0) + first
    found = jnp.zeros((tokens, per), jnp.float32)
    for m in range(micro):
        row = jnp.broadcast_to(ref[m:m + 1, :].astype(jnp.float32), (tokens, per))
        found = found + jnp.where(lane + m * per == token, row, 0.0)
    return jnp.sum(found, axis=1, keepdims=True)


def flatten(blocks):
    return jnp.concatenate(blocks, axis=1)


def section_kernel(
    n_pipe, n_dp,
    w_ref, a_ref, gain_ref, embed_ref, input_ref, fgain_ref, target_ref, rest_ref, ids_ref, offset_ref,
    proj_ref, tied_ref,
    embed, w, w7, a7, g7, every, rows_in, part, parts, sum_out, sum_in, delta_out, delta_all,
    back_out, back_in, block, line_out, hz, tz, col, tg, ps, ps_in, term, core_in, half, line_in, side_out, side_in, stat, stats, coef, gains, column,
    l_sem, w_recv, w_up, w_down, s_recv, s_send, g_recv, g_send, a_recv, a_send, a_fwd, v_recv, v_send, v_relay, v_fwd,
    p_recv, p_send, sum_sem, back_recv, back_send, d_recv, d_send, h_recv, h_send, z_recv, z_send,
    c_recv, c_send, r_recv, r_up, r_down, o_recv, o_send, t_recv, t_send, y_recv, y_send, x_sem, st_recv, st_send,
):
    p, t, j = position()
    last = n_pipe - 1
    up_hops = n_pipe // 2
    down_hops = last - up_hops
    other = 1 - t
    core = lax.rem(j, 2)
    sibling = j + 1 - 2 * core
    n_chips = n_dp // 2
    n_rows = n_chips // 2
    chip = j // 2
    side = lax.rem(chip, 2)
    line = chip // 2
    across = 2 * (chip + 1 - 2 * side) + core
    chunks = w_ref.shape[0] // W_CHUNK
    is_last = p == last
    up = (lax.rem(p + 1, n_pipe), t, j)
    down = (lax.rem(p + last, n_pipe), t, j)
    pair = (p, other, j)
    tokens, width = part.shape[1:]
    vrows, model = embed.shape
    plane = n_dp * tokens
    depth = w.shape[1]
    mine = pl.ds(pl.multiple_of(p * tokens, tokens), tokens)

    def dp_at(k):
        return lax.rem(j + k, n_dp)

    def pipe_at(k):
        return lax.rem(p + k, n_pipe)

    load_embed = pltpu.make_async_copy(embed_ref, embed, l_sem.at[0])
    load_weight = pltpu.make_async_copy(w_ref, w, l_sem.at[1])
    load_rows = pltpu.make_async_copy(input_ref.at[mine], rows_in, l_sem.at[2])
    load_values = pltpu.make_async_copy(a_ref, every.at[:, j], l_sem.at[3])
    load_gains = pltpu.make_async_copy(gain_ref, gains, l_sem.at[7])
    load_weight.start()
    load_rows.start()
    load_gains.start()

    barrier = pltpu.get_barrier_semaphore()
    greet_pipe(barrier, n_pipe)
    greet_dp(barrier, n_dp)

    @pl.loop(0, n_dp)
    def _(k):
        signal(barrier, (p, other, k))

    pl.semaphore_wait(barrier, 2 * n_dp - 1 + n_pipe - 1)

    def piece(ref, c):
        return ref.at[pl.ds(pl.multiple_of(c * W_CHUNK, W_CHUNK), W_CHUNK)]

    def slice_copy(q):
        return remote(a_ref.at[q], a7.at[j], s_send.at[q], s_recv, (q, t, j))

    def gain_copy(q):
        return remote(gain_ref, g7, g_send.at[q], g_recv, (q, t, j))

    def weight_copy(source, c, sems, device):
        return remote(piece(source, c), piece(w7, c), sems.at[c], w_recv.at[c], device)

    def along(k):
        return (lax.rem(line + k, n_rows) * 2 + side) * 2 + core

    def source_of(k, far):
        place = lax.rem(line + n_rows - k, n_rows) * 2
        return (place + (1 - side if far else side)) * 2 + core

    def values_copy(q, sem):
        return remote(a_ref, every.at[:, j], v_send.at[sem], v_recv.at[j], (p, t, q))

    def pass_copy(owner, q, sem):
        return remote(every.at[:, owner], every.at[:, owner], sem, v_recv.at[owner], (p, t, q))

    def relay_copy(k):
        return pass_copy(across, along(k), v_relay.at[k])

    def forward_copy(k, far):
        return pass_copy(source_of(k, far), sibling, v_fwd.at[k + (n_rows if far else 0)])

    def values_arrived(owner):
        return remote(a_ref, every.at[:, owner], v_send.at[0], v_recv.at[owner], (p, t, sibling))

    own_slice = pltpu.make_async_copy(a_ref.at[last], a7.at[j], l_sem.at[4])
    own_weight = pltpu.make_async_copy(w_ref, w7, l_sem.at[5])
    own_gain = pltpu.make_async_copy(gain_ref, g7, l_sem.at[6])

    @pl.when(is_last)
    def _():
        own_slice.start()

        @pl.loop(0, last)
        def _(q):
            slice_copy(q).start()

        @pl.loop(0, chunks)
        def _(c):
            weight_copy(w_ref, c, w_up, up).start()
            if down_hops:
                weight_copy(w_ref, c, w_down, down).start()

        @pl.loop(0, last)
        def _(q):
            gain_copy(q).start()

        own_weight.start()
        own_gain.start()

    values_copy(across, 1).start()

    @pl.loop(1, n_rows)
    def _(k):
        values_copy(along(k), k + 1).start()

    values_copy(sibling, 0).start()
    load_values.start()
    load_embed.start()

    load_gains.wait()
    wide = pl.cdiv(width, 128) * 128
    turned = pltpu.roll(
        jnp.broadcast_to(gains[...], (8, model)), lax.rem(model - width * j, model), 1
    )
    column[...] = turned[:, :wide].T[:width, 0:1]

    @pl.when(is_last)
    def _():
        own_slice.wait()

    @pl.when(jnp.logical_not(is_last))
    def _():
        slice_copy(p).wait_recv()

    def token_copy(k):
        q = lax.rem(chip + k, n_chips) * 2 + core
        return remote(a7.at[j], a7.at[j], a_send.at[k], a_recv.at[j], (p, t, q))

    def tokens_arrived(q):
        return remote(a7.at[j], a7.at[q], a_send.at[0], a_recv.at[q], (p, t, sibling))

    def tokens_forward(k):
        owner = lax.rem(chip + n_chips - k, n_chips) * 2 + core
        return remote(a7.at[owner], a7.at[owner], a_fwd.at[k], a_recv.at[owner], (p, t, sibling))

    @pl.loop(1, n_chips)
    def _(k):
        token_copy(k).start()

    tokens_forward(0).start()

    def relay():
        values_arrived(across).wait_recv()

        @pl.loop(1, n_rows)
        def _(k):
            relay_copy(k).start()

        forward_copy(0, True).start()

        @pl.loop(1, n_chips)
        def _(k):
            tokens_arrived(lax.rem(chip + n_chips - k, n_chips) * 2 + core).wait_recv()
            tokens_forward(k).start()

    next_to_last = jnp.logical_or(p == 0, p == last - 1)
    relay_at = jnp.where(next_to_last, min(4, chunks - 1), 0)

    @pl.when(is_last)
    def _():
        relay()
        own_weight.wait()
        own_gain.wait()

    @pl.when(jnp.logical_not(is_last))
    def _():
        @pl.loop(0, chunks)
        def _(c):
            weight_copy(w_ref, c, w_up, up).wait_recv()

            @pl.when(p < up_hops - 1)
            def _():
                weight_copy(w7, c, w_up, up).start()

            @pl.when(p > up_hops)
            def _():
                weight_copy(w7, c, w_down, down).start()

            @pl.when(c == relay_at)
            def _():
                relay()

        gain_copy(p).wait_recv()

    @pl.loop(0, n_chips)
    def _(k):
        tokens_arrived(2 * k + 1 - core).wait_recv()

    part[...] = (
        lax.dot_general(
            a7[...].reshape(plane, depth), w7[...], CONTRACT_LAST, preferred_element_type=jnp.float32
        )
        .astype(jnp.bfloat16)
        .reshape(n_dp, tokens, width)
    )

    def same_copy(k):
        q = dp_at(k)
        return remote(part.at[q], parts.at[t, j], p_send.at[0, k], p_recv.at[t, j], (p, t, q))

    def cross_copy(k):
        q = dp_at(k)
        return remote(part.at[q], parts.at[t, j], p_send.at[1, k], p_recv.at[t, j], (p, other, q))

    def part_arrived(group, q):
        return remote(part.at[q], parts.at[group, q], p_send.at[0, 0], p_recv.at[group, q], pair)

    @pl.loop(0, n_dp)
    def _(k):
        cross_copy(k).start()

    @pl.loop(1, n_dp)
    def _(k):
        same_copy(k).start()

    parts[t, j] = part[j]

    @pl.loop(1, n_rows)
    def _(k):
        for far in (False, True):
            values_arrived(source_of(k, far)).wait_recv()
            forward_copy(k, far).start()

    load_weight.wait()
    load_values.wait()

    @pl.loop(0, n_chips)
    def _(k):
        values_arrived(2 * k + 1 - core).wait_recv()

    def output_copy(q):
        return remote(ps.at[q], ps_in.at[q], o_send.at[q], o_recv.at[q], pair)

    @pl.loop(0, n_pipe)
    def _(q):
        ps[q] = lax.dot_general(
            w[...], every[q].reshape(plane, depth), CONTRACT_LAST, preferred_element_type=jnp.float32
        ).astype(jnp.bfloat16)

    def send_outputs(first, stop):
        @pl.loop(first, stop)
        def _(q):
            output_copy(q).start()

    after_parts = n_pipe // 2 - n_pipe // 8
    send_outputs(0, n_pipe // 4)

    load_rows.wait()
    load_embed.wait()

    @pl.loop(0, n_dp)
    def _(k):
        part_arrived(other, k).wait_recv()

    @pl.loop(1, n_dp)
    def _(k):
        part_arrived(t, dp_at(k)).wait_recv()

    send_outputs(n_pipe // 4, after_parts)
    output = flatten(
        [parts[0, q].astype(jnp.float32) + parts[1, q].astype(jnp.float32) for q in range(n_dp)]
    )
    _, normed = normalize(output)
    final_gain = fgain_ref[...].reshape(1, model)
    resid = rows_in[...].astype(jnp.float32) + normed * g7[...]
    y_scale, y_normed = normalize(resid)
    head_in = (y_normed * final_gain).astype(jnp.bfloat16)
    cols = hz.shape[2]
    for q in range(n_pipe):
        line_out[0, q] = head_in[:, q * cols:(q + 1) * cols]

    def line_copy(slot, dst, send, recv, k):
        q = pipe_at(k)
        return remote(line_out.at[slot, q], dst.at[p], send.at[k], recv.at[p], (q, t, j))

    def line_arrived(slot, dst, send, recv, q):
        return remote(line_out.at[slot, q], dst.at[q], send.at[0], recv.at[q], (q, t, j))

    @pl.loop(1, n_pipe)
    def _(k):
        line_copy(0, hz, h_send, h_recv, k).start()

    hz[p] = line_out[0, p]

    raw = lax.dot_general(head_in, embed[...], CONTRACT_LAST, preferred_element_type=jnp.float32)
    capped = jnp.tanh(raw / CAP)
    logits = CAP * capped
    own_sum = jnp.sum(jnp.exp(logits), axis=1, keepdims=True)
    sum_out[...] = jnp.broadcast_to(own_sum, sum_out.shape)

    def sum_copy():
        return remote(sum_out, sum_in, sum_sem.at[0], sum_sem.at[1], pair)

    sum_copy().start()
    lane = lax.broadcasted_iota(jnp.int32, (tokens, vrows), 1)
    first_row = offset_ref[0] + t * vrows
    target = own_tokens(target_ref, p * tokens, tokens)
    hit = (target == (first_row + lane).astype(jnp.float32)).astype(jnp.float32)
    slope = 1.0 - capped * capped
    sum_copy().wait_recv()
    log_total = jnp.log(own_sum + sum_in[:, 0:1])
    rest = own_tokens(rest_ref, p * tokens, tokens)
    lse = jnp.maximum(rest, log_total) + jnp.log(1.0 + jnp.exp(-jnp.abs(rest - log_total)))
    delta = ((jnp.exp(logits - lse) - hit) * slope).astype(jnp.bfloat16)
    delta_out[...] = delta
    delta_all[p] = delta

    step = model // BACK_CHUNKS

    def back_copy(c):
        return remote(back_out.at[c], back_in.at[c], back_send.at[c], back_recv.at[c], pair)

    for c in range(BACK_CHUNKS):
        grad = jnp.dot(delta, embed[:, c * step:(c + 1) * step], preferred_element_type=jnp.float32)
        back_out[c] = grad.astype(jnp.bfloat16)
        back_copy(c).start()

    def delta_copy(k):
        return remote(delta_out, delta_all.at[p], d_send.at[k], d_recv.at[p], (pipe_at(k), t, j))

    def delta_arrived(q):
        return remote(delta_out, delta_all.at[q], d_send.at[0], d_recv.at[q], (q, t, j))

    @pl.loop(1, n_pipe)
    def _(k):
        delta_copy(k).start()

    grads = []
    for c in range(BACK_CHUNKS):
        back_copy(c).wait_recv()
        grads.append(back_out[c].astype(jnp.float32) + back_in[c].astype(jnp.float32))
    grad = flatten(grads) * final_gain
    top = y_scale * (grad - y_normed * jnp.mean(grad * y_normed, axis=-1, keepdims=True))
    top = top.astype(jnp.bfloat16)
    for b in range(n_dp):
        block[b] = top[:, b * width:(b + 1) * width]
    for q in range(n_pipe):
        line_out[1, q] = top[:, q * cols:(q + 1) * cols]

    def column_copy(k):
        q = dp_at(k)
        return remote(block.at[q], col.at[j], c_send.at[k], c_recv.at[j], (p, t, q))

    def column_arrived(q):
        return remote(block.at[q], col.at[q], c_send.at[0], c_recv.at[q], pair)

    @pl.loop(1, n_dp)
    def _(k):
        column_copy(k).start()

    @pl.loop(1, n_pipe)
    def _(k):
        line_copy(1, tz, z_send, z_recv, k).start()

    send_outputs(after_parts, n_pipe // 2)
    col[j] = block[j]
    tz[p] = line_out[1, p]

    @pl.loop(1, n_dp)
    def _(k):
        column_arrived(dp_at(k)).wait_recv()

    tg[p] = col[...].reshape(plane, width).T

    ring_rows = width // RING_CHUNKS

    def ring_copy(source, c, send, device):
        ref = tg.at[source, pl.ds(c * ring_rows, ring_rows)]
        return remote(ref, ref, send.at[source, c], r_recv.at[source, c], device)

    def above(s):
        return lax.rem(p + s, n_pipe)

    def below(s):
        return lax.rem(p + n_pipe - s, n_pipe)

    for c in range(RING_CHUNKS):
        ring_copy(p, c, r_up, up).start()
        if down_hops:
            ring_copy(p, c, r_down, down).start()
    send_outputs(n_pipe // 2, n_pipe)

    @pl.loop(1, n_pipe)
    def _(k):
        q = pipe_at(k)
        line_arrived(0, hz, h_send, h_recv, q).wait_recv()
        line_arrived(1, tz, z_send, z_recv, q).wait_recv()
        delta_arrived(q).wait_recv()

    count = n_pipe * tokens
    head_cols = hz[...].reshape(count, cols)
    top_cols = tz[...].reshape(count, cols)
    delta_rows = delta_all[...].reshape(count, vrows).T
    row = lax.broadcasted_iota(jnp.int32, (vrows, count), 0)
    ids = flatten([ids_ref[m:m + 1, :] for m in range(ids_ref.shape[0])])
    used = (ids == first_row + row).astype(jnp.bfloat16)
    term[...] = (
        (
            jnp.dot(delta_rows, head_cols, preferred_element_type=jnp.float32)
            + math.sqrt(model) * jnp.dot(used, top_cols, preferred_element_type=jnp.float32)
        )
        .astype(jnp.bfloat16)
        .reshape(term.shape)
    )

    def core_copy(k):
        return remote(term.at[2 * k + 1 - core], core_in.at[k], t_send.at[k], t_recv.at[k], (p, t, sibling))

    def line_term(k):
        q = lax.rem(line + k, n_rows)
        return remote(
            half.at[pl.ds(2 * q, 2)], line_in.at[line], y_send.at[k], y_recv.at[line], (p, t, along(k))
        )

    def line_term_arrived(q):
        return remote(half.at[pl.ds(0, 2)], line_in.at[q], y_send.at[0], y_recv.at[q], (p, t, sibling))

    def side_copy():
        return remote(side_out, side_in, x_sem.at[0], x_sem.at[1], (p, t, across))

    def sum_cores():
        @pl.loop(0, n_chips)
        def _(k):
            core_copy(k).wait_recv()
            both = term[2 * k + core].astype(jnp.float32) + core_in[k].astype(jnp.float32)
            half[k] = both.astype(jnp.bfloat16)

        @pl.loop(1, n_rows)
        def _(k):
            line_term(k).start()

    def sum_line():
        near = half[2 * line + side].astype(jnp.float32)
        far = half[2 * line + 1 - side].astype(jnp.float32)
        for k in range(1, n_rows):
            q = lax.rem(line + n_rows - k, n_rows)
            line_term_arrived(q).wait_recv()
            near = near + line_in[q, side].astype(jnp.float32)
            far = far + line_in[q, 1 - side].astype(jnp.float32)
        tied_ref[...] = near
        side_out[...] = far.astype(jnp.bfloat16)
        side_copy().start()

    @pl.loop(0, n_chips)
    def _(k):
        core_copy(k).start()

    for s in range(1, up_hops + 1):
        for c in range(RING_CHUNKS):
            ring_copy(below(s), c, r_up, up).wait_recv()
            if s < up_hops:
                ring_copy(below(s), c, r_up, up).start()
            if s <= down_hops:
                ring_copy(above(s), c, r_down, down).wait_recv()
                if s < down_hops:
                    ring_copy(above(s), c, r_down, down).start()
        if s == 1:
            sum_cores()
        if s == up_hops - 1:
            sum_line()
    if up_hops == 1:
        sum_line()

    @pl.loop(0, n_pipe)
    def _(q):
        output_copy(q).wait_recv()
        out = ps[q].astype(jnp.float32) + ps_in[q].astype(jnp.float32)
        grad = tg[q].astype(jnp.float32) * column[...]
        stat[pl.ds(q, 1), :] = jnp.sum(out * out, axis=0, keepdims=True)
        stat[pl.ds(n_pipe + q, 1), :] = jnp.sum(out * grad, axis=0, keepdims=True)

    def stat_copy(k):
        return remote(stat, stats.at[j], st_send.at[k], st_recv.at[j], (p, t, dp_at(k)))

    def stat_arrived(q):
        return remote(stat, stats.at[q], st_send.at[0], st_recv.at[q], pair)

    @pl.loop(1, n_dp)
    def _(k):
        stat_copy(k).start()

    stats[j] = stat[...]

    side_copy().wait_recv()
    tied_ref[...] += side_in[...].astype(jnp.float32)

    @pl.loop(1, n_dp)
    def _(k):
        stat_arrived(dp_at(k)).wait_recv()

    both = jnp.sum(stats[...], axis=0)
    scale = lax.rsqrt(both[:n_pipe] / model + EPS)
    coef[0:n_pipe] = scale
    coef[n_pipe:2 * n_pipe] = scale * scale * both[n_pipe:] / model
    proj_ref[...] = jnp.zeros_like(proj_ref)

    @pl.loop(0, n_pipe)
    def _(q):
        out = ps[q].astype(jnp.float32) + ps_in[q].astype(jnp.float32)
        grad = tg[q].astype(jnp.float32) * column[...]
        out_grad = coef[pl.ds(q, 1), :] * (grad - out * coef[pl.ds(n_pipe + q, 1), :])
        proj_ref[...] += jnp.dot(
            out_grad.astype(jnp.bfloat16),
            every[q].reshape(plane, depth),
            preferred_element_type=jnp.float32,
        )

    @pl.when(is_last)
    def _():
        @pl.loop(0, last)
        def _(q):
            slice_copy(q).wait_send()
            gain_copy(q).wait_send()

        @pl.loop(0, chunks)
        def _(c):
            weight_copy(w_ref, c, w_up, up).wait_send()
            if down_hops:
                weight_copy(w_ref, c, w_down, down).wait_send()

    @pl.when(jnp.logical_not(is_last))
    def _():
        @pl.when(p < up_hops - 1)
        def _():
            @pl.loop(0, chunks)
            def _(c):
                weight_copy(w7, c, w_up, up).wait_send()

        @pl.when(p > up_hops)
        def _():
            @pl.loop(0, chunks)
            def _(c):
                weight_copy(w7, c, w_down, down).wait_send()

    values_copy(sibling, 0).wait_send()
    values_copy(across, 1).wait_send()
    forward_copy(0, True).wait_send()
    tokens_forward(0).wait_send()
    cross_copy(0).wait_send()
    sum_copy().wait_send()

    @pl.loop(1, n_rows)
    def _(k):
        values_copy(along(k), k + 1).wait_send()
        relay_copy(k).wait_send()
        forward_copy(k, False).wait_send()
        forward_copy(k, True).wait_send()

    @pl.loop(1, n_chips)
    def _(k):
        token_copy(k).wait_send()
        tokens_forward(k).wait_send()

    @pl.loop(1, n_dp)
    def _(k):
        cross_copy(k).wait_send()
        same_copy(k).wait_send()
        column_copy(k).wait_send()
        stat_copy(k).wait_send()

    @pl.loop(1, n_pipe)
    def _(k):
        line_copy(0, hz, h_send, h_recv, k).wait_send()
        line_copy(1, tz, z_send, z_recv, k).wait_send()
        delta_copy(k).wait_send()

    @pl.loop(0, n_pipe)
    def _(q):
        output_copy(q).wait_send()

    @pl.loop(0, n_chips)
    def _(k):
        core_copy(k).wait_send()

    @pl.loop(1, n_rows)
    def _(k):
        line_term(k).wait_send()

    side_copy().wait_send()
    for c in range(BACK_CHUNKS):
        back_copy(c).wait_send()
    for c in range(RING_CHUNKS):
        for s in range(up_hops):
            ring_copy(below(s), c, r_up, up).wait_send()
        for s in range(down_hops):
            ring_copy(above(s), c, r_down, down).wait_send()


def sections(weight, values, gain, embed, section_input, final_gain, target, rest, ids, offset, n_pipe, n_dp):
    dma = pltpu.SemaphoreType.DMA
    vmem = pltpu.VMEM
    half, full = jnp.bfloat16, jnp.float32
    width, depth = weight.shape
    tokens = values.shape[1]
    vrows, model = embed.shape
    per_pipe = n_dp // n_pipe
    step = model // BACK_CHUNKS
    plane = n_dp * tokens
    rows = vrows // n_dp
    cols = per_pipe * width
    chunks = width // W_CHUNK
    return pl.pallas_call(
        functools.partial(section_kernel, n_pipe, n_dp),
        out_shape=(
            jax.ShapeDtypeStruct((width, depth), full),
            jax.ShapeDtypeStruct((rows, cols), full),
        ),
        in_specs=[ANY] * 5 + [VMEM] * 4 + [SMEM],
        out_specs=(VMEM, VMEM),
        scratch_shapes=[
            vmem((vrows, model), half),
            vmem((width, depth), half),
            vmem((width, depth), half),
            vmem((n_dp, tokens, depth), half),
            vmem((1, model), full),
            vmem((n_pipe, n_dp, tokens, depth), half),
            vmem((tokens, model), half),
            vmem((n_dp, tokens, width), half),
            vmem((2, n_dp, tokens, width), half),
            vmem((tokens, 128), full),
            vmem((tokens, 128), full),
            vmem((tokens, vrows), half),
            vmem((n_pipe, tokens, vrows), half),
            vmem((BACK_CHUNKS, tokens, step), half),
            vmem((BACK_CHUNKS, tokens, step), half),
            vmem((n_dp, tokens, width), half),
            vmem((2, n_pipe, tokens, cols), half),
            vmem((n_pipe, tokens, cols), half),
            vmem((n_pipe, tokens, cols), half),
            vmem((n_dp, tokens, width), half),
            vmem((n_pipe, width, plane), half),
            vmem((n_pipe, width, plane), half),
            vmem((n_pipe, width, plane), half),
            vmem((n_dp, rows, cols), half),
            vmem((n_dp // 2, rows, cols), half),
            vmem((n_dp // 2, rows, cols), half),
            vmem((n_dp // 4, 2, rows, cols), half),
            vmem((rows, cols), half),
            vmem((rows, cols), half),
            vmem((2 * n_pipe, plane), full),
            vmem((n_dp, 2 * n_pipe, plane), full),
            vmem((2 * n_pipe, plane), full),
            vmem((1, model), full),
            vmem((width, 1), full),
            dma((8,)), dma((chunks,)), dma((chunks,)), dma((chunks,)),
            dma, dma((n_pipe,)), dma, dma((n_pipe,)),
            dma((n_dp,)), dma((n_dp // 2,)), dma((n_dp // 2,)),
            dma((n_dp,)), dma((n_dp // 4 + 1,)), dma((n_dp // 4,)), dma((n_dp // 2,)),
            dma((2, n_dp)), dma((2, n_dp)), dma((2,)), dma((BACK_CHUNKS,)), dma((BACK_CHUNKS,)),
            dma((n_pipe,)), dma((n_pipe,)), dma((n_pipe,)), dma((n_pipe,)), dma((n_pipe,)), dma((n_pipe,)),
            dma((n_dp,)), dma((n_dp,)),
            dma((n_pipe, RING_CHUNKS)), dma((n_pipe, RING_CHUNKS)), dma((n_pipe, RING_CHUNKS)),
            dma((n_pipe,)), dma((n_pipe,)), dma((n_dp // 2,)), dma((n_dp // 2,)),
            dma((n_dp // 4,)), dma((n_dp // 4,)), dma((2,)), dma((n_dp,)), dma((n_dp,)),
        ],
        compiler_params=pltpu.CompilerParams(
            collective_id=0, has_side_effects=True, vmem_limit_bytes=56 * 1024 * 1024
        ),
        name="sections",
    )(weight, values, gain, embed, section_input, final_gain, target, rest, ids, offset)


def per_device(
    section_proj,
    attn_values,
    post_gain,
    section_input,
    final_gain,
    embed_block,
    token_ids,
    target_ids,
    block_offset,
    rest_lse,
):
    n_pipe, n_dp = lax.axis_size("pipe"), lax.axis_size("dp")
    weight = section_proj[0]
    count = section_input.shape[0] * section_input.shape[1]
    own_grad, tied = sections(
        weight,
        attn_values.reshape(n_pipe, count // n_pipe, weight.shape[1]),
        post_gain,
        embed_block,
        section_input.reshape(count, section_input.shape[2]),
        final_gain,
        target_ids,
        rest_lse,
        token_ids,
        block_offset,
        n_pipe,
        n_dp,
    )
    return (own_grad[None], tied)


def solution(mesh):
    in_specs = (
        P("pipe", "dp", "tensor"),
        P("pipe", None, "dp", "tensor"),
        P("pipe", None),
        P(None, "dp", None),
        P(),
        P("tensor", None),
        P(None, "dp"),
        P(None, "dp"),
        P(),
        P(None, "dp"),
    )
    out_specs = (P("pipe", "dp", "tensor"), P(("tensor", "dp"), "pipe"))
    return jax.shard_map(
        per_device, mesh=mesh, in_specs=in_specs, out_specs=out_specs, check_vma=False
    )
```

```python
import functools
import math

import jax
import jax.numpy as jnp
from jax import lax
from jax.experimental import pallas as pl
from jax.experimental.pallas import tpu as pltpu
from jax.sharding import PartitionSpec as P

EPS = 1e-06
CAP = 30.0
MESH = pl.DeviceIdType.MESH
ANY = pl.BlockSpec(memory_space=pl.ANY)
VMEM = pl.BlockSpec(memory_space=pltpu.VMEM)
SMEM = pl.BlockSpec(memory_space=pltpu.SMEM)
CONTRACT_LAST = (((1,), (1,)), ((), ()))
W_CHUNK = 32
BACK_CHUNKS = 4
RING_CHUNKS = 3


def position():
    return lax.axis_index("pipe"), lax.axis_index("tensor"), lax.axis_index("dp")


def remote(src, dst, send_sem, recv_sem, device):
    return pltpu.make_async_remote_copy(
        src_ref=src,
        dst_ref=dst,
        send_sem=send_sem,
        recv_sem=recv_sem,
        device_id=device,
        device_id_type=MESH,
    )


def signal(sem, device):
    pl.semaphore_signal(sem, inc=1, device_id=device, device_id_type=MESH)


def greet_pipe(barrier, n_pipe):
    p, t, j = position()

    @pl.loop(1, n_pipe)
    def _(k):
        signal(barrier, (lax.rem(p + k, n_pipe), t, j))


def greet_dp(barrier, n_dp):
    p, t, j = position()

    @pl.loop(1, n_dp)
    def _(k):
        signal(barrier, (p, t, lax.rem(j + k, n_dp)))


def normalize(value):
    scale = lax.rsqrt(jnp.mean(value * value, axis=-1, keepdims=True) + EPS)
    return scale, value * scale


def own_tokens(ref, first, tokens):
    micro, per = ref.shape
    lane = lax.broadcasted_iota(jnp.int32, (tokens, per), 1)
    token = lax.broadcasted_iota(jnp.int32, (tokens, per), 0) + first
    found = jnp.zeros((tokens, per), jnp.float32)
    for m in range(micro):
        row = jnp.broadcast_to(ref[m:m + 1, :].astype(jnp.float32), (tokens, per))
        found = found + jnp.where(lane + m * per == token, row, 0.0)
    return jnp.sum(found, axis=1, keepdims=True)


def flatten(blocks):
    return jnp.concatenate(blocks, axis=1)


def section_kernel(
    n_pipe, n_dp,
    w_ref, a_ref, gain_ref, embed_ref, input_ref, fgain_ref, target_ref, rest_ref, ids_ref, offset_ref,
    proj_ref, tied_ref,
    embed, w, w7, a7, g7, every, rows_in, part, parts, sum_out, sum_in, delta_out, delta_all,
    back_out, back_in, block, line_out, hz, tz, col, tg, ps, ps_in, term, core_in, half, line_in, side_out, side_in, stat, stats, coef, gains, column,
    l_sem, w_recv, w_up, w_down, s_recv, s_send, g_recv, g_send, a_recv, a_send, a_fwd, v_recv, v_send, v_relay, v_fwd,
    p_recv, p_send, sum_sem, back_recv, back_send, d_recv, d_send, h_recv, h_send, z_recv, z_send,
    c_recv, c_send, r_recv, r_up, r_down, o_recv, o_send, t_recv, t_send, y_recv, y_send, x_sem, st_recv, st_send,
):
    p, t, j = position()
    last = n_pipe - 1
    up_hops = n_pipe // 2
    down_hops = last - up_hops
    other = 1 - t
    core = lax.rem(j, 2)
    sibling = j + 1 - 2 * core
    n_chips = n_dp // 2
    n_rows = n_chips // 2
    chip = j // 2
    side = lax.rem(chip, 2)
    line = chip // 2
    across = 2 * (chip + 1 - 2 * side) + core
    chunks = w_ref.shape[0] // W_CHUNK
    is_last = p == last
    up = (lax.rem(p + 1, n_pipe), t, j)
    down = (lax.rem(p + last, n_pipe), t, j)
    pair = (p, other, j)
    tokens, width = part.shape[1:]
    vrows, model = embed.shape
    plane = n_dp * tokens
    depth = w.shape[1]
    mine = pl.ds(pl.multiple_of(p * tokens, tokens), tokens)

    def dp_at(k):
        return lax.rem(j + k, n_dp)

    def pipe_at(k):
        return lax.rem(p + k, n_pipe)

    load_embed = pltpu.make_async_copy(embed_ref, embed, l_sem.at[0])
    load_weight = pltpu.make_async_copy(w_ref, w, l_sem.at[1])
    load_rows = pltpu.make_async_copy(input_ref.at[mine], rows_in, l_sem.at[2])
    load_values = pltpu.make_async_copy(a_ref, every.at[:, j], l_sem.at[3])
    load_gains = pltpu.make_async_copy(gain_ref, gains, l_sem.at[7])
    load_weight.start()
    load_rows.start()
    load_gains.start()

    barrier = pltpu.get_barrier_semaphore()
    greet_pipe(barrier, n_pipe)
    greet_dp(barrier, n_dp)

    @pl.loop(0, n_dp)
    def _(k):
        signal(barrier, (p, other, k))

    pl.semaphore_wait(barrier, 2 * n_dp - 1 + n_pipe - 1)

    def piece(ref, c):
        return ref.at[pl.ds(pl.multiple_of(c * W_CHUNK, W_CHUNK), W_CHUNK)]

    def slice_copy(q):
        return remote(a_ref.at[q], a7.at[j], s_send.at[q], s_recv, (q, t, j))

    def gain_copy(q):
        return remote(gain_ref, g7, g_send.at[q], g_recv, (q, t, j))

    def weight_copy(source, c, sems, device):
        return remote(piece(source, c), piece(w7, c), sems.at[c], w_recv.at[c], device)

    def along(k):
        return (lax.rem(line + k, n_rows) * 2 + side) * 2 + core

    def source_of(k, far):
        place = lax.rem(line + n_rows - k, n_rows) * 2
        return (place + (1 - side if far else side)) * 2 + core

    def values_copy(q, sem):
        return remote(a_ref, every.at[:, j], v_send.at[sem], v_recv.at[j], (p, t, q))

    def pass_copy(owner, q, sem):
        return remote(every.at[:, owner], every.at[:, owner], sem, v_recv.at[owner], (p, t, q))

    def relay_copy(k):
        return pass_copy(across, along(k), v_relay.at[k])

    def forward_copy(k, far):
        return pass_copy(source_of(k, far), sibling, v_fwd.at[k + (n_rows if far else 0)])

    def values_arrived(owner):
        return remote(a_ref, every.at[:, owner], v_send.at[0], v_recv.at[owner], (p, t, sibling))

    own_slice = pltpu.make_async_copy(a_ref.at[last], a7.at[j], l_sem.at[4])
    own_weight = pltpu.make_async_copy(w_ref, w7, l_sem.at[5])
    own_gain = pltpu.make_async_copy(gain_ref, g7, l_sem.at[6])

    @pl.when(is_last)
    def _():
        own_slice.start()

        @pl.loop(0, last)
        def _(q):
            slice_copy(q).start()

        @pl.loop(0, chunks)
        def _(c):
            weight_copy(w_ref, c, w_up, up).start()
            if down_hops:
                weight_copy(w_ref, c, w_down, down).start()

        @pl.loop(0, last)
        def _(q):
            gain_copy(q).start()

        own_weight.start()
        own_gain.start()

    values_copy(across, 1).start()

    @pl.loop(1, n_rows)
    def _(k):
        values_copy(along(k), k + 1).start()

    values_copy(sibling, 0).start()
    load_values.start()
    load_embed.start()

    load_gains.wait()
    wide = pl.cdiv(width, 128) * 128
    turned = pltpu.roll(
        jnp.broadcast_to(gains[...], (8, model)), lax.rem(model - width * j, model), 1
    )
    column[...] = turned[:, :wide].T[:width, 0:1]

    @pl.when(is_last)
    def _():
        own_slice.wait()

    @pl.when(jnp.logical_not(is_last))
    def _():
        slice_copy(p).wait_recv()

    def token_copy(k):
        q = lax.rem(chip + k, n_chips) * 2 + core
        return remote(a7.at[j], a7.at[j], a_send.at[k], a_recv.at[j], (p, t, q))

    def tokens_arrived(q):
        return remote(a7.at[j], a7.at[q], a_send.at[0], a_recv.at[q], (p, t, sibling))

    def tokens_forward(k):
        owner = lax.rem(chip + n_chips - k, n_chips) * 2 + core
        return remote(a7.at[owner], a7.at[owner], a_fwd.at[k], a_recv.at[owner], (p, t, sibling))

    @pl.loop(1, n_chips)
    def _(k):
        token_copy(k).start()

    tokens_forward(0).start()

    def relay():
        values_arrived(across).wait_recv()

        @pl.loop(1, n_rows)
        def _(k):
            relay_copy(k).start()

        forward_copy(0, True).start()

        @pl.loop(1, n_chips)
        def _(k):
            tokens_arrived(lax.rem(chip + n_chips - k, n_chips) * 2 + core).wait_recv()
            tokens_forward(k).start()

    next_to_last = jnp.logical_or(p == 0, p == last - 1)
    relay_at = jnp.where(next_to_last, min(4, chunks - 1), 0)

    @pl.when(is_last)
    def _():
        relay()
        own_weight.wait()
        own_gain.wait()

    @pl.when(jnp.logical_not(is_last))
    def _():
        @pl.loop(0, chunks)
        def _(c):
            weight_copy(w_ref, c, w_up, up).wait_recv()

            @pl.when(p < up_hops - 1)
            def _():
                weight_copy(w7, c, w_up, up).start()

            @pl.when(p > up_hops)
            def _():
                weight_copy(w7, c, w_down, down).start()

            @pl.when(c == relay_at)
            def _():
                relay()

        gain_copy(p).wait_recv()

    @pl.loop(0, n_chips)
    def _(k):
        tokens_arrived(2 * k + 1 - core).wait_recv()

    part[...] = (
        lax.dot_general(
            a7[...].reshape(plane, depth), w7[...], CONTRACT_LAST, preferred_element_type=jnp.float32
        )
        .astype(jnp.bfloat16)
        .reshape(n_dp, tokens, width)
    )

    def same_copy(k):
        q = dp_at(k)
        return remote(part.at[q], parts.at[t, j], p_send.at[0, k], p_recv.at[t, j], (p, t, q))

    def cross_copy(k):
        q = dp_at(k)
        return remote(part.at[q], parts.at[t, j], p_send.at[1, k], p_recv.at[t, j], (p, other, q))

    def part_arrived(group, q):
        return remote(part.at[q], parts.at[group, q], p_send.at[0, 0], p_recv.at[group, q], pair)

    @pl.loop(0, n_dp)
    def _(k):
        cross_copy(k).start()

    @pl.loop(1, n_dp)
    def _(k):
        same_copy(k).start()

    parts[t, j] = part[j]

    @pl.loop(1, n_rows)
    def _(k):
        for far in (False, True):
            values_arrived(source_of(k, far)).wait_recv()
            forward_copy(k, far).start()

    load_weight.wait()
    load_values.wait()

    @pl.loop(0, n_chips)
    def _(k):
        values_arrived(2 * k + 1 - core).wait_recv()

    def output_copy(q):
        return remote(ps.at[q], ps_in.at[q], o_send.at[q], o_recv.at[q], pair)

    @pl.loop(0, n_pipe)
    def _(q):
        ps[q] = lax.dot_general(
            w[...], every[q].reshape(plane, depth), CONTRACT_LAST, preferred_element_type=jnp.float32
        ).astype(jnp.bfloat16)

    def send_outputs(first, stop):
        @pl.loop(first, stop)
        def _(q):
            output_copy(q).start()

    send_outputs(0, n_pipe // 4)

    load_rows.wait()
    load_embed.wait()

    @pl.loop(0, n_dp)
    def _(k):
        part_arrived(other, k).wait_recv()

    @pl.loop(1, n_dp)
    def _(k):
        part_arrived(t, dp_at(k)).wait_recv()

    output = flatten(
        [parts[0, q].astype(jnp.float32) + parts[1, q].astype(jnp.float32) for q in range(n_dp)]
    )
    _, normed = normalize(output)
    final_gain = fgain_ref[...].reshape(1, model)
    resid = rows_in[...].astype(jnp.float32) + normed * g7[...]
    y_scale, y_normed = normalize(resid)
    head_in = (y_normed * final_gain).astype(jnp.bfloat16)
    cols = hz.shape[2]
    for q in range(n_pipe):
        line_out[0, q] = head_in[:, q * cols:(q + 1) * cols]

    def line_copy(slot, dst, send, recv, k):
        q = pipe_at(k)
        return remote(line_out.at[slot, q], dst.at[p], send.at[k], recv.at[p], (q, t, j))

    def line_arrived(slot, dst, send, recv, q):
        return remote(line_out.at[slot, q], dst.at[q], send.at[0], recv.at[q], (q, t, j))

    @pl.loop(1, n_pipe)
    def _(k):
        line_copy(0, hz, h_send, h_recv, k).start()

    hz[p] = line_out[0, p]

    raw = lax.dot_general(head_in, embed[...], CONTRACT_LAST, preferred_element_type=jnp.float32)
    capped = jnp.tanh(raw / CAP)
    logits = CAP * capped
    own_sum = jnp.sum(jnp.exp(logits), axis=1, keepdims=True)
    sum_out[...] = jnp.broadcast_to(own_sum, sum_out.shape)

    def sum_copy():
        return remote(sum_out, sum_in, sum_sem.at[0], sum_sem.at[1], pair)

    sum_copy().start()
    lane = lax.broadcasted_iota(jnp.int32, (tokens, vrows), 1)
    first_row = offset_ref[0] + t * vrows
    target = own_tokens(target_ref, p * tokens, tokens)
    hit = (target == (first_row + lane).astype(jnp.float32)).astype(jnp.float32)
    slope = 1.0 - capped * capped
    sum_copy().wait_recv()
    log_total = jnp.log(own_sum + sum_in[:, 0:1])
    rest = own_tokens(rest_ref, p * tokens, tokens)
    lse = jnp.maximum(rest, log_total) + jnp.log(1.0 + jnp.exp(-jnp.abs(rest - log_total)))
    delta = ((jnp.exp(logits - lse) - hit) * slope).astype(jnp.bfloat16)
    delta_out[...] = delta
    delta_all[p] = delta

    step = model // BACK_CHUNKS

    def back_copy(c):
        return remote(back_out.at[c], back_in.at[c], back_send.at[c], back_recv.at[c], pair)

    for c in range(BACK_CHUNKS):
        grad = jnp.dot(delta, embed[:, c * step:(c + 1) * step], preferred_element_type=jnp.float32)
        back_out[c] = grad.astype(jnp.bfloat16)
        back_copy(c).start()

    def delta_copy(k):
        return remote(delta_out, delta_all.at[p], d_send.at[k], d_recv.at[p], (pipe_at(k), t, j))

    def delta_arrived(q):
        return remote(delta_out, delta_all.at[q], d_send.at[0], d_recv.at[q], (q, t, j))

    @pl.loop(1, n_pipe)
    def _(k):
        delta_copy(k).start()

    grads = []
    for c in range(BACK_CHUNKS):
        back_copy(c).wait_recv()
        grads.append(back_out[c].astype(jnp.float32) + back_in[c].astype(jnp.float32))
    grad = flatten(grads) * final_gain
    top = y_scale * (grad - y_normed * jnp.mean(grad * y_normed, axis=-1, keepdims=True))
    top = top.astype(jnp.bfloat16)
    for b in range(n_dp):
        block[b] = top[:, b * width:(b + 1) * width]
    for q in range(n_pipe):
        line_out[1, q] = top[:, q * cols:(q + 1) * cols]

    def column_copy(k):
        q = dp_at(k)
        return remote(block.at[q], col.at[j], c_send.at[k], c_recv.at[j], (p, t, q))

    def column_arrived(q):
        return remote(block.at[q], col.at[q], c_send.at[0], c_recv.at[q], pair)

    @pl.loop(1, n_dp)
    def _(k):
        column_copy(k).start()

    @pl.loop(1, n_pipe)
    def _(k):
        line_copy(1, tz, z_send, z_recv, k).start()

    send_outputs(n_pipe // 4, n_pipe // 2)
    col[j] = block[j]
    tz[p] = line_out[1, p]

    @pl.loop(1, n_dp)
    def _(k):
        column_arrived(dp_at(k)).wait_recv()

    tg[p] = col[...].reshape(plane, width).T

    ring_rows = width // RING_CHUNKS

    def ring_copy(source, c, send, device):
        ref = tg.at[source, pl.ds(c * ring_rows, ring_rows)]
        return remote(ref, ref, send.at[source, c], r_recv.at[source, c], device)

    def above(s):
        return lax.rem(p + s, n_pipe)

    def below(s):
        return lax.rem(p + n_pipe - s, n_pipe)

    for c in range(RING_CHUNKS):
        ring_copy(p, c, r_up, up).start()
        if down_hops:
            ring_copy(p, c, r_down, down).start()
    send_outputs(n_pipe // 2, n_pipe)

    @pl.loop(1, n_pipe)
    def _(k):
        q = pipe_at(k)
        line_arrived(0, hz, h_send, h_recv, q).wait_recv()
        line_arrived(1, tz, z_send, z_recv, q).wait_recv()
        delta_arrived(q).wait_recv()

    count = n_pipe * tokens
    head_cols = hz[...].reshape(count, cols)
    top_cols = tz[...].reshape(count, cols)
    delta_rows = delta_all[...].reshape(count, vrows).T
    row = lax.broadcasted_iota(jnp.int32, (vrows, count), 0)
    ids = flatten([ids_ref[m:m + 1, :] for m in range(ids_ref.shape[0])])
    used = (ids == first_row + row).astype(jnp.bfloat16)
    term[...] = (
        (
            jnp.dot(delta_rows, head_cols, preferred_element_type=jnp.float32)
            + math.sqrt(model) * jnp.dot(used, top_cols, preferred_element_type=jnp.float32)
        )
        .astype(jnp.bfloat16)
        .reshape(term.shape)
    )

    def core_copy(k):
        return remote(term.at[2 * k + 1 - core], core_in.at[k], t_send.at[k], t_recv.at[k], (p, t, sibling))

    def line_term(k):
        q = lax.rem(line + k, n_rows)
        return remote(
            half.at[pl.ds(2 * q, 2)], line_in.at[line], y_send.at[k], y_recv.at[line], (p, t, along(k))
        )

    def line_term_arrived(q):
        return remote(half.at[pl.ds(0, 2)], line_in.at[q], y_send.at[0], y_recv.at[q], (p, t, sibling))

    def side_copy():
        return remote(side_out, side_in, x_sem.at[0], x_sem.at[1], (p, t, across))

    def sum_cores():
        @pl.loop(0, n_chips)
        def _(k):
            core_copy(k).wait_recv()
            both = term[2 * k + core].astype(jnp.float32) + core_in[k].astype(jnp.float32)
            half[k] = both.astype(jnp.bfloat16)

        @pl.loop(1, n_rows)
        def _(k):
            line_term(k).start()

    def sum_line():
        near = half[2 * line + side].astype(jnp.float32)
        far = half[2 * line + 1 - side].astype(jnp.float32)
        for k in range(1, n_rows):
            q = lax.rem(line + n_rows - k, n_rows)
            line_term_arrived(q).wait_recv()
            near = near + line_in[q, side].astype(jnp.float32)
            far = far + line_in[q, 1 - side].astype(jnp.float32)
        tied_ref[...] = near
        side_out[...] = far.astype(jnp.bfloat16)
        side_copy().start()

    @pl.loop(0, n_chips)
    def _(k):
        core_copy(k).start()

    for s in range(1, up_hops + 1):
        for c in range(RING_CHUNKS):
            ring_copy(below(s), c, r_up, up).wait_recv()
            if s < up_hops:
                ring_copy(below(s), c, r_up, up).start()
            if s <= down_hops:
                ring_copy(above(s), c, r_down, down).wait_recv()
                if s < down_hops:
                    ring_copy(above(s), c, r_down, down).start()
        if s == 1:
            sum_cores()
        if s == up_hops - 1:
            sum_line()
    if up_hops == 1:
        sum_line()

    @pl.loop(0, n_pipe)
    def _(q):
        output_copy(q).wait_recv()
        out = ps[q].astype(jnp.float32) + ps_in[q].astype(jnp.float32)
        grad = tg[q].astype(jnp.float32) * column[...]
        stat[pl.ds(q, 1), :] = jnp.sum(out * out, axis=0, keepdims=True)
        stat[pl.ds(n_pipe + q, 1), :] = jnp.sum(out * grad, axis=0, keepdims=True)

    def stat_copy(k):
        return remote(stat, stats.at[j], st_send.at[k], st_recv.at[j], (p, t, dp_at(k)))

    def stat_arrived(q):
        return remote(stat, stats.at[q], st_send.at[0], st_recv.at[q], pair)

    @pl.loop(1, n_dp)
    def _(k):
        stat_copy(k).start()

    stats[j] = stat[...]

    side_copy().wait_recv()
    tied_ref[...] += side_in[...].astype(jnp.float32)

    @pl.loop(1, n_dp)
    def _(k):
        stat_arrived(dp_at(k)).wait_recv()

    both = jnp.sum(stats[...], axis=0)
    scale = lax.rsqrt(both[:n_pipe] / model + EPS)
    coef[0:n_pipe] = scale
    coef[n_pipe:2 * n_pipe] = scale * scale * both[n_pipe:] / model
    proj_ref[...] = jnp.zeros_like(proj_ref)

    @pl.loop(0, n_pipe)
    def _(q):
        out = ps[q].astype(jnp.float32) + ps_in[q].astype(jnp.float32)
        grad = tg[q].astype(jnp.float32) * column[...]
        out_grad = coef[pl.ds(q, 1), :] * (grad - out * coef[pl.ds(n_pipe + q, 1), :])
        proj_ref[...] += jnp.dot(
            out_grad.astype(jnp.bfloat16),
            every[q].reshape(plane, depth),
            preferred_element_type=jnp.float32,
        )

    @pl.when(is_last)
    def _():
        @pl.loop(0, last)
        def _(q):
            slice_copy(q).wait_send()
            gain_copy(q).wait_send()

        @pl.loop(0, chunks)
        def _(c):
            weight_copy(w_ref, c, w_up, up).wait_send()
            if down_hops:
                weight_copy(w_ref, c, w_down, down).wait_send()

    @pl.when(jnp.logical_not(is_last))
    def _():
        @pl.when(p < up_hops - 1)
        def _():
            @pl.loop(0, chunks)
            def _(c):
                weight_copy(w7, c, w_up, up).wait_send()

        @pl.when(p > up_hops)
        def _():
            @pl.loop(0, chunks)
            def _(c):
                weight_copy(w7, c, w_down, down).wait_send()

    values_copy(sibling, 0).wait_send()
    values_copy(across, 1).wait_send()
    forward_copy(0, True).wait_send()
    tokens_forward(0).wait_send()
    cross_copy(0).wait_send()
    sum_copy().wait_send()

    @pl.loop(1, n_rows)
    def _(k):
        values_copy(along(k), k + 1).wait_send()
        relay_copy(k).wait_send()
        forward_copy(k, False).wait_send()
        forward_copy(k, True).wait_send()

    @pl.loop(1, n_chips)
    def _(k):
        token_copy(k).wait_send()
        tokens_forward(k).wait_send()

    @pl.loop(1, n_dp)
    def _(k):
        cross_copy(k).wait_send()
        same_copy(k).wait_send()
        column_copy(k).wait_send()
        stat_copy(k).wait_send()

    @pl.loop(1, n_pipe)
    def _(k):
        line_copy(0, hz, h_send, h_recv, k).wait_send()
        line_copy(1, tz, z_send, z_recv, k).wait_send()
        delta_copy(k).wait_send()

    @pl.loop(0, n_pipe)
    def _(q):
        output_copy(q).wait_send()

    @pl.loop(0, n_chips)
    def _(k):
        core_copy(k).wait_send()

    @pl.loop(1, n_rows)
    def _(k):
        line_term(k).wait_send()

    side_copy().wait_send()
    for c in range(BACK_CHUNKS):
        back_copy(c).wait_send()
    for c in range(RING_CHUNKS):
        for s in range(up_hops):
            ring_copy(below(s), c, r_up, up).wait_send()
        for s in range(down_hops):
            ring_copy(above(s), c, r_down, down).wait_send()


def sections(weight, values, gain, embed, section_input, final_gain, target, rest, ids, offset, n_pipe, n_dp):
    dma = pltpu.SemaphoreType.DMA
    vmem = pltpu.VMEM
    half, full = jnp.bfloat16, jnp.float32
    width, depth = weight.shape
    tokens = values.shape[1]
    vrows, model = embed.shape
    per_pipe = n_dp // n_pipe
    step = model // BACK_CHUNKS
    plane = n_dp * tokens
    rows = vrows // n_dp
    cols = per_pipe * width
    chunks = width // W_CHUNK
    return pl.pallas_call(
        functools.partial(section_kernel, n_pipe, n_dp),
        out_shape=(
            jax.ShapeDtypeStruct((width, depth), full),
            jax.ShapeDtypeStruct((rows, cols), full),
        ),
        in_specs=[ANY] * 5 + [VMEM] * 4 + [SMEM],
        out_specs=(VMEM, VMEM),
        scratch_shapes=[
            vmem((vrows, model), half),
            vmem((width, depth), half),
            vmem((width, depth), half),
            vmem((n_dp, tokens, depth), half),
            vmem((1, model), full),
            vmem((n_pipe, n_dp, tokens, depth), half),
            vmem((tokens, model), half),
            vmem((n_dp, tokens, width), half),
            vmem((2, n_dp, tokens, width), half),
            vmem((tokens, 128), full),
            vmem((tokens, 128), full),
            vmem((tokens, vrows), half),
            vmem((n_pipe, tokens, vrows), half),
            vmem((BACK_CHUNKS, tokens, step), half),
            vmem((BACK_CHUNKS, tokens, step), half),
            vmem((n_dp, tokens, width), half),
            vmem((2, n_pipe, tokens, cols), half),
            vmem((n_pipe, tokens, cols), half),
            vmem((n_pipe, tokens, cols), half),
            vmem((n_dp, tokens, width), half),
            vmem((n_pipe, width, plane), half),
            vmem((n_pipe, width, plane), half),
            vmem((n_pipe, width, plane), half),
            vmem((n_dp, rows, cols), half),
            vmem((n_dp // 2, rows, cols), half),
            vmem((n_dp // 2, rows, cols), half),
            vmem((n_dp // 4, 2, rows, cols), half),
            vmem((rows, cols), half),
            vmem((rows, cols), half),
            vmem((2 * n_pipe, plane), full),
            vmem((n_dp, 2 * n_pipe, plane), full),
            vmem((2 * n_pipe, plane), full),
            vmem((1, model), full),
            vmem((width, 1), full),
            dma((8,)), dma((chunks,)), dma((chunks,)), dma((chunks,)),
            dma, dma((n_pipe,)), dma, dma((n_pipe,)),
            dma((n_dp,)), dma((n_dp // 2,)), dma((n_dp // 2,)),
            dma((n_dp,)), dma((n_dp // 4 + 1,)), dma((n_dp // 4,)), dma((n_dp // 2,)),
            dma((2, n_dp)), dma((2, n_dp)), dma((2,)), dma((BACK_CHUNKS,)), dma((BACK_CHUNKS,)),
            dma((n_pipe,)), dma((n_pipe,)), dma((n_pipe,)), dma((n_pipe,)), dma((n_pipe,)), dma((n_pipe,)),
            dma((n_dp,)), dma((n_dp,)),
            dma((n_pipe, RING_CHUNKS)), dma((n_pipe, RING_CHUNKS)), dma((n_pipe, RING_CHUNKS)),
            dma((n_pipe,)), dma((n_pipe,)), dma((n_dp // 2,)), dma((n_dp // 2,)),
            dma((n_dp // 4,)), dma((n_dp // 4,)), dma((2,)), dma((n_dp,)), dma((n_dp,)),
        ],
        compiler_params=pltpu.CompilerParams(
            collective_id=0, has_side_effects=True, vmem_limit_bytes=56 * 1024 * 1024
        ),
        name="sections",
    )(weight, values, gain, embed, section_input, final_gain, target, rest, ids, offset)


def per_device(
    section_proj,
    attn_values,
    post_gain,
    section_input,
    final_gain,
    embed_block,
    token_ids,
    target_ids,
    block_offset,
    rest_lse,
):
    n_pipe, n_dp = lax.axis_size("pipe"), lax.axis_size("dp")
    weight = section_proj[0]
    count = section_input.shape[0] * section_input.shape[1]
    own_grad, tied = sections(
        weight,
        attn_values.reshape(n_pipe, count // n_pipe, weight.shape[1]),
        post_gain,
        embed_block,
        section_input.reshape(count, section_input.shape[2]),
        final_gain,
        target_ids,
        rest_lse,
        token_ids,
        block_offset,
        n_pipe,
        n_dp,
    )
    return (own_grad[None], tied)


def solution(mesh):
    in_specs = (
        P("pipe", "dp", "tensor"),
        P("pipe", None, "dp", "tensor"),
        P("pipe", None),
        P(None, "dp", None),
        P(),
        P("tensor", None),
        P(None, "dp"),
        P(None, "dp"),
        P(),
        P(None, "dp"),
    )
    out_specs = (P("pipe", "dp", "tensor"), P(("tensor", "dp"), "pipe"))
    return jax.shard_map(
        per_device, mesh=mesh, in_specs=in_specs, out_specs=out_specs, check_vma=False
    )
```
